128 devices in a mesh: tomo: 8 (over y_hi, x), orient: 16 (over z, y_lo, core).
Axes of the slice: x: 4, y: 4 (y_hi: 2, y_lo: 2; y = y_hi * 2 + y_lo), z: 4, core: 2. Of those that a mesh axis runs over, the one named last changes fastest.
Arguments:
- subtomograms: bfloat16 [768, 64, 4096], P(('tomo', 'orient')), may hold values from -6 to 6
- rotated_refs: bfloat16 [64, 64, 4096], P('orient'), may hold values from -6 to 6
- wedges: bfloat16 [16, 64, 4096], P('tomo'), may hold values from 0 to 1, as said below
- ref_pick: int32 [2], replicated, may hold values from 0 to 63
- best_pick: int32 [768], P(('tomo', 'orient')), may hold values from 0 to 23
- class_of: int32 [768, 1], P(('tomo', 'orient')), may hold values from 0 to 15; in each aligned block of 6 rows (0 to 5, 6 to 11, ...) at most 3 rows name the same one
Outputs:
- scores: float32 [2, 768], P(None, ('tomo', 'orient'))
- averages: float32 [16, 64, 4096], P('orient', 'tomo')
The draws below stay inside these ranges and needn't reach their ends.
Inputs may be any that keep to these rules, and one draw needn't show every extreme that they name: `class_of`: of the 6 subtomograms of one device at most 3 share a class, and some device has 3 in one class; every class has a subtomogram. `wedges`: each tomogram's weights are zero on a missing wedge of frequencies.
All inputs are finite; a program needn't handle non-finite values.
Results may differ from the reference program's by a relative error of at most 0.015.
Values may be sent and summed in bfloat16 or wider, within the bound.
A program may use at most 256 MiB of HBM per device.

```python
import math
import jax
import jax.numpy as jnp
import numpy as np
from jax import lax

BOX = 64
SUB_DEV = 6
STEPS = 2
CAP = 3
ROTATIONS = 24
SUBS = 768
ORIENTS = 64
TOMOGRAMS = 16
SUB_TOM = 48
CLASSES = 16


def draw_wedges(key, part):
    slope_key, weight_key = jax.random.split(key)
    slopes = jax.random.randint(slope_key, (TOMOGRAMS, 1, 1, 1), 5, 9)
    indices = jnp.arange(BOX, dtype=jnp.int32)
    signed_freq = jnp.where(indices < BOX // 2, indices, indices - BOX)
    magnitude = jnp.abs(signed_freq)
    missing = 4 * magnitude[None, None, None, :] > slopes * magnitude[None, :, None, None]
    weights = jax.random.uniform(weight_key, (TOMOGRAMS, BOX, BOX, BOX), jnp.float32, 0.3, 1.0)
    wedge_values = jnp.where(missing, 0.0, weights)
    return wedge_values.reshape(TOMOGRAMS, BOX, BOX * BOX).astype(jnp.bfloat16)


def with_ends(array, stream_key, smallest, top_value):
    index_at = [jax.random.randint(jax.random.fold_in(stream_key, axis), (), 0, length) for axis, length in enumerate(array.shape)]
    longest = array.shape.index(max(array.shape))
    beside = index_at[:longest] + [(index_at[longest] + 1) % array.shape[longest]] + index_at[longest + 1:]
    return array.at[tuple(index_at)].set(smallest).at[tuple(beside)].set(top_value)


def levels(stream_key, extent, pieces, low, high):
    def one(dim, blocks):
        draws = jax.random.uniform(jax.random.fold_in(jax.random.fold_in(stream_key, 6), dim), (blocks,), jnp.float32, low / len(pieces), high / len(pieces))
        return jnp.repeat(jnp.exp(draws), extent[dim] // blocks).reshape((-1,) + (1,) * (len(extent) - dim - 1))

    factor_of = one(*pieces[0])
    for cut in pieces[1:]:
        factor_of = factor_of * one(*cut)
    return factor_of


def routed_block(stream_key, own, number, rows, number_of, top, reach, lean):
    ranking = jax.random.permutation(stream_key, number_of)
    packed, usual = portions_of(number_of, rows * top, reach, lean, True), portions_of(number_of, rows * top, reach, lean, False)
    places = jnp.arange(number_of)

    def named(tallies, turn):
        used = int((tallies > 0).sum())
        fixed = max(1, used // 4)
        moved = fixed + (places - fixed + turn * (used - fixed)) % max(1, number_of - fixed)
        return jnp.zeros((number_of,), jnp.int32).at[ranking[jnp.where(places < fixed, places, moved)]].set(jnp.asarray(tallies, jnp.int32))

    tallies = jnp.where(number % 4 == 0, named(packed, number // 4), named(usual, number - number // 4 - 1))
    mixed = jax.random.permutation(jax.random.fold_in(own, 3), number_of)
    giver, taker = mixed[0:number_of // 2 * 2:2], mixed[1:number_of // 2 * 2:2]
    room = jnp.minimum(tallies[giver] - 1, reach - tallies[taker]) // 2
    room = jnp.where((giver == ranking[0]) | (taker == ranking[0]) | (tallies[taker] == 0), 0, jnp.maximum(room, 0))
    moved = jax.random.randint(jax.random.fold_in(own, 4), (number_of // 2,), 0, 1 << 20) % (room + 1)
    tallies = tallies.at[giver].add(-moved).at[taker].add(moved)
    members = jnp.searchsorted(jnp.cumsum(tallies), jnp.arange(rows * top), side="right").astype(jnp.int32)
    grid = members.reshape(top, rows).T
    grid = grid[jax.random.permutation(jax.random.fold_in(own, 1), rows)]
    turn = jax.random.randint(jax.random.fold_in(own, 2), (rows, 1), 0, top)
    return jnp.take_along_axis(grid, (jnp.arange(top)[None, :] + turn) % top, axis=1)


def portions_of(number_of, total, bound, slope, full):
    portions = [(1 << 20) // math.isqrt(grade ** slope) + 1 for grade in range(1, number_of + 1)]
    largest = bound if full else min(bound, max(-(-total // number_of), total * portions[0] // sum(portions)))
    least = 1 if total - largest >= number_of - 1 else 0
    holding, surplus = [largest] + [least] * (number_of - 1), total - largest - least * (number_of - 1)
    while surplus > 0:
        candidates = [i for i in range(1, number_of) if holding[i] < largest] or [i for i in range(1, number_of) if holding[i] < bound]
        pool, budget = sum([portions[i] for i in candidates]), surplus
        for i in candidates:
            addition = min(bound - holding[i], max(1, budget * portions[i] // pool), surplus)
            holding[i] = holding[i] + addition
            surplus = surplus - addition
    return np.array(holding)


def centred(key, extent, scale, bound, pieces=(), held_as=jnp.bfloat16):
    result = scale * jax.random.normal(key, extent, jnp.float32)
    if pieces:
        result = result * levels(key, extent, pieces, -0.22, 0.18)
    return jnp.clip(result, -bound, bound).astype(held_as)


def setup_inputs(seed: int = 0) -> dict:
    streams_of = jax.random.split(jax.random.key(seed), 7)
    subtomograms = centred(streams_of[0], (SUBS, BOX, BOX * BOX), 1.0, 6.0, ((0, 128),))
    rotated_refs = centred(streams_of[1], (ORIENTS, BOX, BOX * BOX), 1.0, 6.0, ((0, 16),))
    wedges = draw_wedges(jax.random.fold_in(streams_of[6], 71), 0)
    ref_pick = jax.random.randint(streams_of[3], (STEPS,), 0, ORIENTS).astype(jnp.int32)
    best_pick = with_ends(jax.random.randint(streams_of[4], (SUBS,), 0, ROTATIONS), jax.random.fold_in(streams_of[4], 1), 0, ROTATIONS - 1).astype(jnp.int32)
    class_of_keys = jax.random.split(jax.random.fold_in(streams_of[5], 1), SUBS // SUB_DEV)
    class_of_turns = jax.random.permutation(jax.random.fold_in(streams_of[5], 3), SUBS // SUB_DEV)
    class_of = jax.vmap(lambda own, number: routed_block(jax.random.fold_in(streams_of[5], 2), own, number, SUB_DEV, CLASSES, 1, CAP, 2))(class_of_keys, class_of_turns).reshape((SUBS, 1))
    return dict(subtomograms=subtomograms, rotated_refs=rotated_refs, wedges=wedges, ref_pick=ref_pick, best_pick=best_pick, class_of=class_of)


def dft_tables(length):
    indices = jnp.arange(length, dtype=jnp.int32)
    phases = indices[:, None] * indices[None, :] % length
    angles = phases.astype(jnp.float32) * (2.0 * math.pi / length)
    cosine = jnp.cos(angles)
    sine_part = jnp.sin(angles)
    forward_table = jnp.stack([jnp.stack([cosine, sine_part], 1), jnp.stack([-sine_part, cosine], 1)], 0)
    inverse_table = jnp.stack([jnp.stack([cosine, -sine_part], 1), jnp.stack([sine_part, cosine], 1)], 0)
    return (forward_table.astype(jnp.bfloat16), inverse_table.astype(jnp.bfloat16))

def forward_volume(volume, forward_table):
    table_full = forward_table.astype(jnp.float32)
    first_pass = jnp.einsum('pkj,jyz->pkyz', table_full[:, :, 0, :], volume.astype(jnp.float32)).astype(jnp.bfloat16)
    second_pass = jnp.einsum('pkqj,qxjz->pxkz', table_full, first_pass.astype(jnp.float32)).astype(jnp.bfloat16)
    return jnp.einsum('pkqj,qxyj->pxyk', table_full, second_pass.astype(jnp.float32)).astype(jnp.bfloat16)

def inverse_volume(spectrum, inverse_table):
    table_full = inverse_table.astype(jnp.float32)
    first_pass = jnp.einsum('pkqj,qjyz->pkyz', table_full, spectrum.astype(jnp.float32)).astype(jnp.bfloat16)
    second_pass = jnp.einsum('pkqj,qxjz->pxkz', table_full, first_pass.astype(jnp.float32)).astype(jnp.bfloat16)
    return jnp.einsum('kqj,qxyj->xyk', table_full[0], second_pass.astype(jnp.float32))

def make_turn(axis_order, flip_axes):

    def turn_volume(volume):
        turned = jnp.transpose(volume, axis_order)
        if len(flip_axes) == 0:
            return turned
        return jnp.flip(turned, flip_axes)
    return turn_volume

def turn_list():
    orders = [((0, 1, 2), False), ((0, 2, 1), True), ((1, 0, 2), True), ((1, 2, 0), False), ((2, 0, 1), False), ((2, 1, 0), True)]
    even_flips = [(), (0, 1), (0, 2), (1, 2)]
    odd_flips = [(0,), (1,), (2,), (0, 1, 2)]
    turners = []
    for axis_order, is_odd in orders:
        for flip_axes in odd_flips if is_odd else even_flips:
            turners.append(make_turn(axis_order, flip_axes))
    return turners

def rotate_volume(volume, number):
    return lax.switch(number, turn_list(), volume)

def reference(subtomograms, rotated_refs, wedges, ref_pick, best_pick, class_of):
    forward_table, inverse_table = dft_tables(BOX)
    cell_count = BOX * BOX * BOX
    ref_spectra = []
    for step_index in range(STEPS):
        chosen = lax.dynamic_index_in_dim(rotated_refs, ref_pick[step_index], 0, False)
        ref_spectra.append(forward_volume(chosen.reshape(BOX, BOX, BOX), forward_table).astype(jnp.float32))

    def one_subtomogram(carry, inputs):
        class_sums, class_count = carry
        flat_volume, rotation, class_index, position = inputs
        wedge_mask = lax.dynamic_index_in_dim(wedges, position // SUB_TOM, 0, False)
        wedge_mask = wedge_mask.reshape(BOX, BOX, BOX).astype(jnp.float32)
        volume = flat_volume.reshape(BOX, BOX, BOX)
        spectrum = forward_volume(volume, forward_table)
        spec_real = spectrum[0].astype(jnp.float32)
        spec_imag = spectrum[1].astype(jnp.float32)
        own_power = jnp.sum(wedge_mask * (spec_real ** 2 + spec_imag ** 2))
        row_scores = []
        for step_index in range(STEPS):
            ref_real = ref_spectra[step_index][0]
            ref_imag = ref_spectra[step_index][1]
            ref_power = jnp.sum(wedge_mask * (ref_real ** 2 + ref_imag ** 2))
            cross_spec = jnp.stack([wedge_mask * (spec_real * ref_real + spec_imag * ref_imag), wedge_mask * (spec_imag * ref_real - spec_real * ref_imag)], 0).astype(jnp.bfloat16)
            correlation = inverse_volume(cross_spec, inverse_table)
            row_scores.append(jnp.max(correlation) / jnp.sqrt(own_power * ref_power / cell_count + 1e-06))
        aligned = rotate_volume(volume, rotation).reshape(1, BOX, BOX * BOX).astype(jnp.float32)
        current = lax.dynamic_index_in_dim(class_sums, class_index, 0, True)
        class_sums = lax.dynamic_update_index_in_dim(class_sums, current + aligned, class_index, 0)
        class_hits = (jnp.arange(CLASSES, dtype=jnp.int32) == class_index).astype(jnp.float32)
        return ((class_sums, class_count + class_hits), jnp.stack(row_scores))
    start = (jnp.zeros((CLASSES, BOX, BOX * BOX), jnp.float32), jnp.zeros((CLASSES,), jnp.float32))
    positions = jnp.arange(SUBS, dtype=jnp.int32)
    (class_sums, class_count), score_rows = lax.scan(one_subtomogram, start, (subtomograms, best_pick, class_of[:, 0], positions))
    return (jnp.transpose(score_rows), class_sums / class_count[:, None, None])
```

```python
import functools

import jax
import jax.numpy as jnp
import numpy as np
from jax import lax
from jax.experimental import pallas as pl
from jax.experimental.pallas import tpu as pltpu
from jax.sharding import PartitionSpec as P

STEPS = 2
CLASSES = 16
N = 64
BF = jnp.bfloat16
F32 = jnp.float32


def score_tables():
    i = np.arange(N)
    ang = (i[:, None] * i[None, :] % N) * (2.0 * np.pi / N)
    c, s = np.cos(ang), np.sin(ang)
    c[np.abs(c) < 1e-9] = 0.0
    s[np.abs(s) < 1e-9] = 0.0
    h = N // 2
    eye, rev = np.eye(N), np.eye(N)[(-i) % N]

    def pairs(m00, m01, m10, m11):
        return np.array([[m00, m01], [m10, m11]])

    def lanes_forward(b):
        t = np.einsum("abzk,qr,hg->qahzbgrk", b, np.eye(2), np.eye(2))
        return t.reshape(512, 512)

    def rows_forward(b):
        t = np.transpose(b, (1, 3, 0, 2)).reshape(2, N, 2, h, 2)
        return np.transpose(t, (0, 1, 2, 4, 3)).reshape(128, 128)

    fwd = pairs(c, -s, s, c)
    wdg = pairs(eye, 0 * eye, 0 * eye, rev)
    inv = pairs(c, s, -s, c)
    x_fwd = np.concatenate([c[:h], -s[:h]], 0)
    x_fwd[h] = c[h]
    x_wdg = np.concatenate([eye[:h], rev[:h]], 0)
    x_wdg[h] = eye[h]
    y_inv = np.transpose(inv, (1, 3, 0, 2)).reshape(128, 128)
    z_inv = np.einsum("abzk,qr->aqzbrk", inv, np.eye(2)).reshape(256, 256)
    x_inv = x_fwd.T
    flip_rows = np.kron(np.diag([1.0, -1.0]), rev)
    flip_lanes = np.kron(np.eye(2), rev)
    return [
        np.stack([x_fwd, x_wdg]),
        np.stack([lanes_forward(fwd), lanes_forward(wdg)]),
        np.stack([rows_forward(fwd), rows_forward(wdg)]),
        y_inv, z_inv, x_inv, flip_rows, flip_lanes,
    ]


def dot(a, b):
    return jnp.dot(a, b, preferred_element_type=F32)


def forward(first, second, tx, tz, ty, left, plane, out):
    for q, vol in enumerate((first, second)):
        def x_pass(c, _):
            at = pl.multiple_of(c * 512, 512)
            r = dot(tx, vol[:, pl.ds(at, 512)]).astype(BF)
            for k in range(4):
                rows = pl.ds(pl.multiple_of((c * 4 + k) * 32, 32), 32)
                left[rows, q * 256:q * 256 + 128] = r[:32, k * 128:k * 128 + 128]
                left[rows, q * 256 + 128:q * 256 + 256] = r[32:, k * 128:k * 128 + 128]
            return 0
        lax.fori_loop(0, 8, x_pass, 0, unroll=8)

    def z_pass(m, _):
        at = pl.multiple_of(m * 128, 128)
        r = dot(left[pl.ds(at, 128), :], tz)
        for col in range(4):
            plane[pl.ds(col * 1024 + at, 128), :] = r[:, col * 128:col * 128 + 128]
        return 0
    lax.fori_loop(0, 8, z_pass, 0, unroll=8)

    def y_pass(m, _):
        d = jnp.concatenate(
            [plane[pl.ds(2 * m + k, 128, stride=32), :] for k in range(2)], 1).astype(BF)
        r = dot(ty, d).astype(BF)
        for k in range(2):
            out[pl.ds(pl.multiple_of((2 * m + k) * 128, 128), 128), :] = r[:, k * 128:k * 128 + 128]
        return 0
    lax.fori_loop(0, 16, y_pass, 0, unroll=16)


def mirror(g, flip_rows, flip_lanes):
    return dot(dot(flip_rows, g).astype(BF), flip_lanes)


def split(g, t):
    gr, gi, tr, ti = g[:64], g[64:], t[:64], t[64:]
    return (0.5 * (gr + tr), 0.5 * (gi + ti)), (0.5 * (gi - ti), -0.5 * (gr - tr))


def fold(v):
    return functools.reduce(jnp.add, [v[8 * k:8 * k + 8] for k in range(v.shape[0] // 8)])


def power(spec, twin, weight, edge):
    a, b = split(spec[0:128, :].astype(F32), twin)
    total = fold(edge[0:64, :] * (a[0] ** 2 + a[1] ** 2) + edge[64:128, :] * (b[0] ** 2 + b[1] ** 2))

    def body(kx, total):
        v = spec[pl.ds(pl.multiple_of(kx * 128, 128), 128), :].astype(F32)
        w = weight[pl.ds(pl.multiple_of(kx * 64, 64), 64), :]
        return total + fold(w * (v[:64] ** 2 + v[64:] ** 2))
    return lax.fori_loop(1, 32, body, total, unroll=31)


def wedge_setup(spec, flip_rows, flip_lanes, weight, edge):
    g = spec[0:128, :]
    t = mirror(g, jnp.abs(flip_rows), flip_lanes)
    edge[...] = 0.5 * (g.astype(F32) + t)

    def body(kx, _):
        v = spec[pl.ds(pl.multiple_of(kx * 128, 128), 128), :].astype(F32)
        weight[pl.ds(pl.multiple_of(kx * 64, 64), 64), :] = v[:64] + v[64:]
        return 0
    lax.fori_loop(1, 32, body, 0)


def spread_half(v, s, low):
    r = pltpu.roll(v, 64, 1)
    return jnp.where(low, v, r) if s == 0 else jnp.where(low, r, v)


def reference_setup(spec, twin, weight, edge, low, filt, extra):
    a, b = split(spec[0:128, :].astype(F32), twin)
    w0, w32 = edge[0:64, :], edge[64:128, :]
    for s in range(2):
        p = [spread_half(v, s, low) for v in (w0 * a[0], -w0 * a[1])]
        q = [spread_half(v, s, low) for v in (w32 * b[0], -w32 * b[1])]
        for k in range(2):
            filt[s, 64 * k:64 * k + 64, :] = 0.5 * (p[k] + q[k])
            extra[s, 64 * k:64 * k + 64, :] = 0.5 * (p[k] - q[k])

    def body(kx, _):
        v = spec[pl.ds(pl.multiple_of(kx * 128, 128), 128), :].astype(F32)
        w = weight[pl.ds(pl.multiple_of(kx * 64, 64), 64), :]
        re, im = w * v[:64], -w * v[64:]
        for s in range(2):
            filt[s, pl.ds(pl.multiple_of(kx * 128, 128), 64), :] = spread_half(re, s, low)
            filt[s, pl.ds(pl.multiple_of(kx * 128 + 64, 64), 64), :] = spread_half(im, s, low)
        return 0
    lax.fori_loop(1, 32, body, 0)


def correlate(spec, twin, filt, extra, ty, tz, tx, left, plane):
    def times(v, w):
        return (v[:64] * w[:64] - v[64:] * w[64:], v[:64] * w[64:] + v[64:] * w[:64])

    def cross(kx):
        at = pl.multiple_of(kx * 128, 128)
        return times(spec[pl.ds(at, 128), :].astype(F32), filt[pl.ds(at, 128), :])

    def finish(m, parts):
        d = jnp.concatenate([jnp.concatenate(p, 0).astype(BF) for p in parts], 1)
        r = dot(ty, d).astype(BF)
        for k in range(2):
            rows = pl.ds(pl.multiple_of((2 * m + k) * 64, 64), 64)
            left[rows, 0:128] = r[:64, k * 128:k * 128 + 128]
            left[rows, 128:256] = r[64:, k * 128:k * 128 + 128]

    c0, e0 = cross(0), times(twin, extra)
    finish(0, [(c0[0] + e0[0], c0[1] + e0[1]), cross(1)])

    def y_pass(m, _):
        finish(m, [cross(2 * m), cross(2 * m + 1)])
        return 0
    lax.fori_loop(1, 16, y_pass, 0, unroll=15)

    def z_pass(m, _):
        at = pl.multiple_of(m * 256, 256)
        r = dot(left[pl.ds(at, 256), 0:256], tz)
        for p in range(2):
            plane[pl.ds(p * 2048 + at, 256), :] = r[:, p * 128:p * 128 + 128]
        return 0
    lax.fori_loop(0, 8, z_pass, 0, unroll=8)

    def x_pass(m, top):
        d = jnp.concatenate(
            [plane[pl.ds(2 * m + k, 64, stride=64), :] for k in range(2)], 1).astype(BF)
        r = dot(tx, d)
        return jnp.maximum(top, jnp.maximum(r[:, :128], r[:, 128:]))
    top = lax.fori_loop(0, 32, x_pass, jnp.full((64, 128), -jnp.inf, F32), unroll=16)
    return functools.reduce(jnp.maximum, [top[8 * k:8 * k + 8] for k in range(8)])


def score_kernel(v, refs, wedge, txf, tzf, tyf, tyi, tzi, txi, fr, fl, out,
                 left, plane, spec, rspec, twin, weight, edge, filt, extra):
    low = lax.broadcasted_iota(jnp.int32, (64, 128), 1) < 64
    low8 = low[:8]

    def halves(t, op, fill):
        f = jnp.max if op == "max" else jnp.sum
        return [f(jnp.where(low8 == (k == 0), t, fill), keepdims=True) for k in range(2)]

    forward(wedge, wedge, txf[1], tzf[1], tyf[1], left, plane, rspec)
    wedge_setup(rspec, fr[...], fl[...], weight, edge)
    forward(refs.at[0], refs.at[1], txf[0], tzf[0], tyf[0], left, plane, rspec)
    rt = mirror(rspec[0:128, :], fr[...], fl[...])
    rp = halves(power(rspec, rt, weight, edge), "sum", 0.0)
    reference_setup(rspec, rt, weight, edge, low, filt, extra)
    row = lax.broadcasted_iota(jnp.int32, (8, 128), 0)
    lane = lax.broadcasted_iota(jnp.int32, (8, 128), 1)

    def one_pair(pair, result):
        forward(v.at[2 * pair], v.at[2 * pair + 1], txf[0], tzf[0], tyf[0], left, plane, spec)
        t = mirror(spec[0:128, :], fr[...], fl[...])
        own = halves(power(spec, t, weight, edge), "sum", 0.0)

        def one_step(s, result):
            top = halves(correlate(spec, t, filt.at[s], extra[s], tyi[...], tzi[...], txi[...], left, plane), "max", -jnp.inf)
            for k in range(2):
                norm = jnp.sqrt(own[k] * jnp.where(s == 0, rp[0], rp[1]) / float(N ** 3) + 1e-6)
                result = jnp.where((row == s) & (lane == 2 * pair + k), top[k] / norm, result)
            return result
        return lax.fori_loop(0, 2, one_step, result)
    out[...] = lax.fori_loop(0, 3, one_pair, jnp.zeros((8, 128), F32))


def scores_call(v, refs, wedge):
    tables = [jnp.asarray(t, dtype=BF) for t in score_tables()]
    return pl.pallas_call(
        score_kernel,
        out_shape=jax.ShapeDtypeStruct((8, 128), F32),
        in_specs=[pl.BlockSpec(memory_space=pltpu.VMEM)] * 11,
        out_specs=pl.BlockSpec(memory_space=pltpu.VMEM),
        scratch_shapes=[
            pltpu.VMEM((2048, 512), BF), pltpu.VMEM((4096, 128), F32),
            pltpu.VMEM((4096, 128), BF), pltpu.VMEM((4096, 128), BF),
            pltpu.VMEM((128, 128), F32), pltpu.VMEM((2048, 128), F32), pltpu.VMEM((128, 128), F32),
            pltpu.VMEM((2, 4096, 128), F32), pltpu.VMEM((2, 128, 128), F32),
        ],
        cost_estimate=pl.CostEstimate(flops=20 * 10**9, bytes_accessed=6 * 10**6, transcendentals=0),
        compiler_params=pltpu.CompilerParams(vmem_limit_bytes=50 * 2**20),
    )(v, refs, wedge, *tables)


def turn_tables():
    eye, rev = np.eye(N), np.eye(N)[::-1]
    two, swap = np.eye(2), np.eye(2)[::-1]
    pair = np.concatenate([eye, eye], 1)
    lanes = np.einsum("ac,hg,zw->ahzgcw", two, two, eye).reshape(256, 256)
    rows = np.transpose(eye.reshape(N, 32, 2), (0, 2, 1)).reshape(N, N)
    flip_rows = np.stack([eye, rev])
    flip_lanes = np.stack([np.kron(a, b) for a in (two, swap) for b in (eye, rev)])
    return [pair, lanes, rows, flip_rows, flip_lanes]


def turn_kernel(pick, classes, v, pair, lanes, rows, flip_rows, flip_lanes, out, held, wide, mixed, sums):
    low = lax.broadcasted_iota(jnp.int32, (64, 128), 1) < 64

    def clear(k, _):
        sums[pl.ds(pl.multiple_of(k * 512, 512), 512), :] = jnp.zeros((512, 128), F32)
        return 0
    lax.fori_loop(0, 64, clear, 0)

    def swap_ends():
        def body(m, _):
            blocks = []
            for k in range(2):
                blk = held[pl.ds(pl.multiple_of((2 * m + k) * 64, 64), 64), :].astype(F32)
                blocks += [jnp.where(low, blk, 0.0), jnp.where(low, 0.0, blk)]
            w = jnp.concatenate(blocks, 0).astype(BF)
            r = lax.dot_general(pair[...], w, (((1,), (1,)), ((), ())), preferred_element_type=F32).astype(BF)
            for k in range(2):
                held[pl.ds(pl.multiple_of((2 * m + k) * 64, 64), 64), :] = r[:, k * 128:k * 128 + 128]
            return 0
        lax.fori_loop(0, 16, body, 0, unroll=16)

    def swap_first():
        def widen(m, _):
            at = pl.ds(pl.multiple_of(m * 256, 256), 256)
            wide[at, :] = held[at, :].astype(F32)
            return 0
        lax.fori_loop(0, 8, widen, 0, unroll=8)

        def gather(m, _):
            d = [wide[pl.ds(2 * m + k, 32, stride=64), :] for k in range(2)]
            mixed[pl.ds(pl.multiple_of(m * 32, 32), 32), :] = jnp.concatenate(d, 1).astype(BF)
            return 0
        lax.fori_loop(0, 32, gather, 0, unroll=32)

        def body(m, _):
            r = dot(mixed[pl.ds(pl.multiple_of(m * 256, 256), 256), :], lanes[...]).astype(BF)
            halves = [jnp.concatenate([r[k * 32:k * 32 + 32, h * 128:h * 128 + 128] for k in range(8)], 1)
                      for h in range(2)]
            t = dot(rows[...], jnp.concatenate(halves, 0)).astype(BF)
            for k in range(8):
                held[pl.ds(pl.multiple_of((m * 8 + k) * 64, 64), 64), :] = t[:, k * 128:k * 128 + 128]
            return 0
        lax.fori_loop(0, 4, body, 0, unroll=4)

    def one(i, _):
        number = pick[i]
        order, place = number // 4, number % 4
        even = (order == 0) | (order == 3) | (order == 4)
        f0 = jnp.where(even, (place == 1) | (place == 2), (place == 0) | (place == 3)).astype(jnp.int32)
        f1 = place % 2
        f2 = place // 2
        for b in range(32):
            held[b * 64:b * 64 + 64, :] = v[i, :, b * 128:b * 128 + 128]
        pl.when((order == 1) | (order == 3) | (order == 5))(swap_ends)
        pl.when((order >= 1) & (order <= 4))(swap_first)
        pl.when((order == 1) | (order == 4))(swap_ends)
        c = classes[i]
        base = c * 2048
        j0, jl = flip_rows[f0], flip_lanes[f1 * 2 + f2]

        def flip_ends(m, _):
            at = pl.ds(pl.multiple_of(m * 256, 256), 256)
            held[at, :] = dot(held[at, :], jl).astype(BF)
            return 0

        @pl.when(f1 + f2 > 0)
        def _():
            lax.fori_loop(0, 8, flip_ends, 0, unroll=8)

        def add(m, flipped):
            blocks = []
            for k in range(4):
                b = m * 4 + k
                src = b + f1 * (31 - 2 * b)
                blocks.append(held[pl.ds(pl.multiple_of(src * 64, 64), 64), :])
            if flipped:
                u = dot(j0, jnp.concatenate(blocks, 1))
                blocks = [u[:, k * 128:k * 128 + 128] for k in range(4)]
            for k in range(4):
                at = pl.ds(base + m * 4 + k, 64, stride=32)
                sums[at, :] = sums[at, :] + blocks[k].astype(F32)

        @pl.when(f0 > 0)
        def _():
            lax.fori_loop(0, 8, lambda m, c: (add(m, True), c)[1], 0, unroll=8)

        @pl.when(f0 == 0)
        def _():
            lax.fori_loop(0, 8, lambda m, c: (add(m, False), c)[1], 0, unroll=8)
        return 0
    lax.fori_loop(0, 6, one, 0)

    def narrow(k, _):
        at = pl.ds(pl.multiple_of(k * 512, 512), 512)
        out[at, :] = sums[at, :].astype(BF)
        return 0
    lax.fori_loop(0, 64, narrow, 0)


def turn_call(v, pick, classes):
    tables = [jnp.asarray(t, dtype=BF) for t in turn_tables()]
    vm = pl.BlockSpec(memory_space=pltpu.VMEM)
    return pl.pallas_call(
        turn_kernel,
        out_shape=jax.ShapeDtypeStruct((32768, 128), BF),
        in_specs=[pl.BlockSpec(memory_space=pltpu.SMEM)] * 2 + [vm] * 6,
        out_specs=vm,
        scratch_shapes=[pltpu.VMEM((2048, 128), BF), pltpu.VMEM((2048, 128), F32), pltpu.VMEM((1024, 256), BF), pltpu.VMEM((32768, 128), F32)],
        compiler_params=pltpu.CompilerParams(vmem_limit_bytes=50 * 2**20),
    )(pick, classes, v, *tables)


def local(subtomograms, rotated_refs, wedges, ref_pick, best_pick, class_of):
    orient_size, orient_index = lax.axis_size("orient"), lax.axis_index("orient")
    per = rotated_refs.shape[0]
    wedge = lax.dynamic_index_in_dim(wedges, orient_index * wedges.shape[0] // orient_size, 0, False)
    mine = [
        jnp.where(
            ref_pick[s] // per == orient_index,
            lax.dynamic_index_in_dim(rotated_refs, ref_pick[s] % per, 0, False), 0
        ) for s in range(STEPS)
    ]
    refs = lax.psum(jnp.stack(mine), "orient")
    class_index = class_of[:, 0]
    sums = turn_call(subtomograms, best_pick, class_index)
    received = lax.all_to_all(sums.reshape(CLASSES, 2048, 128), "orient", split_axis=0, concat_axis=0, tiled=True)
    hits = class_index[None, :] == jnp.arange(CLASSES, dtype=jnp.int32)[:, None]
    counts = lax.psum(jnp.sum(hits.astype(F32), axis=1), ("tomo", "orient"))
    result = scores_call(subtomograms, refs, wedge)
    total = jnp.sum(received.astype(F32), axis=0).astype(BF)
    slab = lax.psum_scatter(total, "tomo", scatter_dimension=0, tiled=True).astype(F32)
    averages = (slab / lax.dynamic_index_in_dim(counts, orient_index, 0, False)).reshape(1, 8, 4096)
    return (result[:STEPS, :subtomograms.shape[0]], averages)


def solution(mesh):
    placed = (
        P(("tomo", "orient"), None, None),
        P("orient", None, None),
        P("tomo", None, None),
        P(),
        P(("tomo", "orient")),
        P(("tomo", "orient"), None),
    )
    return jax.shard_map(
        local,
        mesh=mesh,
        in_specs=placed,
        out_specs=(P(None, ("tomo", "orient")), P("orient", "tomo", None)),
        check_vma=False,
    )
```

```python
import functools

import jax
import jax.numpy as jnp
import numpy as np
from jax import lax
from jax.experimental import pallas as pl
from jax.experimental.pallas import tpu as pltpu
from jax.sharding import PartitionSpec as P

STEPS = 2
CLASSES = 16
N = 64
BF = jnp.bfloat16
F32 = jnp.float32
MESH = pl.DeviceIdType.MESH


def score_tables():
    i = np.arange(N)
    ang = (i[:, None] * i[None, :] % N) * (2.0 * np.pi / N)
    c, s = np.cos(ang), np.sin(ang)
    c[np.abs(c) < 1e-9] = 0.0
    s[np.abs(s) < 1e-9] = 0.0
    h = N // 2
    eye, rev = np.eye(N), np.eye(N)[(-i) % N]

    def pairs(m00, m01, m10, m11):
        return np.array([[m00, m01], [m10, m11]])

    def lanes_forward(b):
        t = np.einsum("abzk,qr,hg->qahzbgrk", b, np.eye(2), np.eye(2))
        return t.reshape(512, 512)

    def rows_forward(b):
        t = np.transpose(b, (1, 3, 0, 2)).reshape(2, N, 2, h, 2)
        return np.transpose(t, (0, 1, 2, 4, 3)).reshape(128, 128)

    fwd = pairs(c, -s, s, c)
    wdg = pairs(eye, 0 * eye, 0 * eye, rev)
    inv = pairs(c, s, -s, c)
    x_fwd = np.concatenate([c[:h], -s[:h]], 0)
    x_fwd[h] = c[h]
    x_wdg = np.concatenate([eye[:h], rev[:h]], 0)
    x_wdg[h] = eye[h]
    y_inv = np.transpose(inv, (1, 3, 0, 2)).reshape(128, 128)
    z_inv = np.einsum("abzk,qr->aqzbrk", inv, np.eye(2)).reshape(256, 256)
    x_inv = x_fwd.T
    flip_rows = np.kron(np.diag([1.0, -1.0]), rev)
    flip_lanes = np.kron(np.eye(2), rev)
    return [
        np.stack([x_fwd, x_wdg]),
        np.stack([lanes_forward(fwd), lanes_forward(wdg)]),
        np.stack([rows_forward(fwd), rows_forward(wdg)]),
        y_inv, z_inv, x_inv, flip_rows, flip_lanes,
    ]


def dot(a, b):
    return jnp.dot(a, b, preferred_element_type=F32)


def forward(first, second, tx, tz, ty, left, plane, out):
    for q, vol in enumerate((first, second)):
        def x_pass(c, _):
            at = pl.multiple_of(c * 512, 512)
            r = dot(tx, vol[:, pl.ds(at, 512)]).astype(BF)
            for k in range(4):
                rows = pl.ds(pl.multiple_of((c * 4 + k) * 32, 32), 32)
                left[rows, q * 256:q * 256 + 128] = r[:32, k * 128:k * 128 + 128]
                left[rows, q * 256 + 128:q * 256 + 256] = r[32:, k * 128:k * 128 + 128]
            return 0
        lax.fori_loop(0, 8, x_pass, 0, unroll=8)

    def z_pass(m, _):
        at = pl.multiple_of(m * 128, 128)
        r = dot(left[pl.ds(at, 128), :], tz)
        for col in range(4):
            plane[pl.ds(col * 1024 + at, 128), :] = r[:, col * 128:col * 128 + 128]
        return 0
    lax.fori_loop(0, 8, z_pass, 0, unroll=8)

    def y_pass(m, _):
        d = jnp.concatenate(
            [plane[pl.ds(2 * m + k, 128, stride=32), :] for k in range(2)], 1).astype(BF)
        r = dot(ty, d).astype(BF)
        for k in range(2):
            out[pl.ds(pl.multiple_of((2 * m + k) * 128, 128), 128), :] = r[:, k * 128:k * 128 + 128]
        return 0
    lax.fori_loop(0, 16, y_pass, 0, unroll=16)


def mirror(g, flip_rows, flip_lanes):
    return dot(dot(flip_rows, g).astype(BF), flip_lanes)


def split(g, t):
    gr, gi, tr, ti = g[:64], g[64:], t[:64], t[64:]
    return (0.5 * (gr + tr), 0.5 * (gi + ti)), (0.5 * (gi - ti), -0.5 * (gr - tr))


def fold(v):
    return functools.reduce(jnp.add, [v[8 * k:8 * k + 8] for k in range(v.shape[0] // 8)])


def power(spec, twin, weight, edge):
    a, b = split(spec[0:128, :].astype(F32), twin)
    total = fold(edge[0:64, :] * (a[0] ** 2 + a[1] ** 2) + edge[64:128, :] * (b[0] ** 2 + b[1] ** 2))

    def body(kx, total):
        v = spec[pl.ds(pl.multiple_of(kx * 128, 128), 128), :].astype(F32)
        w = weight[pl.ds(pl.multiple_of(kx * 64, 64), 64), :]
        return total + fold(w * (v[:64] ** 2 + v[64:] ** 2))
    return lax.fori_loop(1, 32, body, total, unroll=31)


def wedge_setup(spec, flip_rows, flip_lanes, weight, edge):
    g = spec[0:128, :]
    t = mirror(g, jnp.abs(flip_rows), flip_lanes)
    edge[...] = 0.5 * (g.astype(F32) + t)

    def body(kx, _):
        v = spec[pl.ds(pl.multiple_of(kx * 128, 128), 128), :].astype(F32)
        weight[pl.ds(pl.multiple_of(kx * 64, 64), 64), :] = v[:64] + v[64:]
        return 0
    lax.fori_loop(1, 32, body, 0)


def spread_half(v, s, low):
    r = pltpu.roll(v, 64, 1)
    return jnp.where(low, v, r) if s == 0 else jnp.where(low, r, v)


def reference_setup(spec, twin, weight, edge, low, filt, extra):
    a, b = split(spec[0:128, :].astype(F32), twin)
    w0, w32 = edge[0:64, :], edge[64:128, :]
    for s in range(2):
        p = [spread_half(v, s, low) for v in (w0 * a[0], -w0 * a[1])]
        q = [spread_half(v, s, low) for v in (w32 * b[0], -w32 * b[1])]
        for k in range(2):
            filt[s, 64 * k:64 * k + 64, :] = 0.5 * (p[k] + q[k])
            extra[s, 64 * k:64 * k + 64, :] = 0.5 * (p[k] - q[k])

    def body(kx, _):
        v = spec[pl.ds(pl.multiple_of(kx * 128, 128), 128), :].astype(F32)
        w = weight[pl.ds(pl.multiple_of(kx * 64, 64), 64), :]
        re, im = w * v[:64], -w * v[64:]
        for s in range(2):
            filt[s, pl.ds(pl.multiple_of(kx * 128, 128), 64), :] = spread_half(re, s, low)
            filt[s, pl.ds(pl.multiple_of(kx * 128 + 64, 64), 64), :] = spread_half(im, s, low)
        return 0
    lax.fori_loop(1, 32, body, 0)


def correlate(spec, twin, filt, extra, ty, tz, tx, left, plane):
    def times(v, w):
        return (v[:64] * w[:64] - v[64:] * w[64:], v[:64] * w[64:] + v[64:] * w[:64])

    def cross(kx):
        at = pl.multiple_of(kx * 128, 128)
        return times(spec[pl.ds(at, 128), :].astype(F32), filt[pl.ds(at, 128), :])

    def finish(m, parts):
        d = jnp.concatenate([jnp.concatenate(p, 0).astype(BF) for p in parts], 1)
        r = dot(ty, d).astype(BF)
        for k in range(2):
            rows = pl.ds(pl.multiple_of((2 * m + k) * 64, 64), 64)
            left[rows, 0:128] = r[:64, k * 128:k * 128 + 128]
            left[rows, 128:256] = r[64:, k * 128:k * 128 + 128]

    c0, e0 = cross(0), times(twin, extra)
    finish(0, [(c0[0] + e0[0], c0[1] + e0[1]), cross(1)])

    def y_pass(m, _):
        finish(m, [cross(2 * m), cross(2 * m + 1)])
        return 0
    lax.fori_loop(1, 16, y_pass, 0, unroll=15)

    def z_pass(m, _):
        at = pl.multiple_of(m * 256, 256)
        r = dot(left[pl.ds(at, 256), 0:256], tz)
        for p in range(2):
            plane[pl.ds(p * 2048 + at, 256), :] = r[:, p * 128:p * 128 + 128]
        return 0
    lax.fori_loop(0, 8, z_pass, 0, unroll=8)

    def x_pass(m, top):
        d = jnp.concatenate(
            [plane[pl.ds(2 * m + k, 64, stride=64), :] for k in range(2)], 1).astype(BF)
        r = dot(tx, d)
        return jnp.maximum(top, jnp.maximum(r[:, :128], r[:, 128:]))
    top = lax.fori_loop(0, 32, x_pass, jnp.full((64, 128), -jnp.inf, F32), unroll=16)
    return functools.reduce(jnp.maximum, [top[8 * k:8 * k + 8] for k in range(8)])


def score_kernel(v, refs, wedge, txf, tzf, tyf, tyi, tzi, txi, fr, fl, out,
                 left, plane, spec, rspec, twin, weight, edge, filt, extra):
    low = lax.broadcasted_iota(jnp.int32, (64, 128), 1) < 64
    low8 = low[:8]

    def halves(t, op, fill):
        f = jnp.max if op == "max" else jnp.sum
        return [f(jnp.where(low8 == (k == 0), t, fill), keepdims=True) for k in range(2)]

    forward(wedge, wedge, txf[1], tzf[1], tyf[1], left, plane, rspec)
    wedge_setup(rspec, fr[...], fl[...], weight, edge)
    forward(refs.at[0], refs.at[1], txf[0], tzf[0], tyf[0], left, plane, rspec)
    rt = mirror(rspec[0:128, :], fr[...], fl[...])
    rp = halves(power(rspec, rt, weight, edge), "sum", 0.0)
    reference_setup(rspec, rt, weight, edge, low, filt, extra)
    row = lax.broadcasted_iota(jnp.int32, (8, 128), 0)
    lane = lax.broadcasted_iota(jnp.int32, (8, 128), 1)

    def one_pair(pair, result):
        forward(v.at[2 * pair], v.at[2 * pair + 1], txf[0], tzf[0], tyf[0], left, plane, spec)
        t = mirror(spec[0:128, :], fr[...], fl[...])
        own = halves(power(spec, t, weight, edge), "sum", 0.0)

        def one_step(s, result):
            top = halves(correlate(spec, t, filt.at[s], extra[s], tyi[...], tzi[...], txi[...], left, plane), "max", -jnp.inf)
            for k in range(2):
                norm = jnp.sqrt(own[k] * jnp.where(s == 0, rp[0], rp[1]) / float(N ** 3) + 1e-6)
                result = jnp.where((row == s) & (lane == 2 * pair + k), top[k] / norm, result)
            return result
        return lax.fori_loop(0, 2, one_step, result)
    out[...] = lax.fori_loop(0, 3, one_pair, jnp.zeros((8, 128), F32))


def scores_call(v, refs, wedge):
    tables = [jnp.asarray(t, dtype=BF) for t in score_tables()]
    return pl.pallas_call(
        score_kernel,
        out_shape=jax.ShapeDtypeStruct((8, 128), F32),
        in_specs=[pl.BlockSpec(memory_space=pltpu.VMEM)] * 11,
        out_specs=pl.BlockSpec(memory_space=pltpu.VMEM),
        scratch_shapes=[
            pltpu.VMEM((2048, 512), BF), pltpu.VMEM((4096, 128), F32),
            pltpu.VMEM((4096, 128), BF), pltpu.VMEM((4096, 128), BF),
            pltpu.VMEM((128, 128), F32), pltpu.VMEM((2048, 128), F32), pltpu.VMEM((128, 128), F32),
            pltpu.VMEM((2, 4096, 128), F32), pltpu.VMEM((2, 128, 128), F32),
        ],
        compiler_params=pltpu.CompilerParams(vmem_limit_bytes=50 * 2**20),
    )(v, refs, wedge, *tables)


def turn_tables():
    eye, rev = np.eye(N), np.eye(N)[::-1]
    two, swap = np.eye(2), np.eye(2)[::-1]
    pair = np.concatenate([eye, eye], 1)
    lanes = np.einsum("ac,hg,zw->ahzgcw", two, two, eye).reshape(256, 256)
    rows = np.transpose(eye.reshape(N, 32, 2), (0, 2, 1)).reshape(N, N)
    flip_rows = np.stack([eye, rev])
    flip_lanes = np.stack([np.kron(a, b) for a in (two, swap) for b in (eye, rev)])
    return [pair, lanes, rows, flip_rows, flip_lanes]


def turn_kernel(pick, classes, v, pair, lanes, rows, flip_rows, flip_lanes, out, held, wide, mixed, sums):
    low = lax.broadcasted_iota(jnp.int32, (64, 128), 1) < 64

    def clear(k, _):
        sums[pl.ds(pl.multiple_of(k * 512, 512), 512), :] = jnp.zeros((512, 128), F32)
        return 0
    lax.fori_loop(0, 64, clear, 0)

    def swap_ends():
        def body(m, _):
            blocks = []
            for k in range(2):
                blk = held[pl.ds(pl.multiple_of((2 * m + k) * 64, 64), 64), :].astype(F32)
                blocks += [jnp.where(low, blk, 0.0), jnp.where(low, 0.0, blk)]
            w = jnp.concatenate(blocks, 0).astype(BF)
            r = lax.dot_general(pair[...], w, (((1,), (1,)), ((), ())), preferred_element_type=F32).astype(BF)
            for k in range(2):
                held[pl.ds(pl.multiple_of((2 * m + k) * 64, 64), 64), :] = r[:, k * 128:k * 128 + 128]
            return 0
        lax.fori_loop(0, 16, body, 0, unroll=16)

    def swap_first():
        def widen(m, _):
            at = pl.ds(pl.multiple_of(m * 256, 256), 256)
            wide[at, :] = held[at, :].astype(F32)
            return 0
        lax.fori_loop(0, 8, widen, 0, unroll=8)

        def gather(m, _):
            d = [wide[pl.ds(2 * m + k, 32, stride=64), :] for k in range(2)]
            mixed[pl.ds(pl.multiple_of(m * 32, 32), 32), :] = jnp.concatenate(d, 1).astype(BF)
            return 0
        lax.fori_loop(0, 32, gather, 0, unroll=32)

        def body(m, _):
            r = dot(mixed[pl.ds(pl.multiple_of(m * 256, 256), 256), :], lanes[...]).astype(BF)
            halves = [jnp.concatenate([r[k * 32:k * 32 + 32, h * 128:h * 128 + 128] for k in range(8)], 1)
                      for h in range(2)]
            t = dot(rows[...], jnp.concatenate(halves, 0)).astype(BF)
            for k in range(8):
                held[pl.ds(pl.multiple_of((m * 8 + k) * 64, 64), 64), :] = t[:, k * 128:k * 128 + 128]
            return 0
        lax.fori_loop(0, 4, body, 0, unroll=4)

    def one(i, _):
        number = pick[i]
        order, place = number // 4, number % 4
        even = (order == 0) | (order == 3) | (order == 4)
        f0 = jnp.where(even, (place == 1) | (place == 2), (place == 0) | (place == 3)).astype(jnp.int32)
        f1 = place % 2
        f2 = place // 2
        for b in range(32):
            held[b * 64:b * 64 + 64, :] = v[i, :, b * 128:b * 128 + 128]
        pl.when((order == 1) | (order == 3) | (order == 5))(swap_ends)
        pl.when((order >= 1) & (order <= 4))(swap_first)
        pl.when((order == 1) | (order == 4))(swap_ends)
        c = classes[i]
        base = ((c % 2) * 8 + c // 2) * 2048
        j0, jl = flip_rows[f0], flip_lanes[f1 * 2 + f2]

        def flip_ends(m, _):
            at = pl.ds(pl.multiple_of(m * 256, 256), 256)
            held[at, :] = dot(held[at, :], jl).astype(BF)
            return 0

        @pl.when(f1 + f2 > 0)
        def _():
            lax.fori_loop(0, 8, flip_ends, 0, unroll=8)

        def add(m, flipped):
            blocks = []
            for k in range(4):
                b = m * 4 + k
                src = b + f1 * (31 - 2 * b)
                blocks.append(held[pl.ds(pl.multiple_of(src * 64, 64), 64), :])
            if flipped:
                u = dot(j0, jnp.concatenate(blocks, 1))
                blocks = [u[:, k * 128:k * 128 + 128] for k in range(4)]
            for k in range(4):
                at = pl.ds(base + m * 4 + k, 64, stride=32)
                sums[at, :] = sums[at, :] + blocks[k].astype(F32)

        @pl.when(f0 > 0)
        def _():
            lax.fori_loop(0, 8, lambda m, c: (add(m, True), c)[1], 0, unroll=8)

        @pl.when(f0 == 0)
        def _():
            lax.fori_loop(0, 8, lambda m, c: (add(m, False), c)[1], 0, unroll=8)
        return 0
    lax.fori_loop(0, 6, one, 0)

    def narrow(k, _):
        at = pl.ds(pl.multiple_of(k * 512, 512), 512)
        out[at, :] = sums[at, :].astype(BF)
        return 0
    lax.fori_loop(0, 64, narrow, 0)


def turn_call(v, pick, classes):
    tables = [jnp.asarray(t, dtype=BF) for t in turn_tables()]
    vm = pl.BlockSpec(memory_space=pltpu.VMEM)
    return pl.pallas_call(
        turn_kernel,
        out_shape=jax.ShapeDtypeStruct((32768, 128), BF),
        in_specs=[pl.BlockSpec(memory_space=pltpu.SMEM)] * 2 + [vm] * 6,
        out_specs=vm,
        scratch_shapes=[pltpu.VMEM((2048, 128), BF), pltpu.VMEM((2048, 128), F32), pltpu.VMEM((1024, 256), BF), pltpu.VMEM((32768, 128), F32)],
        compiler_params=pltpu.CompilerParams(vmem_limit_bytes=50 * 2**20),
    )(pick, classes, v, *tables)


PARTS = (
    ((0, 1, 2), False, 0, 48), ((0, 1, 2), True, 48, 32),
    ((1, 2, 0), False, 80, 48), ((1, 2, 0), True, 128, 32),
    ((2, 0, 1), False, 160, 48), ((2, 0, 1), True, 208, 48),
)
MOVES = 10


class Place:
    def __init__(self):
        tomo, orient = lax.axis_index("tomo"), lax.axis_index("orient")
        self.core = orient % 2
        self.at = (orient // 4, (tomo // 4) * 2 + (orient // 2) % 2, tomo % 4)
        self.near = tuple(c + 1 - 2 * (c % 2) for c in self.at)
        self.far = tuple(3 - c for c in self.at)
        self.cross = tuple((c + 2) % 4 for c in self.at)

    def device(self, axis=None, to=None, core=None):
        z, y, x = [to if axis == k else c for k, c in enumerate(self.at)]
        core = self.core if core is None else core
        return ((y // 2) * 4 + x, z * 4 + (y % 2) * 2 + core)

    def other_core(self):
        return self.device(core=1 - self.core)

    def partners(self):
        return [self.other_core()] + [self.device(k, t[k]) for k in range(3) for t in (self.near, self.far)]


def greet(place):
    barrier = pltpu.get_barrier_semaphore()
    for device in place.partners():
        pl.semaphore_signal(barrier, inc=1, device_id=device, device_id_type=MESH)
    pl.semaphore_wait(barrier, 7)


class ClassSums:
    def __init__(self, place, sums, mine, got, keep, send, first, second, total, send_sem, recv_sem, load_sem):
        self.p, self.sums, self.mine, self.got, self.keep, self.send = place, sums, mine, got, keep, send
        self.first, self.second, self.total = first, second, total
        self.send_sem, self.recv_sem = send_sem, recv_sem
        self.load = pltpu.make_async_copy(sums.at[place.core], mine, load_sem)
        self.sent = []
        self.coming = {}

    def move(self, part, k, src, dst, device):
        copy = pltpu.make_async_remote_copy(
            src_ref=src, dst_ref=dst, send_sem=self.send_sem.at[part * MOVES + k],
            recv_sem=self.recv_sem.at[part * MOVES + k], device_id=device, device_id_type=MESH)
        copy.start()
        self.sent.append(copy)
        self.coming[part, k] = copy

    def start(self):
        for i, (_, _, row, rows) in enumerate(PARTS):
            cells = pl.ds(row, rows)
            self.move(i, 0, self.sums.at[1 - self.p.core, :, cells, :], self.got.at[:, cells, :], self.p.other_core())
        self.load.start()

    def links(self, part, level):
        axis = PARTS[part][0][level]
        near, far = self.p.near[axis], self.p.far[axis]
        f, g = (far, near) if PARTS[part][1] else (near, far)
        return axis, self.p.at[axis], f, g, self.p.cross[axis]

    def prefix(self, part, level):
        base = 0
        for k in range(level):
            base = base + self.p.at[PARTS[part][0][k]] * 4 ** (2 - k)
        return base, 4 ** (2 - level)

    def halves(self, part, level, value):
        _, _, row, rows = PARTS[part]
        cells = pl.ds(row, rows)
        axis, c, f, g, h = self.links(part, level)
        base, size = self.prefix(part, level)
        for slot, d in ((1, h), (0, f)):
            def out(k, _, d=d):
                at = base + d * size + k
                self.send[at, cells, :] = value(d * size + k).astype(BF)
                return 0
            lax.fori_loop(0, size, out, 0, unroll=min(size, 4))
            self.move(part, 1 + 3 * level + slot, self.send.at[pl.ds(base + d * size, size), cells, :],
                      self.first[level].at[slot, :, cells, :], self.p.device(axis, f))
        for d in (g, c):
            def stay(k, _, d=d):
                self.keep[base + d * size + k, cells, :] = value(d * size + k)
                return 0
            lax.fori_loop(0, size, stay, 0, unroll=min(size, 4))

    def round(self, r):
        for part in range(len(PARTS)):
            self.step(r, part)

    def step(self, r, part):
        order, _, row, rows = PARTS[part]
        cells = pl.ds(row, rows)
        if r == 0:
            if part == 0:
                self.load.wait()
            self.coming[part, 0].wait_recv()

            def value(at):
                d = (at // 16, at // 4 % 4, at % 4)
                z, y, x = [d[order.index(k)] for k in range(3)]
                src = (z * 2 + y % 2) * 8 + (y // 2) * 4 + x
                return self.mine[src, cells, :].astype(F32) + self.got[src, cells, :].astype(F32)
            self.halves(part, 0, value)
            return
        level = (r - 1) // 2
        axis, c, f, g, h = self.links(part, level)
        base, size = self.prefix(part, level)
        if r % 2:
            self.coming[part, 2 + 3 * level].wait_recv()

            def body(k, _):
                at = base + g * size + k
                v = self.keep[at, cells, :] + self.first[level][1, k, cells, :].astype(F32)
                self.send[at, cells, :] = v.astype(BF)
                return 0
            lax.fori_loop(0, size, body, 0, unroll=min(size, 4))
            self.move(part, 3 + 3 * level, self.send.at[pl.ds(base + g * size, size), cells, :],
                      self.second[level].at[:, cells, :], self.p.device(axis, g))
            return
        self.coming[part, 1 + 3 * level].wait_recv()
        self.coming[part, 3 + 3 * level].wait_recv()

        def value(k):
            return (self.keep[base + c * size + k, cells, :] + self.first[level][0, k, cells, :].astype(F32)
                    + self.second[level][k, cells, :].astype(F32))
        if level < 2:
            self.halves(part, level + 1, value)
        else:
            self.total[cells, :] = value(0)

    def finish(self):
        for copy in self.sent:
            copy.wait_send()

    @staticmethod
    def scratch():
        vm = pltpu.VMEM
        return [
            vm((64, 256, 128), BF), vm((64, 256, 128), BF), vm((64, 256, 128), F32), vm((64, 256, 128), BF),
            vm((2, 16, 256, 128), BF), vm((2, 4, 256, 128), BF), vm((2, 1, 256, 128), BF),
            vm((16, 256, 128), BF), vm((4, 256, 128), BF), vm((1, 256, 128), BF),
            vm((256, 128), F32),
            pltpu.SemaphoreType.DMA((len(PARTS) * MOVES,)), pltpu.SemaphoreType.DMA((len(PARTS) * MOVES,)),
            pltpu.SemaphoreType.DMA(()),
        ]


class Counts:
    def __init__(self, place, own, held, got, send_sem, recv_sem):
        self.p, self.held, self.got, self.send_sem, self.recv_sem = place, held, got, send_sem, recv_sem
        held[0] = own[...]
        self.partners = place.partners()
        self.sent = []

    def go(self, k):
        copy = pltpu.make_async_remote_copy(
            src_ref=self.held.at[k], dst_ref=self.got.at[k], send_sem=self.send_sem.at[k],
            recv_sem=self.recv_sem.at[k], device_id=self.partners[k], device_id_type=MESH)
        copy.start()
        self.sent.append(copy)

    def start(self):
        self.go(0)

    def round(self, k):
        self.sent[k].wait_recv()
        self.held[k + 1] = self.held[k] + self.got[k]
        if k < 6:
            self.go(k + 1)

    def result(self):
        return self.held[7]

    def finish(self):
        for copy in self.sent:
            copy.wait_send()

    @staticmethod
    def scratch():
        return [pltpu.VMEM((8, 8, 128), F32), pltpu.VMEM((7, 8, 128), F32),
                pltpu.SemaphoreType.DMA((7,)), pltpu.SemaphoreType.DMA((7,))]


class References:
    def __init__(self, place, own, full, half, acc, zfirst, zsecond, pass_on, yown, ysend, ygot, send_sem, recv_sem):
        self.p, self.own, self.full, self.half, self.acc = place, own, full, half, acc
        self.zfirst, self.zsecond, self.pass_on = zfirst, zsecond, pass_on
        self.yown, self.ysend, self.ygot = yown, ysend, ygot
        self.send_sem, self.recv_sem = send_sem, recv_sem
        self.sent, self.coming = [], {}
        c = place.at[0]
        self.c = c
        self.f = (place.near[0], place.far[0])
        self.g = (place.far[0], place.near[0])
        self.h = place.cross[0]
        self.ylo = place.at[1] % 2
        self.lane = place.core * 2048

    def move(self, s, k, src, dst, device):
        copy = pltpu.make_async_remote_copy(
            src_ref=src, dst_ref=dst, send_sem=self.send_sem.at[s * 10 + k], recv_sem=self.recv_sem.at[s * 10 + k],
            device_id=device, device_id_type=MESH)
        copy.start()
        self.sent.append(copy)
        self.coming[s, k] = copy

    def lanes(self, at, size):
        return pl.ds(pl.multiple_of(at, 256), size)

    def share(self, s, k, at, size, device):
        cells = self.full.at[s, :, self.lanes(at, size)]
        self.move(s, k, cells, cells, device)

    def start(self):
        for s in range(2):
            other = self.lanes((1 - self.p.core) * 2048, 2048)
            self.move(s, 0, self.own.at[s, :, other], self.half.at[s], self.p.other_core())

    def round(self, r):
        for s in range(2):
            self.step(r, s)

    def step(self, r, s):
        f, g, c, h = self.f[s], self.g[s], self.c, self.h
        to_f, to_g = self.p.device(0, f), self.p.device(0, g)
        to_y = self.p.device(1, self.p.near[1])
        chunk = self.lane + c * 512
        if r == 0:
            self.coming[s, 0].wait_recv()
            for k in range(4):
                mine = self.own[s, :, self.lanes(self.lane + k * 512, 512)]
                self.acc[s, k] = mine + self.half[s, :, k * 512:k * 512 + 512]
            self.move(s, 2, self.acc.at[s, h], self.zfirst.at[s, 1], to_f)
            self.move(s, 1, self.acc.at[s, f], self.zfirst.at[s, 0], to_f)
        elif r == 1:
            self.coming[s, 2].wait_recv()
            self.pass_on[s] = self.acc[s, g] + self.zfirst[s, 1]
            self.move(s, 3, self.pass_on.at[s], self.zsecond.at[s], to_g)
        elif r == 2:
            self.coming[s, 1].wait_recv()
            self.coming[s, 3].wait_recv()
            v = self.acc[s, c] + self.zfirst[s, 0] + self.zsecond[s]
            low = self.ylo == 0
            self.yown[s] = jnp.where(low, v[:, :256], v[:, 256:])
            self.ysend[s] = jnp.where(low, v[:, 256:], v[:, :256])
            self.move(s, 4, self.ysend.at[s], self.ygot.at[s], to_y)
        elif r == 3:
            self.coming[s, 4].wait_recv()
            at = chunk + self.ylo * 256
            self.full[s, :, self.lanes(at, 256)] = self.yown[s] + self.ygot[s]
            self.share(s, 5, at, 256, to_y)
        elif r == 4:
            self.coming[s, 5].wait_recv()
            self.share(s, 6, chunk, 512, to_g)
        elif r == 5:
            self.coming[s, 6].wait_recv()
            self.share(s, 7, chunk, 512, to_f)
            self.share(s, 8, self.lane + g * 512, 512, to_f)
        elif r == 6:
            self.coming[s, 7].wait_recv()
            self.coming[s, 8].wait_recv()
            self.share(s, 9, self.lane, 2048, self.p.other_core())
        else:
            self.coming[s, 9].wait_recv()

    def finish(self):
        for copy in self.sent:
            copy.wait_send()

    @staticmethod
    def scratch():
        vm = pltpu.VMEM
        return [
            vm((2, 64, 4096), BF), vm((2, 64, 2048), BF), vm((2, 4, 64, 512), BF), vm((2, 2, 64, 512), BF),
            vm((2, 64, 512), BF), vm((2, 64, 512), BF), vm((2, 64, 256), BF), vm((2, 64, 256), BF), vm((2, 64, 256), BF),
            pltpu.SemaphoreType.DMA((20,)), pltpu.SemaphoreType.DMA((20,)),
        ]


def average(total, counts, orient, out):
    lane = lax.broadcasted_iota(jnp.int32, (8, 128), 1)
    row = lax.broadcasted_iota(jnp.int32, (8, 128), 0)
    count = jnp.sum(jnp.where((lane == orient) & (row == 0), counts, 0.0), keepdims=True)
    for b in range(32):
        out[0, :, b * 128:b * 128 + 128] = total[pl.ds(b, 8, stride=32), :] / count


def exchange_kernel(own_refs, sums, counts, full_out, out, *scratch):
    place = Place()
    a, b, c = len(ClassSums.scratch()), len(Counts.scratch()), len(References.scratch())
    s = scratch[:a]
    classes = ClassSums(place, sums, s[0], s[1], s[2], s[3], s[4:7], s[7:10], s[10], s[11], s[12], s[13])
    tally = Counts(place, counts, *scratch[a:a + b])
    refs = References(place, own_refs, *scratch[a + b:a + b + c])
    greet(place)
    refs.start()
    tally.start()
    classes.start()
    for r in range(8):
        refs.round(r)
        if r < 7:
            tally.round(r)
            classes.round(r)
    full_out[...] = refs.full[...]
    average(classes.total, tally.result(), lax.axis_index("orient"), out)
    for part in (refs, tally, classes):
        part.finish()


def exchange_call(own_refs, sums, counts):
    vm = pl.BlockSpec(memory_space=pltpu.VMEM)
    return pl.pallas_call(
        exchange_kernel,
        out_shape=(jax.ShapeDtypeStruct((2, 64, 4096), BF), jax.ShapeDtypeStruct((1, 8, 4096), F32)),
        in_specs=[vm, pl.BlockSpec(memory_space=pl.ANY), vm],
        out_specs=(vm, vm),
        scratch_shapes=ClassSums.scratch() + Counts.scratch() + References.scratch(),
        compiler_params=pltpu.CompilerParams(
            collective_id=0, has_side_effects=True, vmem_limit_bytes=56 * 2**20),
    )(own_refs, sums.reshape(2, 64, 256, 128), counts)


def local(subtomograms, rotated_refs, wedges, ref_pick, best_pick, class_of):
    orient_size, orient_index = lax.axis_size("orient"), lax.axis_index("orient")
    per = rotated_refs.shape[0]
    wedge = lax.dynamic_index_in_dim(wedges, orient_index * wedges.shape[0] // orient_size, 0, False)
    mine = [
        jnp.where(
            ref_pick[s] // per == orient_index,
            lax.dynamic_index_in_dim(rotated_refs, ref_pick[s] % per, 0, False), 0
        ) for s in range(STEPS)
    ]
    class_index = class_of[:, 0]
    sums = turn_call(subtomograms, best_pick, class_index)
    hits = class_index[None, :] == jnp.arange(128, dtype=jnp.int32)[:, None]
    counts = jnp.broadcast_to(jnp.sum(hits.astype(F32), axis=1)[None], (8, 128))
    refs, averages = exchange_call(jnp.stack(mine), sums, counts)
    result = scores_call(subtomograms, refs, wedge)
    return (result[:STEPS, :subtomograms.shape[0]], averages)


def solution(mesh):
    placed = (
        P(("tomo", "orient"), None, None),
        P("orient", None, None),
        P("tomo", None, None),
        P(),
        P(("tomo", "orient")),
        P(("tomo", "orient"), None),
    )
    return jax.shard_map(
        local,
        mesh=mesh,
        in_specs=placed,
        out_specs=(P(None, ("tomo", "orient")), P("orient", "tomo", None)),
        check_vma=False,
    )
```

```python
import functools

import jax
import jax.numpy as jnp
import numpy as np
from jax import lax
from jax.experimental import pallas as pl
from jax.experimental.pallas import tpu as pltpu
from jax.sharding import PartitionSpec as P

STEPS = 2
CLASSES = 16
N = 64
BF = jnp.bfloat16
F32 = jnp.float32
MESH = pl.DeviceIdType.MESH
PITCH_FWD = 36
PITCH_INV = 68
PITCH_WIDE = 68
PITCH_TOTAL = 36


def score_tables():
    i = np.arange(N)
    ang = (i[:, None] * i[None, :] % N) * (2.0 * np.pi / N)
    c, s = np.cos(ang), np.sin(ang)
    c[np.abs(c) < 1e-9] = 0.0
    s[np.abs(s) < 1e-9] = 0.0
    h = N // 2
    eye, rev = np.eye(N), np.eye(N)[(-i) % N]

    def pairs(m00, m01, m10, m11):
        return np.array([[m00, m01], [m10, m11]])

    def lanes_forward(b):
        t = np.einsum("abzk,qr,hg->qahzbgrk", b, np.eye(2), np.eye(2))
        return t.reshape(512, 512)

    def rows_forward(b):
        t = np.transpose(b, (1, 3, 0, 2)).reshape(2, N, 2, h, 2)
        return np.transpose(t, (0, 1, 2, 4, 3)).reshape(128, 128)

    fwd = pairs(c, -s, s, c)
    wdg = pairs(eye, 0 * eye, 0 * eye, rev)
    inv = pairs(c, s, -s, c)
    x_fwd = np.concatenate([c[:h], -s[:h]], 0)
    x_fwd[h] = c[h]
    x_wdg = np.concatenate([eye[:h], rev[:h]], 0)
    x_wdg[h] = eye[h]
    y_inv = np.transpose(inv, (1, 3, 0, 2)).reshape(128, 128)
    z_inv = np.einsum("abzk,qr->aqzbrk", inv, np.eye(2)).reshape(256, 256)
    x_inv = x_fwd.T
    flip_rows = np.kron(np.diag([1.0, -1.0]), rev)
    flip_lanes = np.kron(np.eye(2), rev)
    return [
        np.stack([x_fwd, x_wdg]),
        np.stack([lanes_forward(fwd), lanes_forward(wdg)]),
        np.stack([rows_forward(fwd), rows_forward(wdg)]),
        y_inv, z_inv, x_inv, flip_rows, flip_lanes,
    ]


def dot(a, b):
    return jnp.dot(a, b, preferred_element_type=F32)


def forward_x(vol, q, tx, left):
    def x_pass(c, _):
        at = pl.multiple_of(c * 512, 512)
        r = dot(tx, vol[:, pl.ds(at, 512)]).astype(BF)
        for k in range(4):
            rows = pl.ds(pl.multiple_of((c * 4 + k) * 32, 32), 32)
            left[rows, q * 256:q * 256 + 128] = r[:32, k * 128:k * 128 + 128]
            left[rows, q * 256 + 128:q * 256 + 256] = r[32:, k * 128:k * 128 + 128]
        return 0
    lax.fori_loop(0, 8, x_pass, 0, unroll=8)


def forward_z(tz, left, plane):
    def z_pass(m, _):
        at = pl.multiple_of(m * 128, 128)
        r = dot(left[pl.ds(at, 128), :], tz)
        for col in range(4):
            for k in range(4):
                row = (col * 32 + m * 4 + k) * PITCH_FWD
                plane[pl.ds(row, 32), :] = r[k * 32:k * 32 + 32, col * 128:col * 128 + 128]
        return 0
    lax.fori_loop(0, 8, z_pass, 0, unroll=8)


def forward_y(ty, plane, out):
    def y_pass(m, _):
        d = jnp.concatenate(
            [plane[pl.ds(2 * m + k, 128, stride=PITCH_FWD), :] for k in range(2)], 1).astype(BF)
        r = dot(ty, d).astype(BF)
        for k in range(2):
            out[pl.ds(pl.multiple_of((2 * m + k) * 128, 128), 128), :] = r[:, k * 128:k * 128 + 128]
        return 0
    lax.fori_loop(0, 16, y_pass, 0, unroll=16)


def mirror(g, flip_rows, flip_lanes):
    return dot(dot(flip_rows, g).astype(BF), flip_lanes)


def split(g, t):
    gr, gi, tr, ti = g[:64], g[64:], t[:64], t[64:]
    return (0.5 * (gr + tr), 0.5 * (gi + ti)), (0.5 * (gi - ti), -0.5 * (gr - tr))


def fold(v):
    return functools.reduce(jnp.add, [v[8 * k:8 * k + 8] for k in range(v.shape[0] // 8)])


def power(spec, twin, weight, edge):
    a, b = split(spec[0:128, :].astype(F32), twin)
    total = fold(edge[0:64, :] * (a[0] ** 2 + a[1] ** 2) + edge[64:128, :] * (b[0] ** 2 + b[1] ** 2))

    def body(kx, total):
        v = spec[pl.ds(pl.multiple_of(kx * 128, 128), 128), :].astype(F32)
        w = weight[pl.ds(pl.multiple_of(kx * 64, 64), 64), :]
        return total + fold(w * (v[:64] ** 2 + v[64:] ** 2))
    return lax.fori_loop(1, 32, body, total, unroll=31)


def wedge_setup(spec, flip_rows, flip_lanes, weight, edge):
    g = spec[0:128, :]
    t = mirror(g, jnp.abs(flip_rows), flip_lanes)
    edge[...] = 0.5 * (g.astype(F32) + t)

    def body(kx, _):
        v = spec[pl.ds(pl.multiple_of(kx * 128, 128), 128), :].astype(F32)
        weight[pl.ds(pl.multiple_of(kx * 64, 64), 64), :] = v[:64] + v[64:]
        return 0
    lax.fori_loop(1, 32, body, 0)


def spread_half(v, s, low):
    r = pltpu.roll(v, 64, 1)
    return jnp.where(low, v, r) if s == 0 else jnp.where(low, r, v)


def reference_setup(spec, twin, weight, edge, low, filt, extra):
    a, b = split(spec[0:128, :].astype(F32), twin)
    w0, w32 = edge[0:64, :], edge[64:128, :]
    for s in range(2):
        p = [spread_half(v, s, low) for v in (w0 * a[0], -w0 * a[1])]
        q = [spread_half(v, s, low) for v in (w32 * b[0], -w32 * b[1])]
        for k in range(2):
            filt[s, 64 * k:64 * k + 64, :] = 0.5 * (p[k] + q[k])
            extra[s, 64 * k:64 * k + 64, :] = 0.5 * (p[k] - q[k])

    def body(kx, _):
        v = spec[pl.ds(pl.multiple_of(kx * 128, 128), 128), :].astype(F32)
        w = weight[pl.ds(pl.multiple_of(kx * 64, 64), 64), :]
        re, im = w * v[:64], -w * v[64:]
        for s in range(2):
            filt[s, pl.ds(pl.multiple_of(kx * 128, 128), 64), :] = spread_half(re, s, low)
            filt[s, pl.ds(pl.multiple_of(kx * 128 + 64, 64), 64), :] = spread_half(im, s, low)
        return 0
    lax.fori_loop(1, 32, body, 0)


def correlate_y(spec, twin, filt, extra, ty, left):
    def times(v, w):
        return (v[:64] * w[:64] - v[64:] * w[64:], v[:64] * w[64:] + v[64:] * w[:64])

    def cross(kx):
        at = pl.multiple_of(kx * 128, 128)
        return times(spec[pl.ds(at, 128), :].astype(F32), filt[pl.ds(at, 128), :])

    def finish(m, parts):
        d = jnp.concatenate([jnp.concatenate(p, 0).astype(BF) for p in parts], 1)
        r = dot(ty, d).astype(BF)
        for k in range(2):
            rows = pl.ds(pl.multiple_of((2 * m + k) * 64, 64), 64)
            left[rows, 0:128] = r[:64, k * 128:k * 128 + 128]
            left[rows, 128:256] = r[64:, k * 128:k * 128 + 128]

    c0, e0 = cross(0), times(twin, extra)
    finish(0, [(c0[0] + e0[0], c0[1] + e0[1]), cross(1)])

    def y_pass(m, _):
        finish(m, [cross(2 * m), cross(2 * m + 1)])
        return 0
    lax.fori_loop(1, 16, y_pass, 0, unroll=15)


def correlate_z(tz, left, plane):
    def z_pass(m, _):
        at = pl.multiple_of(m * 256, 256)
        r = dot(left[pl.ds(at, 256), 0:256], tz)
        for p in range(2):
            for k in range(4):
                row = (p * 32 + m * 4 + k) * PITCH_INV
                plane[pl.ds(row, 64), :] = r[k * 64:k * 64 + 64, p * 128:p * 128 + 128]
        return 0
    lax.fori_loop(0, 8, z_pass, 0, unroll=8)


def correlate_x(tx, plane):
    def x_pass(m, top):
        d = jnp.concatenate(
            [plane[pl.ds(2 * m + k, 64, stride=PITCH_INV), :] for k in range(2)], 1).astype(BF)
        r = dot(tx, d)
        return jnp.maximum(top, jnp.maximum(r[:, :128], r[:, 128:]))
    top = lax.fori_loop(0, 32, x_pass, jnp.full((64, 128), -jnp.inf, F32), unroll=16)
    return functools.reduce(jnp.maximum, [top[8 * k:8 * k + 8] for k in range(8)])


def turn_tables():
    eye, rev = np.eye(N), np.eye(N)[::-1]
    two, swap = np.eye(2), np.eye(2)[::-1]
    pair = np.concatenate([eye, eye], 1)
    lanes = np.einsum("ac,hg,zw->ahzgcw", two, two, eye).reshape(256, 256)
    rows = np.transpose(eye.reshape(N, 32, 2), (0, 2, 1)).reshape(N, N)
    flip_rows = np.stack([eye, rev])
    flip_lanes = np.stack([np.kron(a, b) for a in (two, swap) for b in (eye, rev)])
    return [pair, lanes, rows, flip_rows, flip_lanes]


def turn_kernel(ref_pick, pick, classes, refs, v, pair, lanes, rows, flip_rows, flip_lanes,
                out, own_refs, counts, held, wide, mixed, total, narrow, empty, out_sem, ref_sem):
    low = lax.broadcasted_iota(jnp.int32, (64, 128), 1) < 64
    me, per = lax.axis_index("orient"), refs.shape[0]

    def fetch(s):
        return pltpu.make_async_copy(refs.at[ref_pick[s] % per], own_refs.at[s], ref_sem.at[s])

    for s in range(2):
        @pl.when(ref_pick[s] // per == me)
        def _():
            fetch(s).start()

        @pl.when(ref_pick[s] // per != me)
        def _():
            own_refs[s] = jnp.zeros(own_refs.shape[1:], BF)

    def store(c, src):
        return pltpu.make_async_copy(src, out.at[c % 2, c // 2], out_sem.at[c])

    empty[...] = jnp.zeros(empty.shape, BF)
    lane = lax.broadcasted_iota(jnp.int32, (8, 128), 1)
    tally = jnp.zeros((8, 128), F32)
    for i in range(6):
        tally = tally + (lane == classes[i]).astype(F32)
    counts[...] = tally
    for c in range(CLASSES):
        hit = classes[0] == c
        for i in range(1, 6):
            hit = hit | (classes[i] == c)

        @pl.when(jnp.logical_not(hit))
        def _():
            store(c, empty).start()

    def swap_ends():
        def body(m, _):
            blocks = []
            for k in range(2):
                blk = held[pl.ds(pl.multiple_of((2 * m + k) * 64, 64), 64), :].astype(F32)
                blocks += [jnp.where(low, blk, 0.0), jnp.where(low, 0.0, blk)]
            w = jnp.concatenate(blocks, 0).astype(BF)
            r = lax.dot_general(pair[...], w, (((1,), (1,)), ((), ())), preferred_element_type=F32).astype(BF)
            for k in range(2):
                held[pl.ds(pl.multiple_of((2 * m + k) * 64, 64), 64), :] = r[:, k * 128:k * 128 + 128]
            return 0
        lax.fori_loop(0, 16, body, 0, unroll=16)

    def swap_first():
        def widen(m, _):
            for k in range(4):
                b = m * 4 + k
                blk = held[pl.ds(pl.multiple_of(b * 64, 64), 64), :]
                wide[pl.ds(b * PITCH_WIDE, 64), :] = blk.astype(F32)
            return 0
        lax.fori_loop(0, 8, widen, 0, unroll=8)

        def gather(m, _):
            d = [wide[pl.ds(2 * m + k, 32, stride=PITCH_WIDE), :] for k in range(2)]
            mixed[pl.ds(pl.multiple_of(m * 32, 32), 32), :] = jnp.concatenate(d, 1).astype(BF)
            return 0
        lax.fori_loop(0, 32, gather, 0, unroll=32)

        def body(m, _):
            r = dot(mixed[pl.ds(pl.multiple_of(m * 256, 256), 256), :], lanes[...]).astype(BF)
            halves = [jnp.concatenate([r[k * 32:k * 32 + 32, h * 128:h * 128 + 128] for k in range(8)], 1)
                      for h in range(2)]
            t = dot(rows[...], jnp.concatenate(halves, 0)).astype(BF)
            for k in range(8):
                held[pl.ds(pl.multiple_of((m * 8 + k) * 64, 64), 64), :] = t[:, k * 128:k * 128 + 128]
            return 0
        lax.fori_loop(0, 4, body, 0, unroll=4)

    def turn(i, first):
        number = pick[i]
        order, place = number // 4, number % 4
        even = (order == 0) | (order == 3) | (order == 4)
        f0 = jnp.where(even, (place == 1) | (place == 2), (place == 0) | (place == 3)).astype(jnp.int32)
        f1 = place % 2
        f2 = place // 2
        for b in range(32):
            held[b * 64:b * 64 + 64, :] = v[i, :, b * 128:b * 128 + 128]
        pl.when((order == 1) | (order == 3) | (order == 5))(swap_ends)
        pl.when((order >= 1) & (order <= 4))(swap_first)
        pl.when((order == 1) | (order == 4))(swap_ends)
        j0, jl = flip_rows[f0], flip_lanes[f1 * 2 + f2]

        def flip_ends(m, _):
            at = pl.ds(pl.multiple_of(m * 256, 256), 256)
            held[at, :] = dot(held[at, :], jl).astype(BF)
            return 0

        @pl.when(f1 + f2 > 0)
        def _():
            lax.fori_loop(0, 8, flip_ends, 0, unroll=8)

        def add(m, flipped):
            blocks = []
            for k in range(4):
                b = m * 4 + k
                src = b + f1 * (31 - 2 * b)
                blocks.append(held[pl.ds(pl.multiple_of(src * 64, 64), 64), :])
            if flipped:
                u = dot(j0, jnp.concatenate(blocks, 1))
                blocks = [u[:, k * 128:k * 128 + 128] for k in range(4)]
            for k in range(4):
                at = pl.ds(m * 4 + k, 64, stride=PITCH_TOTAL)
                u = blocks[k].astype(F32)
                total[at, :] = u if first else total[at, :] + u

        @pl.when(f0 > 0)
        def _():
            lax.fori_loop(0, 8, lambda m, c: (add(m, True), c)[1], 0, unroll=8)

        @pl.when(f0 == 0)
        def _():
            lax.fori_loop(0, 8, lambda m, c: (add(m, False), c)[1], 0, unroll=8)

    def one(i, _):
        c = classes[i]

        def count(j, n):
            return n + (classes[j] == c).astype(jnp.int32)

        @pl.when(lax.fori_loop(0, i, count, 0) == 0)
        def _():
            turn(i, True)

            def later(j, _):
                @pl.when(classes[j] == c)
                def _():
                    turn(j, False)
                return 0
            lax.fori_loop(i + 1, 6, later, 0)

            def shorten(k, _):
                for d in range(8):
                    at = pl.ds(pl.multiple_of(k * 256 + d * 32, 32), 32)
                    narrow[i, at, :] = total[pl.ds((k * 8 + d) * PITCH_TOTAL, 32), :].astype(BF)
                return 0
            lax.fori_loop(0, 8, shorten, 0, unroll=8)
            store(c, narrow.at[i]).start()
        return 0
    lax.fori_loop(0, 6, one, 0)

    for s in range(2):
        @pl.when(ref_pick[s] // per == me)
        def _():
            fetch(s).wait()
    for c in range(CLASSES):
        store(c, empty).wait()


def turn_call(ref_pick, pick, classes, refs, v):
    tables = [jnp.asarray(t, dtype=BF) for t in turn_tables()]
    sm, vm, far = [pl.BlockSpec(memory_space=m) for m in (pltpu.SMEM, pltpu.VMEM, pl.ANY)]
    return pl.pallas_call(
        turn_kernel,
        out_shape=(
            jax.ShapeDtypeStruct((2, 8, 2048, 128), BF),
            jax.ShapeDtypeStruct((2,) + refs.shape[1:], BF),
            jax.ShapeDtypeStruct((8, 128), F32),
        ),
        in_specs=[sm] * 3 + [far] + [vm] * 6,
        out_specs=(far, vm, vm),
        scratch_shapes=[
            pltpu.VMEM((2048, 128), BF), pltpu.VMEM((2304, 128), F32), pltpu.VMEM((1024, 256), BF),
            pltpu.VMEM((2560, 128), F32), pltpu.VMEM((6, 2048, 128), BF), pltpu.VMEM((2048, 128), BF),
            pltpu.SemaphoreType.DMA((CLASSES,)), pltpu.SemaphoreType.DMA((2,)),
        ],
        compiler_params=pltpu.CompilerParams(vmem_limit_bytes=40 * 2**20),
    )(ref_pick, pick, classes, refs, v, *tables)


PARTS = (
    ((0, 1, 2), False, 0, 48), ((0, 1, 2), True, 48, 32),
    ((1, 2, 0), False, 80, 48), ((1, 2, 0), True, 128, 32),
    ((2, 0, 1), False, 160, 48), ((2, 0, 1), True, 208, 48),
)
MOVES = 10


class Place:
    def __init__(self):
        tomo, orient = lax.axis_index("tomo"), lax.axis_index("orient")
        self.core = orient % 2
        self.at = (orient // 4, (tomo // 4) * 2 + (orient // 2) % 2, tomo % 4)
        self.near = tuple(c + 1 - 2 * (c % 2) for c in self.at)
        self.far = tuple(3 - c for c in self.at)
        self.cross = tuple((c + 2) % 4 for c in self.at)

    def device(self, axis=None, to=None, core=None):
        z, y, x = [to if axis == k else c for k, c in enumerate(self.at)]
        core = self.core if core is None else core
        return ((y // 2) * 4 + x, z * 4 + (y % 2) * 2 + core)

    def other_core(self):
        return self.device(core=1 - self.core)

    def partners(self):
        return [self.other_core()] + [self.device(k, t[k]) for k in range(3) for t in (self.near, self.far)]


def greet(place):
    barrier = pltpu.get_barrier_semaphore()
    for device in place.partners():
        pl.semaphore_signal(barrier, inc=1, device_id=device, device_id_type=MESH)
    pl.semaphore_wait(barrier, 7)


class ClassSums:
    def __init__(self, place, sums, mine, got, keep, send, first, second, total, send_sem, recv_sem, load_sem):
        self.p, self.sums, self.mine, self.got, self.keep, self.send = place, sums, mine, got, keep, send
        self.first, self.second, self.total = first, second, total
        self.send_sem, self.recv_sem = send_sem, recv_sem
        self.load = pltpu.make_async_copy(sums.at[place.core], mine, load_sem)
        self.sent = []
        self.coming = {}

    def move(self, part, k, src, dst, device):
        copy = pltpu.make_async_remote_copy(
            src_ref=src, dst_ref=dst, send_sem=self.send_sem.at[part * MOVES + k],
            recv_sem=self.recv_sem.at[part * MOVES + k], device_id=device, device_id_type=MESH)
        copy.start()
        self.sent.append(copy)
        self.coming[part, k] = copy

    def start(self):
        for i, (_, _, row, rows) in enumerate(PARTS):
            cells = pl.ds(row, rows)
            self.move(i, 0, self.sums.at[1 - self.p.core, :, cells, :], self.got.at[:, cells, :], self.p.other_core())
        self.load.start()

    def links(self, part, level):
        axis = PARTS[part][0][level]
        near, far = self.p.near[axis], self.p.far[axis]
        f, g = (far, near) if PARTS[part][1] else (near, far)
        return axis, self.p.at[axis], f, g, self.p.cross[axis]

    def prefix(self, part, level):
        base = 0
        for k in range(level):
            base = base + self.p.at[PARTS[part][0][k]] * 4 ** (2 - k)
        return base, 4 ** (2 - level)

    def halves(self, part, level, value):
        _, _, row, rows = PARTS[part]
        cells = pl.ds(row, rows)
        axis, c, f, g, h = self.links(part, level)
        base, size = self.prefix(part, level)
        for slot, d in ((1, h), (0, f)):
            def out(k, _, d=d):
                at = base + d * size + k
                self.send[at, cells, :] = value(d * size + k).astype(BF)
                return 0
            lax.fori_loop(0, size, out, 0, unroll=min(size, 4))
            self.move(part, 1 + 3 * level + slot, self.send.at[pl.ds(base + d * size, size), cells, :],
                      self.first[level].at[slot, :, cells, :], self.p.device(axis, f))
        for d in (g, c):
            def stay(k, _, d=d):
                self.keep[base + d * size + k, cells, :] = value(d * size + k)
                return 0
            lax.fori_loop(0, size, stay, 0, unroll=min(size, 4))

    def round(self, r):
        for part in range(len(PARTS)):
            self.step(r, part)

    def step(self, r, part):
        order, _, row, rows = PARTS[part]
        cells = pl.ds(row, rows)
        if r == 0:
            if part == 0:
                self.load.wait()
            self.coming[part, 0].wait_recv()

            def value(at):
                d = (at // 16, at // 4 % 4, at % 4)
                z, y, x = [d[order.index(k)] for k in range(3)]
                src = (z * 2 + y % 2) * 8 + (y // 2) * 4 + x
                return self.mine[src, cells, :].astype(F32) + self.got[src, cells, :].astype(F32)
            self.halves(part, 0, value)
            return
        level = (r - 1) // 2
        axis, c, f, g, h = self.links(part, level)
        base, size = self.prefix(part, level)
        if r % 2:
            self.coming[part, 2 + 3 * level].wait_recv()

            def body(k, _):
                at = base + g * size + k
                v = self.keep[at, cells, :] + self.first[level][1, k, cells, :].astype(F32)
                self.send[at, cells, :] = v.astype(BF)
                return 0
            lax.fori_loop(0, size, body, 0, unroll=min(size, 4))
            self.move(part, 3 + 3 * level, self.send.at[pl.ds(base + g * size, size), cells, :],
                      self.second[level].at[:, cells, :], self.p.device(axis, g))
            return
        self.coming[part, 1 + 3 * level].wait_recv()
        self.coming[part, 3 + 3 * level].wait_recv()

        def value(k):
            return (self.keep[base + c * size + k, cells, :] + self.first[level][0, k, cells, :].astype(F32)
                    + self.second[level][k, cells, :].astype(F32))
        if level < 2:
            self.halves(part, level + 1, value)
        else:
            self.total[cells, :] = value(0)

    def finish(self):
        for copy in self.sent:
            copy.wait_send()

    @staticmethod
    def scratch():
        vm = pltpu.VMEM
        return [
            vm((64, 256, 128), BF), vm((64, 256, 128), BF), vm((64, 256, 128), F32), vm((64, 256, 128), BF),
            vm((2, 16, 256, 128), BF), vm((2, 4, 256, 128), BF), vm((2, 1, 256, 128), BF),
            vm((16, 256, 128), BF), vm((4, 256, 128), BF), vm((1, 256, 128), BF),
            vm((256, 128), F32),
            pltpu.SemaphoreType.DMA((len(PARTS) * MOVES,)), pltpu.SemaphoreType.DMA((len(PARTS) * MOVES,)),
            pltpu.SemaphoreType.DMA(()),
        ]


class Counts:
    def __init__(self, place, own, held, got, send_sem, recv_sem):
        self.p, self.held, self.got, self.send_sem, self.recv_sem = place, held, got, send_sem, recv_sem
        held[0] = own[...]
        self.partners = place.partners()
        self.sent = []

    def go(self, k):
        copy = pltpu.make_async_remote_copy(
            src_ref=self.held.at[k], dst_ref=self.got.at[k], send_sem=self.send_sem.at[k],
            recv_sem=self.recv_sem.at[k], device_id=self.partners[k], device_id_type=MESH)
        copy.start()
        self.sent.append(copy)

    def start(self):
        self.go(0)

    def round(self, k):
        self.sent[k].wait_recv()
        self.held[k + 1] = self.held[k] + self.got[k]
        if k < 6:
            self.go(k + 1)

    def result(self):
        return self.held[7]

    def finish(self):
        for copy in self.sent:
            copy.wait_send()

    @staticmethod
    def scratch():
        return [pltpu.VMEM((8, 8, 128), F32), pltpu.VMEM((7, 8, 128), F32),
                pltpu.SemaphoreType.DMA((7,)), pltpu.SemaphoreType.DMA((7,))]


class References:
    def __init__(self, place, own, full, half, acc, zfirst, zsecond, pass_on, yown, ysend, ygot, send_sem, recv_sem):
        self.p, self.own, self.full, self.half, self.acc = place, own, full, half, acc
        self.zfirst, self.zsecond, self.pass_on = zfirst, zsecond, pass_on
        self.yown, self.ysend, self.ygot = yown, ysend, ygot
        self.send_sem, self.recv_sem = send_sem, recv_sem
        self.sent, self.coming = [], {}
        c = place.at[0]
        self.c = c
        self.f = (place.near[0], place.far[0])
        self.g = (place.far[0], place.near[0])
        self.h = place.cross[0]
        self.ylo = place.at[1] % 2
        self.lane = place.core * 2048

    def move(self, s, k, src, dst, device):
        copy = pltpu.make_async_remote_copy(
            src_ref=src, dst_ref=dst, send_sem=self.send_sem.at[s * 10 + k], recv_sem=self.recv_sem.at[s * 10 + k],
            device_id=device, device_id_type=MESH)
        copy.start()
        self.sent.append(copy)
        self.coming[s, k] = copy

    def lanes(self, at, size):
        return pl.ds(pl.multiple_of(at, 256), size)

    def share(self, s, k, at, size, device):
        cells = self.full.at[s, :, self.lanes(at, size)]
        self.move(s, k, cells, cells, device)

    def start(self):
        for s in range(2):
            other = self.lanes((1 - self.p.core) * 2048, 2048)
            self.move(s, 0, self.own.at[s, :, other], self.half.at[s], self.p.other_core())

    def round(self, r):
        for s in range(2):
            self.step(r, s)

    def step(self, r, s):
        f, g, c, h = self.f[s], self.g[s], self.c, self.h
        to_f, to_g = self.p.device(0, f), self.p.device(0, g)
        to_y = self.p.device(1, self.p.near[1])
        chunk = self.lane + c * 512
        if r == 0:
            self.coming[s, 0].wait_recv()
            for k in range(4):
                mine = self.own[s, :, self.lanes(self.lane + k * 512, 512)]
                self.acc[s, k] = mine + self.half[s, :, k * 512:k * 512 + 512]
            self.move(s, 2, self.acc.at[s, h], self.zfirst.at[s, 1], to_f)
            self.move(s, 1, self.acc.at[s, f], self.zfirst.at[s, 0], to_f)
        elif r == 1:
            self.coming[s, 2].wait_recv()
            self.pass_on[s] = self.acc[s, g] + self.zfirst[s, 1]
            self.move(s, 3, self.pass_on.at[s], self.zsecond.at[s], to_g)
        elif r == 2:
            self.coming[s, 1].wait_recv()
            self.coming[s, 3].wait_recv()
            v = self.acc[s, c] + self.zfirst[s, 0] + self.zsecond[s]
            low = self.ylo == 0
            self.yown[s] = jnp.where(low, v[:, :256], v[:, 256:])
            self.ysend[s] = jnp.where(low, v[:, 256:], v[:, :256])
            self.move(s, 4, self.ysend.at[s], self.ygot.at[s], to_y)
        elif r == 3:
            self.coming[s, 4].wait_recv()
            at = chunk + self.ylo * 256
            self.full[s, :, self.lanes(at, 256)] = self.yown[s] + self.ygot[s]
            self.share(s, 5, at, 256, to_y)
        elif r == 4:
            self.coming[s, 5].wait_recv()
            self.share(s, 6, chunk, 512, to_g)
        elif r == 5:
            self.coming[s, 6].wait_recv()
            self.share(s, 7, chunk, 512, to_f)
            self.share(s, 8, self.lane + g * 512, 512, to_f)
        elif r == 6:
            self.coming[s, 7].wait_recv()
            self.coming[s, 8].wait_recv()
            self.share(s, 9, self.lane, 2048, self.p.other_core())
        else:
            self.coming[s, 9].wait_recv()

    def finish(self):
        for copy in self.sent:
            copy.wait_send()

    @staticmethod
    def scratch():
        vm = pltpu.VMEM
        return [
            vm((2, 64, 4096), BF), vm((2, 64, 2048), BF), vm((2, 4, 64, 512), BF), vm((2, 2, 64, 512), BF),
            vm((2, 64, 512), BF), vm((2, 64, 512), BF), vm((2, 64, 256), BF), vm((2, 64, 256), BF), vm((2, 64, 256), BF),
            pltpu.SemaphoreType.DMA((20,)), pltpu.SemaphoreType.DMA((20,)),
        ]


def average(total, counts, orient, out):
    lane = lax.broadcasted_iota(jnp.int32, (8, 128), 1)
    row = lax.broadcasted_iota(jnp.int32, (8, 128), 0)
    count = jnp.sum(jnp.where((lane == orient) & (row == 0), counts, 0.0), keepdims=True)
    for b in range(32):
        out[0, :, b * 128:b * 128 + 128] = total[pl.ds(b, 8, stride=32), :] / count


class Scores:
    def __init__(self, v, wedge, full, tables, out, scratch):
        self.v, self.wedge, self.full, self.out = v, wedge, full, out
        self.txf, self.tzf, self.tyf, self.tyi, self.tzi, self.txi, self.fr, self.fl = tables
        self.left, self.plane, self.spec, self.rspec, self.weight, self.edge, self.filt, self.extra = scratch
        self.low = lax.broadcasted_iota(jnp.int32, (64, 128), 1) < 64
        self.row = lax.broadcasted_iota(jnp.int32, (8, 128), 0)
        self.lane = lax.broadcasted_iota(jnp.int32, (8, 128), 1)
        self.result = jnp.zeros((8, 128), F32)
        self.twin, self.own = {}, {}

    def halves(self, t, op, fill):
        return [op(jnp.where(self.low[:8] == (k == 0), t, fill), keepdims=True) for k in range(2)]

    def forward(self, first, second, kind, out):
        def x():
            forward_x(first, 0, self.txf[kind], self.left)
            forward_x(second, 1, self.txf[kind], self.left)
        return [
            (0.6, x),
            (0.9, lambda: forward_z(self.tzf[kind], self.left, self.plane)),
            (0.6, lambda: forward_y(self.tyf[kind], self.plane, out)),
        ]

    def mirror(self, spec):
        return mirror(spec[0:128, :], self.fr[...], self.fl[...])

    def wedge_work(self):
        return self.forward(self.wedge, self.wedge, 1, self.rspec) + [
            (0.2, lambda: wedge_setup(self.rspec, self.fr[...], self.fl[...], self.weight, self.edge))]

    def pair_work(self, pair):
        spec = self.spec.at[pair]

        def after():
            self.twin[pair] = self.mirror(spec)
            self.own[pair] = self.halves(power(spec, self.twin[pair], self.weight, self.edge), jnp.sum, 0.0)
        return self.forward(self.v.at[2 * pair], self.v.at[2 * pair + 1], 0, spec) + [(0.3, after)]

    def reference_work(self):
        def after():
            t = self.mirror(self.rspec)
            self.norm = self.halves(power(self.rspec, t, self.weight, self.edge), jnp.sum, 0.0)
            reference_setup(self.rspec, t, self.weight, self.edge, self.low, self.filt, self.extra)
        return self.forward(self.full.at[0], self.full.at[1], 0, self.rspec) + [(0.7, after)]

    def score_work(self, pair, s):
        def last():
            top = self.halves(correlate_x(self.txi[...], self.plane), jnp.max, -jnp.inf)
            for k in range(2):
                score = top[k] / jnp.sqrt(self.own[pair][k] * self.norm[s] / float(N ** 3) + 1e-6)
                self.result = jnp.where((self.row == s) & (self.lane == 2 * pair + k), score, self.result)
        return [
            (1.0, lambda: correlate_y(self.spec.at[pair], self.twin[pair], self.filt.at[s], self.extra[s],
                                      self.tyi[...], self.left)),
            (0.6, lambda: correlate_z(self.tzi[...], self.left, self.plane)),
            (0.8, last),
        ]

    def finish(self):
        self.out[...] = self.result[:self.out.shape[0], :self.out.shape[1]]

    @staticmethod
    def scratch():
        vm = pltpu.VMEM
        return [
            vm((2048, 512), BF), vm((4608, 128), F32), vm((3, 4096, 128), BF), vm((4096, 128), BF),
            vm((2048, 128), F32), vm((128, 128), F32), vm((2, 4096, 128), F32), vm((2, 128, 128), F32),
        ]


def interleave(work, events):
    events = sorted(events, key=lambda e: e[0])
    clock = 0.0
    for length, piece in work:
        while events and events[0][0] <= clock:
            events.pop(0)[1]()
        piece()
        clock += length
    for _, action in events:
        action()


REF_TIMES = (1.5, 2.4, 3.3, 4.2, 5.4, 6.3, 7.5, 9.2)
CLASS_TIMES = ((2.2, 1.2), (10.0, 1.0), (16.0, 0.8), (21.0, 0.4), (24.0, 0.3), (26.0, 0.3), (28.0, 0.2))


def fused_kernel(own_refs, sums, counts, v, wedges, *rest):
    tables, (scores_out, out), scratch = rest[:8], rest[8:10], rest[10:]
    place = Place()
    ends = np.cumsum([0] + [len(c.scratch()) for c in (ClassSums, Counts, References, Scores)])
    s, tally_s, refs_s, score_s = [scratch[i:j] for i, j in zip(ends, ends[1:])]
    classes = ClassSums(place, sums, s[0], s[1], s[2], s[3], s[4:7], s[7:10], s[10], s[11], s[12], s[13])
    tally = Counts(place, counts, *tally_s)
    refs = References(place, own_refs, *refs_s)
    orient = lax.axis_index("orient")
    scores = Scores(v, wedges.at[orient * wedges.shape[0] // lax.axis_size("orient")], refs.full, tables, scores_out, score_s)
    greet(place)
    refs.start()
    tally.start()
    classes.start()
    events = [(t, functools.partial(refs.round, r)) for r, t in enumerate(REF_TIMES)]
    for r, (t, gap) in enumerate(CLASS_TIMES):
        events += [(t + gap * part, functools.partial(classes.step, r, part)) for part in range(len(PARTS))]
        events.append((t + gap * len(PARTS), functools.partial(tally.round, r)))
    work = scores.wedge_work()
    for pair in range(3):
        work += scores.pair_work(pair)
    work += scores.reference_work()
    for pair in range(3):
        for step in range(STEPS):
            work += scores.score_work(pair, step)
    interleave(work, events)
    scores.finish()
    average(classes.total, tally.result(), orient, out)
    for part in (refs, tally, classes):
        part.finish()


def fused_call(own_refs, sums, counts, v, wedges):
    tables = [jnp.asarray(t, dtype=BF) for t in score_tables()]
    vm = pl.BlockSpec(memory_space=pltpu.VMEM)
    return pl.pallas_call(
        fused_kernel,
        out_shape=(jax.ShapeDtypeStruct((STEPS, v.shape[0]), F32), jax.ShapeDtypeStruct((1, 8, 4096), F32)),
        in_specs=[vm, pl.BlockSpec(memory_space=pl.ANY)] + [vm] * 11,
        out_specs=(vm, vm),
        scratch_shapes=sum([c.scratch() for c in (ClassSums, Counts, References, Scores)], []),
        compiler_params=pltpu.CompilerParams(
            collective_id=0, has_side_effects=True, vmem_limit_bytes=60 * 2**20),
    )(own_refs, sums.reshape(2, 64, 256, 128), counts, v, wedges, *tables)


def local(subtomograms, rotated_refs, wedges, ref_pick, best_pick, class_of):
    sums, own_refs, counts = turn_call(ref_pick, best_pick, class_of[:, 0], rotated_refs, subtomograms)
    return fused_call(own_refs, sums, counts, subtomograms, wedges)


def solution(mesh):
    placed = (
        P(("tomo", "orient"), None, None),
        P("orient", None, None),
        P("tomo", None, None),
        P(),
        P(("tomo", "orient")),
        P(("tomo", "orient"), None),
    )
    return jax.shard_map(
        local,
        mesh=mesh,
        in_specs=placed,
        out_specs=(P(None, ("tomo", "orient")), P("orient", "tomo", None)),
        check_vma=False,
    )
```

```python
import functools

import jax
import jax.numpy as jnp
import numpy as np
from jax import lax
from jax.experimental import pallas as pl
from jax.experimental.pallas import tpu as pltpu
from jax.sharding import PartitionSpec as P

STEPS = 2
CLASSES = 16
N = 64
BF = jnp.bfloat16
F32 = jnp.float32
MESH = pl.DeviceIdType.MESH
PITCH_FWD = 36
PITCH_INV = 68
PITCH_WIDE = 68
PITCH_TOTAL = 36


def score_tables():
    i = np.arange(N)
    ang = (i[:, None] * i[None, :] % N) * (2.0 * np.pi / N)
    c, s = np.cos(ang), np.sin(ang)
    c[np.abs(c) < 1e-9] = 0.0
    s[np.abs(s) < 1e-9] = 0.0
    h = N // 2
    eye, rev = np.eye(N), np.eye(N)[(-i) % N]

    def pairs(m00, m01, m10, m11):
        return np.array([[m00, m01], [m10, m11]])

    def lanes_forward(b):
        t = np.einsum("abzk,qr,hg->qahzbgrk", b, np.eye(2), np.eye(2))
        return t.reshape(512, 512)

    def rows_forward(b):
        t = np.transpose(b, (1, 3, 0, 2)).reshape(2, N, 2, h, 2)
        return np.transpose(t, (0, 1, 2, 4, 3)).reshape(128, 128)

    fwd = pairs(c, -s, s, c)
    wdg = pairs(eye, 0 * eye, 0 * eye, rev)
    inv = pairs(c, s, -s, c)
    x_fwd = np.concatenate([c[:h], -s[:h]], 0)
    x_fwd[h] = c[h]
    x_wdg = np.concatenate([eye[:h], rev[:h]], 0)
    x_wdg[h] = eye[h]
    y_inv = np.transpose(inv, (1, 3, 0, 2)).reshape(128, 128)
    z_inv = np.einsum("abzk,qr->aqzbrk", inv, np.eye(2)).reshape(256, 256)
    x_inv = x_fwd.T
    flip_rows = np.kron(np.diag([1.0, -1.0]), rev)
    flip_lanes = np.kron(np.eye(2), rev)
    table = np.zeros((1408, 512))
    for k, t in enumerate((fwd, wdg)):
        table[512 * k:512 * k + 512] = lanes_forward(t)
        table[1024 + 128 * k:1152 + 128 * k, 256:384] = rows_forward(t)
    table[1024:1280, :256] = z_inv
    table[1024:1152, 384:] = y_inv
    table[1152:1280, 384:] = flip_rows
    table[1280:, :128] = flip_lanes
    table[1280:1344, 128:192] = x_fwd
    table[1344:, 128:192] = x_wdg
    table[1280:1344, 256:320] = x_inv
    return table


def table_views(table):
    return (
        [table.at[1280:1344, 128:192], table.at[1344:1408, 128:192]],
        [table.at[0:512, :], table.at[512:1024, :]],
        [table.at[1024:1152, 256:384], table.at[1152:1280, 256:384]],
        table.at[1024:1152, 384:512], table.at[1024:1280, 0:256], table.at[1280:1344, 256:320],
        table.at[1152:1280, 384:512], table.at[1280:1408, 0:128],
    )


def dot(a, b):
    return jnp.dot(a, b, preferred_element_type=F32)


def forward_x(vol, q, tx, left):
    def x_pass(c, _):
        at = pl.multiple_of(c * 512, 512)
        r = dot(tx, vol[:, pl.ds(at, 512)]).astype(BF)
        for k in range(4):
            rows = pl.ds(pl.multiple_of((c * 4 + k) * 32, 32), 32)
            left[rows, q * 256:q * 256 + 128] = r[:32, k * 128:k * 128 + 128]
            left[rows, q * 256 + 128:q * 256 + 256] = r[32:, k * 128:k * 128 + 128]
        return 0
    lax.fori_loop(0, 8, x_pass, 0, unroll=8)


def forward_z(tz, left, plane):
    def z_pass(m, _):
        at = pl.multiple_of(m * 128, 128)
        r = dot(left[pl.ds(at, 128), :], tz)
        for col in range(4):
            for k in range(4):
                row = (col * 32 + m * 4 + k) * PITCH_FWD
                plane[pl.ds(row, 32), :] = r[k * 32:k * 32 + 32, col * 128:col * 128 + 128]
        return 0
    lax.fori_loop(0, 8, z_pass, 0, unroll=8)


def forward_y(ty, plane, out):
    def y_pass(m, _):
        d = jnp.concatenate(
            [plane[pl.ds(2 * m + k, 128, stride=PITCH_FWD), :] for k in range(2)], 1).astype(BF)
        r = dot(ty, d).astype(BF)
        for k in range(2):
            out[pl.ds(pl.multiple_of((2 * m + k) * 128, 128), 128), :] = r[:, k * 128:k * 128 + 128]
        return 0
    lax.fori_loop(0, 16, y_pass, 0, unroll=16)


def mirror(g, flip_rows, flip_lanes):
    return dot(dot(flip_rows, g).astype(BF), flip_lanes)


def split(g, t):
    gr, gi, tr, ti = g[:64], g[64:], t[:64], t[64:]
    return (0.5 * (gr + tr), 0.5 * (gi + ti)), (0.5 * (gi - ti), -0.5 * (gr - tr))


def fold(v):
    return functools.reduce(jnp.add, [v[8 * k:8 * k + 8] for k in range(v.shape[0] // 8)])


def power(spec, twin, weight, edge):
    a, b = split(spec[0:128, :].astype(F32), twin)
    total = fold(edge[0:64, :] * (a[0] ** 2 + a[1] ** 2) + edge[64:128, :] * (b[0] ** 2 + b[1] ** 2))

    def body(kx, total):
        v = spec[pl.ds(pl.multiple_of(kx * 128, 128), 128), :].astype(F32)
        w = weight[pl.ds(pl.multiple_of(kx * 64, 64), 64), :]
        return total + fold(w * (v[:64] ** 2 + v[64:] ** 2))
    return lax.fori_loop(1, 32, body, total, unroll=31)


def wedge_setup(spec, flip_rows, flip_lanes, weight, edge):
    g = spec[0:128, :]
    t = mirror(g, jnp.abs(flip_rows), flip_lanes)
    edge[...] = 0.5 * (g.astype(F32) + t)

    def body(kx, _):
        v = spec[pl.ds(pl.multiple_of(kx * 128, 128), 128), :].astype(F32)
        weight[pl.ds(pl.multiple_of(kx * 64, 64), 64), :] = v[:64] + v[64:]
        return 0
    lax.fori_loop(1, 32, body, 0)


def spread_half(v, s, low):
    r = pltpu.roll(v, 64, 1)
    return jnp.where(low, v, r) if s == 0 else jnp.where(low, r, v)


def reference_setup(spec, twin, weight, edge, low, filt, extra):
    a, b = split(spec[0:128, :].astype(F32), twin)
    w0, w32 = edge[0:64, :], edge[64:128, :]
    for s in range(2):
        p = [spread_half(v, s, low) for v in (w0 * a[0], -w0 * a[1])]
        q = [spread_half(v, s, low) for v in (w32 * b[0], -w32 * b[1])]
        for k in range(2):
            filt[s, 64 * k:64 * k + 64, :] = 0.5 * (p[k] + q[k])
            extra[s, 64 * k:64 * k + 64, :] = 0.5 * (p[k] - q[k])

    def body(kx, _):
        v = spec[pl.ds(pl.multiple_of(kx * 128, 128), 128), :].astype(F32)
        w = weight[pl.ds(pl.multiple_of(kx * 64, 64), 64), :]
        re, im = w * v[:64], -w * v[64:]
        for s in range(2):
            filt[s, pl.ds(pl.multiple_of(kx * 128, 128), 64), :] = spread_half(re, s, low)
            filt[s, pl.ds(pl.multiple_of(kx * 128 + 64, 64), 64), :] = spread_half(im, s, low)
        return 0
    lax.fori_loop(1, 32, body, 0)


def correlate_y(spec, twin, filt, extra, ty, left):
    def times(v, w):
        return (v[:64] * w[:64] - v[64:] * w[64:], v[:64] * w[64:] + v[64:] * w[:64])

    def cross(kx):
        at = pl.multiple_of(kx * 128, 128)
        return times(spec[pl.ds(at, 128), :].astype(F32), filt[pl.ds(at, 128), :])

    def finish(m, parts):
        d = jnp.concatenate([jnp.concatenate(p, 0).astype(BF) for p in parts], 1)
        r = dot(ty, d).astype(BF)
        for k in range(2):
            rows = pl.ds(pl.multiple_of((2 * m + k) * 64, 64), 64)
            left[rows, 0:128] = r[:64, k * 128:k * 128 + 128]
            left[rows, 128:256] = r[64:, k * 128:k * 128 + 128]

    c0, e0 = cross(0), times(twin, extra)
    finish(0, [(c0[0] + e0[0], c0[1] + e0[1]), cross(1)])

    def y_pass(m, _):
        finish(m, [cross(2 * m), cross(2 * m + 1)])
        return 0
    lax.fori_loop(1, 16, y_pass, 0, unroll=15)


def correlate_z(tz, left, plane):
    def z_pass(m, _):
        at = pl.multiple_of(m * 256, 256)
        r = dot(left[pl.ds(at, 256), 0:256], tz)
        for p in range(2):
            for k in range(4):
                row = (p * 32 + m * 4 + k) * PITCH_INV
                plane[pl.ds(row, 64), :] = r[k * 64:k * 64 + 64, p * 128:p * 128 + 128]
        return 0
    lax.fori_loop(0, 8, z_pass, 0, unroll=8)


def correlate_x(tx, plane):
    def x_pass(m, top):
        d = jnp.concatenate(
            [plane[pl.ds(2 * m + k, 64, stride=PITCH_INV), :] for k in range(2)], 1).astype(BF)
        r = dot(tx, d)
        return jnp.maximum(top, jnp.maximum(r[:, :128], r[:, 128:]))
    top = lax.fori_loop(0, 32, x_pass, jnp.full((64, 128), -jnp.inf, F32), unroll=16)
    return functools.reduce(jnp.maximum, [top[8 * k:8 * k + 8] for k in range(8)])


def turn_tables():
    eye, rev = np.eye(N), np.eye(N)[::-1]
    two, swap = np.eye(2), np.eye(2)[::-1]
    pair = np.concatenate([eye, eye], 1)
    lanes = np.einsum("ac,hg,zw->ahzgcw", two, two, eye).reshape(256, 256)
    rows = np.transpose(eye.reshape(N, 32, 2), (0, 2, 1)).reshape(N, N)
    flip_rows = np.stack([eye, rev])
    flip_lanes = np.stack([np.kron(a, b) for b in (eye, rev) for a in (two, swap)])
    table = np.zeros((512, 512))
    table[:256, :256] = lanes
    table[:, 256:384] = flip_lanes.reshape(512, 128)
    table[:64, 384:] = pair
    table[64:128, 384:448] = rows
    table[128:256, 384:448] = flip_rows.reshape(128, 64)
    return table


def turn_kernel(ref_pick, pick, classes, refs, v, table,
                out, own_refs, counts, held, wide, mixed, total, narrow, empty, out_sem, ref_sem):
    pair, lanes, rows = table.at[0:64, 384:512], table.at[0:256, 0:256], table.at[64:128, 384:448]
    low = lax.broadcasted_iota(jnp.int32, (64, 128), 1) < 64
    me, per = lax.axis_index("orient"), refs.shape[0]

    def fetch(s):
        return pltpu.make_async_copy(refs.at[ref_pick[s] % per], own_refs.at[s], ref_sem.at[s])

    for s in range(2):
        @pl.when(ref_pick[s] // per == me)
        def _():
            fetch(s).start()

        @pl.when(ref_pick[s] // per != me)
        def _():
            own_refs[s] = jnp.zeros(own_refs.shape[1:], BF)

    def store(c, src):
        return pltpu.make_async_copy(src, out.at[c % 2, c // 2], out_sem.at[c])

    empty[...] = jnp.zeros(empty.shape, BF)
    lane = lax.broadcasted_iota(jnp.int32, (8, 128), 1)
    tally = jnp.zeros((8, 128), F32)
    for i in range(6):
        tally = tally + (lane == classes[i]).astype(F32)
    counts[...] = tally
    for c in range(CLASSES):
        hit = classes[0] == c
        for i in range(1, 6):
            hit = hit | (classes[i] == c)

        @pl.when(jnp.logical_not(hit))
        def _():
            store(c, empty).start()

    def swap_ends():
        def body(m, _):
            blocks = []
            for k in range(2):
                blk = held[pl.ds(pl.multiple_of((2 * m + k) * 64, 64), 64), :].astype(F32)
                blocks += [jnp.where(low, blk, 0.0), jnp.where(low, 0.0, blk)]
            w = jnp.concatenate(blocks, 0).astype(BF)
            r = lax.dot_general(pair[...], w, (((1,), (1,)), ((), ())), preferred_element_type=F32).astype(BF)
            for k in range(2):
                held[pl.ds(pl.multiple_of((2 * m + k) * 64, 64), 64), :] = r[:, k * 128:k * 128 + 128]
            return 0
        lax.fori_loop(0, 16, body, 0, unroll=16)

    def swap_first():
        def widen(m, _):
            for k in range(4):
                b = m * 4 + k
                blk = held[pl.ds(pl.multiple_of(b * 64, 64), 64), :]
                wide[pl.ds(b * PITCH_WIDE, 64), :] = blk.astype(F32)
            return 0
        lax.fori_loop(0, 8, widen, 0, unroll=8)

        def gather(m, _):
            d = [wide[pl.ds(2 * m + k, 32, stride=PITCH_WIDE), :] for k in range(2)]
            mixed[pl.ds(pl.multiple_of(m * 32, 32), 32), :] = jnp.concatenate(d, 1).astype(BF)
            return 0
        lax.fori_loop(0, 32, gather, 0, unroll=32)

        def body(m, _):
            r = dot(mixed[pl.ds(pl.multiple_of(m * 256, 256), 256), :], lanes[...]).astype(BF)
            halves = [jnp.concatenate([r[k * 32:k * 32 + 32, h * 128:h * 128 + 128] for k in range(8)], 1)
                      for h in range(2)]
            t = dot(rows[...], jnp.concatenate(halves, 0)).astype(BF)
            for k in range(8):
                held[pl.ds(pl.multiple_of((m * 8 + k) * 64, 64), 64), :] = t[:, k * 128:k * 128 + 128]
            return 0
        lax.fori_loop(0, 4, body, 0, unroll=4)

    def turn(i, first):
        number = pick[i]
        order, place = number // 4, number % 4
        even = (order == 0) | (order == 3) | (order == 4)
        f0 = jnp.where(even, (place == 1) | (place == 2), (place == 0) | (place == 3)).astype(jnp.int32)
        f1 = place % 2
        f2 = place // 2
        for b in range(32):
            held[b * 64:b * 64 + 64, :] = v[i, :, b * 128:b * 128 + 128]
        pl.when((order == 1) | (order == 3) | (order == 5))(swap_ends)
        pl.when((order >= 1) & (order <= 4))(swap_first)
        pl.when((order == 1) | (order == 4))(swap_ends)
        j0 = table[pl.ds(pl.multiple_of(128 + f0 * 64, 64), 64), 384:448]
        jl = table[pl.ds(pl.multiple_of(place * 128, 128), 128), 256:384]

        def flip_ends(m, _):
            at = pl.ds(pl.multiple_of(m * 256, 256), 256)
            held[at, :] = dot(held[at, :], jl).astype(BF)
            return 0

        @pl.when(f1 + f2 > 0)
        def _():
            lax.fori_loop(0, 8, flip_ends, 0, unroll=8)

        def add(m, flipped):
            blocks = []
            for k in range(4):
                b = m * 4 + k
                src = b + f1 * (31 - 2 * b)
                blocks.append(held[pl.ds(pl.multiple_of(src * 64, 64), 64), :])
            if flipped:
                u = dot(j0, jnp.concatenate(blocks, 1))
                blocks = [u[:, k * 128:k * 128 + 128] for k in range(4)]
            for k in range(4):
                at = pl.ds(m * 4 + k, 64, stride=PITCH_TOTAL)
                u = blocks[k].astype(F32)
                total[at, :] = u if first else total[at, :] + u

        @pl.when(f0 > 0)
        def _():
            lax.fori_loop(0, 8, lambda m, c: (add(m, True), c)[1], 0, unroll=8)

        @pl.when(f0 == 0)
        def _():
            lax.fori_loop(0, 8, lambda m, c: (add(m, False), c)[1], 0, unroll=8)

    def one(i, _):
        c = classes[i]

        def count(j, n):
            return n + (classes[j] == c).astype(jnp.int32)

        @pl.when(lax.fori_loop(0, i, count, 0) == 0)
        def _():
            turn(i, True)

            def later(j, _):
                @pl.when(classes[j] == c)
                def _():
                    turn(j, False)
                return 0
            lax.fori_loop(i + 1, 6, later, 0)

            def shorten(k, _):
                for d in range(8):
                    at = pl.ds(pl.multiple_of(k * 256 + d * 32, 32), 32)
                    narrow[i, at, :] = total[pl.ds((k * 8 + d) * PITCH_TOTAL, 32), :].astype(BF)
                return 0
            lax.fori_loop(0, 8, shorten, 0, unroll=8)
            store(c, narrow.at[i]).start()
        return 0
    lax.fori_loop(0, 6, one, 0)

    for s in range(2):
        @pl.when(ref_pick[s] // per == me)
        def _():
            fetch(s).wait()
    for c in range(CLASSES):
        store(c, empty).wait()


def turn_call(ref_pick, pick, classes, refs, v):
    table = jnp.asarray(turn_tables(), dtype=BF)
    sm, vm, far = [pl.BlockSpec(memory_space=m) for m in (pltpu.SMEM, pltpu.VMEM, pl.ANY)]
    return pl.pallas_call(
        turn_kernel,
        out_shape=(
            jax.ShapeDtypeStruct((2, 8, 2048, 128), BF),
            jax.ShapeDtypeStruct((2,) + refs.shape[1:], BF),
            jax.ShapeDtypeStruct((8, 128), F32),
        ),
        in_specs=[sm] * 3 + [far] + [vm] * 2,
        out_specs=(far, vm, vm),
        scratch_shapes=[
            pltpu.VMEM((2048, 128), BF), pltpu.VMEM((2304, 128), F32), pltpu.VMEM((1024, 256), BF),
            pltpu.VMEM((2560, 128), F32), pltpu.VMEM((6, 2048, 128), BF), pltpu.VMEM((2048, 128), BF),
            pltpu.SemaphoreType.DMA((CLASSES,)), pltpu.SemaphoreType.DMA((2,)),
        ],
        compiler_params=pltpu.CompilerParams(vmem_limit_bytes=40 * 2**20),
    )(ref_pick, pick, classes, refs, v, table)


PARTS = (
    ((0, 1, 2), False, 0, 48), ((0, 1, 2), True, 48, 32),
    ((1, 2, 0), False, 80, 48), ((1, 2, 0), True, 128, 32),
    ((2, 0, 1), False, 160, 48), ((2, 0, 1), True, 208, 48),
)
MOVES = 10


class Place:
    def __init__(self):
        tomo, orient = lax.axis_index("tomo"), lax.axis_index("orient")
        self.core = orient % 2
        self.at = (orient // 4, (tomo // 4) * 2 + (orient // 2) % 2, tomo % 4)
        self.near = tuple(c + 1 - 2 * (c % 2) for c in self.at)
        self.far = tuple(3 - c for c in self.at)
        self.cross = tuple((c + 2) % 4 for c in self.at)

    def device(self, axis=None, to=None, core=None):
        z, y, x = [to if axis == k else c for k, c in enumerate(self.at)]
        core = self.core if core is None else core
        return ((y // 2) * 4 + x, z * 4 + (y % 2) * 2 + core)

    def other_core(self):
        return self.device(core=1 - self.core)

    def partners(self):
        return [self.other_core()] + [self.device(k, t[k]) for k in range(3) for t in (self.near, self.far)]

    def group(self, j):
        return (lax.axis_index("tomo"), j * 2 + self.core)

    def all_partners(self):
        j = self.at[0] * 2 + self.at[1] % 2
        around = [self.group((j + d) % 8) for d in range(1, 8)]
        return around + [self.other_core(), self.device(1, self.far[1]),
                         self.device(2, self.near[2]), self.device(2, self.far[2])]


def greet(place):
    barrier = pltpu.get_barrier_semaphore()
    for device in place.all_partners():
        pl.semaphore_signal(barrier, inc=1, device_id=device, device_id_type=MESH)
    pl.semaphore_wait(barrier, 11)


class ClassSums:
    def __init__(self, place, sums, mine, got, keep, send, first, second, total, send_sem, recv_sem, load_sem):
        self.p, self.sums, self.mine, self.got, self.keep, self.send = place, sums, mine, got, keep, send
        self.first, self.second, self.total = first, second, total
        self.send_sem, self.recv_sem = send_sem, recv_sem
        self.load = pltpu.make_async_copy(sums.at[place.core], mine, load_sem)
        self.sent = []
        self.coming = {}

    def move(self, part, k, src, dst, device):
        copy = pltpu.make_async_remote_copy(
            src_ref=src, dst_ref=dst, send_sem=self.send_sem.at[part * MOVES + k],
            recv_sem=self.recv_sem.at[part * MOVES + k], device_id=device, device_id_type=MESH)
        copy.start()
        self.sent.append(copy)
        self.coming[part, k] = copy

    def start(self):
        for i, (_, _, row, rows) in enumerate(PARTS):
            cells = pl.ds(row, rows)
            self.move(i, 0, self.sums.at[1 - self.p.core, :, cells, :], self.got.at[:, cells, :], self.p.other_core())
        self.load.start()

    def links(self, part, level):
        axis = PARTS[part][0][level]
        near, far = self.p.near[axis], self.p.far[axis]
        f, g = (far, near) if PARTS[part][1] else (near, far)
        return axis, self.p.at[axis], f, g, self.p.cross[axis]

    def prefix(self, part, level):
        base = 0
        for k in range(level):
            base = base + self.p.at[PARTS[part][0][k]] * 4 ** (2 - k)
        return base, 4 ** (2 - level)

    def halves(self, part, level, value):
        _, _, row, rows = PARTS[part]
        cells = pl.ds(row, rows)
        axis, c, f, g, h = self.links(part, level)
        base, size = self.prefix(part, level)
        for slot, d in ((1, h), (0, f)):
            def out(k, _, d=d):
                at = base + d * size + k
                self.send[at, cells, :] = value(d * size + k).astype(BF)
                return 0
            lax.fori_loop(0, size, out, 0, unroll=min(size, 4))
            self.move(part, 1 + 3 * level + slot, self.send.at[pl.ds(base + d * size, size), cells, :],
                      self.first[level].at[slot, :, cells, :], self.p.device(axis, f))
        for d in (g, c):
            def stay(k, _, d=d):
                self.keep[base + d * size + k, cells, :] = value(d * size + k)
                return 0
            lax.fori_loop(0, size, stay, 0, unroll=min(size, 4))

    def round(self, r):
        for part in range(len(PARTS)):
            self.step(r, part)

    def step(self, r, part):
        order, _, row, rows = PARTS[part]
        cells = pl.ds(row, rows)
        if r == 0:
            if part == 0:
                self.load.wait()
            self.coming[part, 0].wait_recv()

            def value(at):
                d = (at // 16, at // 4 % 4, at % 4)
                z, y, x = [d[order.index(k)] for k in range(3)]
                src = (z * 2 + y % 2) * 8 + (y // 2) * 4 + x
                return self.mine[src, cells, :].astype(F32) + self.got[src, cells, :].astype(F32)
            self.halves(part, 0, value)
            return
        level = (r - 1) // 2
        axis, c, f, g, h = self.links(part, level)
        base, size = self.prefix(part, level)
        if r % 2:
            self.coming[part, 2 + 3 * level].wait_recv()

            def body(k, _):
                at = base + g * size + k
                v = self.keep[at, cells, :] + self.first[level][1, k, cells, :].astype(F32)
                self.send[at, cells, :] = v.astype(BF)
                return 0
            lax.fori_loop(0, size, body, 0, unroll=min(size, 4))
            self.move(part, 3 + 3 * level, self.send.at[pl.ds(base + g * size, size), cells, :],
                      self.second[level].at[:, cells, :], self.p.device(axis, g))
            return
        self.coming[part, 1 + 3 * level].wait_recv()
        self.coming[part, 3 + 3 * level].wait_recv()

        def value(k):
            return (self.keep[base + c * size + k, cells, :] + self.first[level][0, k, cells, :].astype(F32)
                    + self.second[level][k, cells, :].astype(F32))
        if level < 2:
            self.halves(part, level + 1, value)
        else:
            self.total[cells, :] = value(0)

    def finish(self):
        for copy in self.sent:
            copy.wait_send()

    @staticmethod
    def scratch():
        vm = pltpu.VMEM
        return [
            vm((64, 256, 128), BF), vm((64, 256, 128), BF), vm((64, 256, 128), F32), vm((64, 256, 128), BF),
            vm((2, 16, 256, 128), BF), vm((2, 4, 256, 128), BF), vm((2, 1, 256, 128), BF),
            vm((16, 256, 128), BF), vm((4, 256, 128), BF), vm((1, 256, 128), BF),
            vm((256, 128), F32),
            pltpu.SemaphoreType.DMA((len(PARTS) * MOVES,)), pltpu.SemaphoreType.DMA((len(PARTS) * MOVES,)),
            pltpu.SemaphoreType.DMA(()),
        ]


class Counts:
    def __init__(self, place, own, held, got, send_sem, recv_sem):
        self.p, self.held, self.got, self.send_sem, self.recv_sem = place, held, got, send_sem, recv_sem
        held[0] = own[...]
        self.partners = place.partners()
        self.sent = []

    def go(self, k):
        copy = pltpu.make_async_remote_copy(
            src_ref=self.held.at[k], dst_ref=self.got.at[k], send_sem=self.send_sem.at[k],
            recv_sem=self.recv_sem.at[k], device_id=self.partners[k], device_id_type=MESH)
        copy.start()
        self.sent.append(copy)

    def start(self):
        self.go(0)

    def round(self, k):
        self.sent[k].wait_recv()
        self.held[k + 1] = self.held[k] + self.got[k]
        if k < 6:
            self.go(k + 1)

    def result(self):
        return self.held[7]

    def finish(self):
        for copy in self.sent:
            copy.wait_send()

    @staticmethod
    def scratch():
        return [pltpu.VMEM((8, 8, 128), F32), pltpu.VMEM((7, 8, 128), F32),
                pltpu.SemaphoreType.DMA((7,)), pltpu.SemaphoreType.DMA((7,))]


class References:
    ROUNDS = 4

    def __init__(self, place, own, full, half, acc, got, send_sem, recv_sem):
        self.p, self.own, self.full, self.half, self.acc, self.got = place, own, full, half, acc, got
        self.send_sem, self.recv_sem = send_sem, recv_sem
        self.sent, self.coming = [], {}
        self.j = place.at[0] * 2 + place.at[1] % 2
        self.lane = place.core * 2048

    def move(self, k, src, dst, device):
        copy = pltpu.make_async_remote_copy(
            src_ref=src, dst_ref=dst, send_sem=self.send_sem.at[k], recv_sem=self.recv_sem.at[k],
            device_id=device, device_id_type=MESH)
        copy.start()
        self.sent.append(copy)
        self.coming[k] = copy

    def lanes(self, at, size):
        return pl.ds(pl.multiple_of(at, 256), size)

    def share(self, k, j, device):
        cells = self.full.at[:, :, self.lanes(self.lane + j * 256, 256)]
        self.move(k, cells, cells, device)

    def start(self):
        for s in range(2):
            other = self.lanes((1 - self.p.core) * 2048, 2048)
            self.move(s, self.own.at[s, :, other], self.half.at[s], self.p.other_core())

    def round(self, r):
        if r == 0:
            for s in range(2):
                self.coming[s].wait_recv()
            for k in range(8):
                mine = self.own[:, :, self.lanes(self.lane + k * 256, 256)]
                self.acc[k] = mine + self.half[:, :, k * 256:k * 256 + 256]
            for d in (1, 7, 2, 6, 3, 5, 4):
                to = (self.j + d) % 8
                self.move(1 + d, self.acc.at[to], self.got.at[d - 1], self.p.group(to))
        elif r == 1:
            total = self.acc[self.j]
            for d in (1, 7, 2, 6, 3, 5, 4):
                self.coming[1 + d].wait_recv()
                total = total + self.got[d - 1]
            self.full[:, :, self.lanes(self.lane + self.j * 256, 256)] = total
            for d in (1, 7, 2, 6, 3, 5, 4):
                self.share(8 + d, self.j, self.p.group((self.j + d) % 8))
            self.share(16, self.j, self.p.other_core())
        elif r == 2:
            for d in (1, 7, 2, 6, 3, 5, 4):
                self.coming[8 + d].wait_recv()
                self.share(16 + d, (self.j - d + 8) % 8, self.p.other_core())
        else:
            for d in range(8):
                self.coming[16 + d].wait_recv()

    def finish(self):
        for copy in self.sent:
            copy.wait_send()

    @staticmethod
    def scratch():
        vm = pltpu.VMEM
        return [
            vm((2, 64, 4096), BF), vm((2, 64, 2048), BF), vm((8, 2, 64, 256), BF), vm((7, 2, 64, 256), BF),
            pltpu.SemaphoreType.DMA((24,)), pltpu.SemaphoreType.DMA((24,)),
        ]


def average(total, counts, orient, out):
    lane = lax.broadcasted_iota(jnp.int32, (8, 128), 1)
    row = lax.broadcasted_iota(jnp.int32, (8, 128), 0)
    count = jnp.sum(jnp.where((lane == orient) & (row == 0), counts, 0.0), keepdims=True)
    for b in range(32):
        out[0, :, b * 128:b * 128 + 128] = total[pl.ds(b, 8, stride=32), :] / count


class Scores:
    def __init__(self, v, wedge, full, table, out, scratch):
        self.v, self.wedge, self.full, self.out = v, wedge, full, out
        self.txf, self.tzf, self.tyf, self.tyi, self.tzi, self.txi, self.fr, self.fl = table_views(table)
        self.left, self.plane, self.spec, self.rspec, self.weight, self.edge, self.filt, self.extra = scratch
        self.low = lax.broadcasted_iota(jnp.int32, (64, 128), 1) < 64
        self.row = lax.broadcasted_iota(jnp.int32, (8, 128), 0)
        self.lane = lax.broadcasted_iota(jnp.int32, (8, 128), 1)
        self.result = jnp.zeros((8, 128), F32)
        self.twin, self.own = {}, {}

    def halves(self, t, op, fill):
        return [op(jnp.where(self.low[:8] == (k == 0), t, fill), keepdims=True) for k in range(2)]

    def forward(self, first, second, kind, out):
        def x():
            forward_x(first, 0, self.txf[kind][...], self.left)
            forward_x(second, 1, self.txf[kind][...], self.left)
        return [
            (0.6, x),
            (0.9, lambda: forward_z(self.tzf[kind][...], self.left, self.plane)),
            (0.6, lambda: forward_y(self.tyf[kind][...], self.plane, out)),
        ]

    def mirror(self, spec):
        return mirror(spec[0:128, :], self.fr[...], self.fl[...])

    def wedge_work(self):
        return self.forward(self.wedge, self.wedge, 1, self.rspec) + [
            (0.2, lambda: wedge_setup(self.rspec, self.fr[...], self.fl[...], self.weight, self.edge))]

    def pair_work(self, pair):
        spec = self.spec.at[pair]

        def after():
            self.twin[pair] = self.mirror(spec)
            self.own[pair] = self.halves(power(spec, self.twin[pair], self.weight, self.edge), jnp.sum, 0.0)
        return self.forward(self.v.at[2 * pair], self.v.at[2 * pair + 1], 0, spec) + [(0.3, after)]

    def reference_work(self):
        def after():
            t = self.mirror(self.rspec)
            self.norm = self.halves(power(self.rspec, t, self.weight, self.edge), jnp.sum, 0.0)
            reference_setup(self.rspec, t, self.weight, self.edge, self.low, self.filt, self.extra)
        return self.forward(self.full.at[0], self.full.at[1], 0, self.rspec) + [(0.7, after)]

    def score_work(self, pair, s):
        def last():
            top = self.halves(correlate_x(self.txi[...], self.plane), jnp.max, -jnp.inf)
            for k in range(2):
                score = top[k] / jnp.sqrt(self.own[pair][k] * self.norm[s] / float(N ** 3) + 1e-6)
                self.result = jnp.where((self.row == s) & (self.lane == 2 * pair + k), score, self.result)
        return [
            (1.0, lambda: correlate_y(self.spec.at[pair], self.twin[pair], self.filt.at[s], self.extra[s],
                                      self.tyi[...], self.left)),
            (0.6, lambda: correlate_z(self.tzi[...], self.left, self.plane)),
            (0.8, last),
        ]

    def finish(self):
        self.out[...] = self.result[:self.out.shape[0], :self.out.shape[1]]

    @staticmethod
    def scratch():
        vm = pltpu.VMEM
        return [
            vm((2048, 512), BF), vm((4608, 128), F32), vm((3, 4096, 128), BF), vm((4096, 128), BF),
            vm((2048, 128), F32), vm((128, 128), F32), vm((2, 4096, 128), F32), vm((2, 128, 128), F32),
        ]


def interleave(work, events):
    events = sorted(events, key=lambda e: e[0])
    clock = 0.0
    for length, piece in work:
        while events and events[0][0] <= clock:
            events.pop(0)[1]()
        piece()
        clock += length
    for _, action in events:
        action()


REF_TIMES = (2.0, 6.0, 9.0, 9.2)
CLASS_TIMES = ((3.0, 0.9), (9.05, 0.02), (14.0, 0.5), (17.0, 0.4), (20, 0.3), (23, 0.3), (26, 0.2))


def fused_kernel(own_refs, sums, counts, v, wedges, table, scores_out, out, *scratch):
    place = Place()
    ends = np.cumsum([0] + [len(c.scratch()) for c in (ClassSums, Counts, References, Scores)])
    s, tally_s, refs_s, score_s = [scratch[i:j] for i, j in zip(ends, ends[1:])]
    classes = ClassSums(place, sums, s[0], s[1], s[2], s[3], s[4:7], s[7:10], s[10], s[11], s[12], s[13])
    tally = Counts(place, counts, *tally_s)
    refs = References(place, own_refs, *refs_s)
    orient = lax.axis_index("orient")
    scores = Scores(v, wedges.at[orient * wedges.shape[0] // lax.axis_size("orient")], refs.full, table, scores_out, score_s)
    greet(place)
    refs.start()
    tally.start()
    classes.start()
    events = [(t, functools.partial(refs.round, r)) for r, t in enumerate(REF_TIMES)]
    for r, (t, gap) in enumerate(CLASS_TIMES):
        events += [(t + gap * part, functools.partial(classes.step, r, part)) for part in range(len(PARTS))]
        events.append((t + gap * len(PARTS), functools.partial(tally.round, r)))
    work = scores.wedge_work()
    for pair in range(3):
        work += scores.pair_work(pair)
    work += scores.reference_work()
    for pair in range(3):
        for step in range(STEPS):
            work += scores.score_work(pair, step)
    interleave(work, events)
    scores.finish()
    average(classes.total, tally.result(), orient, out)
    for part in (refs, tally, classes):
        part.finish()


def fused_call(own_refs, sums, counts, v, wedges):
    table = jnp.asarray(score_tables(), dtype=BF)
    vm = pl.BlockSpec(memory_space=pltpu.VMEM)
    return pl.pallas_call(
        fused_kernel,
        out_shape=(jax.ShapeDtypeStruct((STEPS, v.shape[0]), F32), jax.ShapeDtypeStruct((1, 8, 4096), F32)),
        in_specs=[vm, pl.BlockSpec(memory_space=pl.ANY)] + [vm] * 4,
        out_specs=(vm, vm),
        scratch_shapes=sum([c.scratch() for c in (ClassSums, Counts, References, Scores)], []),
        compiler_params=pltpu.CompilerParams(
            collective_id=0, has_side_effects=True, vmem_limit_bytes=60 * 2**20),
    )(own_refs, sums.reshape(2, 64, 256, 128), counts, v, wedges, table)


def local(subtomograms, rotated_refs, wedges, ref_pick, best_pick, class_of):
    sums, own_refs, counts = turn_call(ref_pick, best_pick, class_of[:, 0], rotated_refs, subtomograms)
    return fused_call(own_refs, sums, counts, subtomograms, wedges)


def solution(mesh):
    placed = (
        P(("tomo", "orient"), None, None),
        P("orient", None, None),
        P("tomo", None, None),
        P(),
        P(("tomo", "orient")),
        P(("tomo", "orient"), None),
    )
    return jax.shard_map(
        local,
        mesh=mesh,
        in_specs=placed,
        out_specs=(P(None, ("tomo", "orient")), P("orient", "tomo", None)),
        check_vma=False,
    )
```

```python
import functools

import jax
import jax.numpy as jnp
import numpy as np
from jax import lax
from jax.experimental import pallas as pl
from jax.experimental.pallas import tpu as pltpu
from jax.sharding import PartitionSpec as P

STEPS = 2
CLASSES = 16
N = 64
BF = jnp.bfloat16
F32 = jnp.float32
MESH = pl.DeviceIdType.MESH
PITCH_FWD = 36
PITCH_INV = 68
PITCH_WIDE = 68
PITCH_TOTAL = 36


def score_tables():
    i = np.arange(N)
    ang = (i[:, None] * i[None, :] % N) * (2.0 * np.pi / N)
    c, s = np.cos(ang), np.sin(ang)
    c[np.abs(c) < 1e-9] = 0.0
    s[np.abs(s) < 1e-9] = 0.0
    h = N // 2
    eye, rev = np.eye(N), np.eye(N)[(-i) % N]

    def pairs(m00, m01, m10, m11):
        return np.array([[m00, m01], [m10, m11]])

    def lanes_forward(b):
        t = np.einsum("abzk,qr,hg->qahzbgrk", b, np.eye(2), np.eye(2))
        return t.reshape(512, 512)

    def rows_forward(b):
        t = np.transpose(b, (1, 3, 0, 2)).reshape(2, N, 2, h, 2)
        return np.transpose(t, (0, 1, 2, 4, 3)).reshape(128, 128)

    fwd = pairs(c, -s, s, c)
    wdg = pairs(eye, 0 * eye, 0 * eye, rev)
    inv = pairs(c, s, -s, c)
    x_fwd = np.concatenate([c[:h], -s[:h]], 0)
    x_fwd[h] = c[h]
    x_wdg = np.concatenate([eye[:h], rev[:h]], 0)
    x_wdg[h] = eye[h]
    y_inv = np.transpose(inv, (1, 3, 0, 2)).reshape(128, 128)
    z_inv = np.einsum("abzk,qr->aqzbrk", inv, np.eye(2)).reshape(256, 256)
    x_inv = x_fwd.T
    flip_rows = np.kron(np.diag([1.0, -1.0]), rev)
    flip_lanes = np.kron(np.eye(2), rev)
    table = np.zeros((1408, 512))
    for k, t in enumerate((fwd, wdg)):
        table[512 * k:512 * k + 512] = lanes_forward(t)
        table[1024 + 128 * k:1152 + 128 * k, 256:384] = rows_forward(t)
    table[1024:1280, :256] = z_inv
    table[1024:1152, 384:] = y_inv
    table[1152:1280, 384:] = flip_rows
    table[1280:, :128] = flip_lanes
    table[1280:1344, 128:192] = x_fwd
    table[1344:, 128:192] = x_wdg
    table[1280:1344, 256:320] = x_inv
    return table


def table_views(table):
    return (
        [table.at[1280:1344, 128:192], table.at[1344:1408, 128:192]],
        [table.at[0:512, :], table.at[512:1024, :]],
        [table.at[1024:1152, 256:384], table.at[1152:1280, 256:384]],
        table.at[1024:1152, 384:512], table.at[1024:1280, 0:256], table.at[1280:1344, 256:320],
        table.at[1152:1280, 384:512], table.at[1280:1408, 0:128],
    )


def dot(a, b):
    return jnp.dot(a, b, preferred_element_type=F32)


def forward_x(vol, q, tx, left):
    def x_pass(c, _):
        at = pl.multiple_of(c * 512, 512)
        r = dot(tx, vol[:, pl.ds(at, 512)]).astype(BF)
        for k in range(4):
            rows = pl.ds(pl.multiple_of((c * 4 + k) * 32, 32), 32)
            left[rows, q * 256:q * 256 + 128] = r[:32, k * 128:k * 128 + 128]
            left[rows, q * 256 + 128:q * 256 + 256] = r[32:, k * 128:k * 128 + 128]
        return 0
    lax.fori_loop(0, 8, x_pass, 0, unroll=8)


def forward_z(tz, left, plane):
    def z_pass(m, _):
        at = pl.multiple_of(m * 128, 128)
        r = dot(left[pl.ds(at, 128), :], tz)
        for col in range(4):
            for k in range(4):
                row = (col * 32 + m * 4 + k) * PITCH_FWD
                plane[pl.ds(row, 32), :] = r[k * 32:k * 32 + 32, col * 128:col * 128 + 128]
        return 0
    lax.fori_loop(0, 8, z_pass, 0, unroll=8)


def forward_y(ty, plane, out):
    def y_pass(m, _):
        d = jnp.concatenate(
            [plane[pl.ds(2 * m + k, 128, stride=PITCH_FWD), :] for k in range(2)], 1).astype(BF)
        r = dot(ty, d).astype(BF)
        for k in range(2):
            out[pl.ds(pl.multiple_of((2 * m + k) * 128, 128), 128), :] = r[:, k * 128:k * 128 + 128]
        return 0
    lax.fori_loop(0, 16, y_pass, 0, unroll=16)


def mirror(g, flip_rows, flip_lanes):
    return dot(dot(flip_rows, g).astype(BF), flip_lanes)


def split(g, t):
    gr, gi, tr, ti = g[:64], g[64:], t[:64], t[64:]
    return (0.5 * (gr + tr), 0.5 * (gi + ti)), (0.5 * (gi - ti), -0.5 * (gr - tr))


def fold(v):
    return functools.reduce(jnp.add, [v[8 * k:8 * k + 8] for k in range(v.shape[0] // 8)])


def power(spec, twin, weight, edge):
    a, b = split(spec[0:128, :].astype(F32), twin)
    total = fold(edge[0:64, :] * (a[0] ** 2 + a[1] ** 2) + edge[64:128, :] * (b[0] ** 2 + b[1] ** 2))

    def body(kx, total):
        v = spec[pl.ds(pl.multiple_of(kx * 128, 128), 128), :].astype(F32)
        w = weight[pl.ds(pl.multiple_of(kx * 64, 64), 64), :]
        return total + fold(w * (v[:64] ** 2 + v[64:] ** 2))
    return lax.fori_loop(1, 32, body, total, unroll=31)


def wedge_setup(spec, flip_rows, flip_lanes, weight, edge):
    g = spec[0:128, :]
    t = mirror(g, jnp.abs(flip_rows), flip_lanes)
    edge[...] = 0.5 * (g.astype(F32) + t)

    def body(kx, _):
        v = spec[pl.ds(pl.multiple_of(kx * 128, 128), 128), :].astype(F32)
        weight[pl.ds(pl.multiple_of(kx * 64, 64), 64), :] = v[:64] + v[64:]
        return 0
    lax.fori_loop(1, 32, body, 0)


def spread_half(v, s, low):
    r = pltpu.roll(v, 64, 1)
    return jnp.where(low, v, r) if s == 0 else jnp.where(low, r, v)


def reference_setup(spec, twin, weight, edge, low, filt, extra):
    a, b = split(spec[0:128, :].astype(F32), twin)
    w0, w32 = edge[0:64, :], edge[64:128, :]
    for s in range(2):
        p = [spread_half(v, s, low) for v in (w0 * a[0], -w0 * a[1])]
        q = [spread_half(v, s, low) for v in (w32 * b[0], -w32 * b[1])]
        for k in range(2):
            filt[s, 64 * k:64 * k + 64, :] = 0.5 * (p[k] + q[k])
            extra[s, 64 * k:64 * k + 64, :] = 0.5 * (p[k] - q[k])

    def body(kx, _):
        v = spec[pl.ds(pl.multiple_of(kx * 128, 128), 128), :].astype(F32)
        w = weight[pl.ds(pl.multiple_of(kx * 64, 64), 64), :]
        re, im = w * v[:64], -w * v[64:]
        for s in range(2):
            filt[s, pl.ds(pl.multiple_of(kx * 128, 128), 64), :] = spread_half(re, s, low)
            filt[s, pl.ds(pl.multiple_of(kx * 128 + 64, 64), 64), :] = spread_half(im, s, low)
        return 0
    lax.fori_loop(1, 32, body, 0)


def correlate_y(spec, twin, filt, extra, ty, left):
    def times(v, w):
        return (v[:64] * w[:64] - v[64:] * w[64:], v[:64] * w[64:] + v[64:] * w[:64])

    def cross(kx):
        at = pl.multiple_of(kx * 128, 128)
        return times(spec[pl.ds(at, 128), :].astype(F32), filt[pl.ds(at, 128), :])

    def finish(m, parts):
        d = jnp.concatenate([jnp.concatenate(p, 0).astype(BF) for p in parts], 1)
        r = dot(ty, d).astype(BF)
        for k in range(2):
            rows = pl.ds(pl.multiple_of((2 * m + k) * 64, 64), 64)
            left[rows, 0:128] = r[:64, k * 128:k * 128 + 128]
            left[rows, 128:256] = r[64:, k * 128:k * 128 + 128]

    c0, e0 = cross(0), times(twin, extra)
    finish(0, [(c0[0] + e0[0], c0[1] + e0[1]), cross(1)])

    def y_pass(m, _):
        finish(m, [cross(2 * m), cross(2 * m + 1)])
        return 0
    lax.fori_loop(1, 16, y_pass, 0, unroll=15)


def correlate_z(tz, left, plane):
    def z_pass(m, _):
        at = pl.multiple_of(m * 256, 256)
        r = dot(left[pl.ds(at, 256), 0:256], tz)
        for p in range(2):
            for k in range(4):
                row = (p * 32 + m * 4 + k) * PITCH_INV
                plane[pl.ds(row, 64), :] = r[k * 64:k * 64 + 64, p * 128:p * 128 + 128]
        return 0
    lax.fori_loop(0, 8, z_pass, 0, unroll=8)


def correlate_x(tx, plane):
    def x_pass(m, top):
        d = jnp.concatenate(
            [plane[pl.ds(2 * m + k, 64, stride=PITCH_INV), :] for k in range(2)], 1).astype(BF)
        r = dot(tx, d)
        return jnp.maximum(top, jnp.maximum(r[:, :128], r[:, 128:]))
    top = lax.fori_loop(0, 32, x_pass, jnp.full((64, 128), -jnp.inf, F32), unroll=16)
    return functools.reduce(jnp.maximum, [top[8 * k:8 * k + 8] for k in range(8)])


def turn_tables():
    eye, rev = np.eye(N), np.eye(N)[::-1]
    two, swap = np.eye(2), np.eye(2)[::-1]
    pair = np.concatenate([eye, eye], 1)
    lanes = np.einsum("ac,hg,zw->ahzgcw", two, two, eye).reshape(256, 256)
    rows = np.transpose(eye.reshape(N, 32, 2), (0, 2, 1)).reshape(N, N)
    flip_rows = np.stack([eye, rev])
    flip_lanes = np.stack([np.kron(a, b) for b in (eye, rev) for a in (two, swap)])
    table = np.zeros((512, 512))
    table[:256, :256] = lanes
    table[:, 256:384] = flip_lanes.reshape(512, 128)
    table[:64, 384:] = pair
    table[64:128, 384:448] = rows
    table[128:256, 384:448] = flip_rows.reshape(128, 64)
    return table


def turn_kernel(ref_pick, pick, classes, refs, v, table,
                out, own_refs, counts, held, wide, mixed, total, narrow, empty, out_sem, ref_sem):
    pair, lanes, rows = table.at[0:64, 384:512], table.at[0:256, 0:256], table.at[64:128, 384:448]
    low = lax.broadcasted_iota(jnp.int32, (64, 128), 1) < 64
    me, per = lax.axis_index("orient"), refs.shape[0]

    def fetch(s):
        return pltpu.make_async_copy(refs.at[ref_pick[s] % per], own_refs.at[s], ref_sem.at[s])

    for s in range(2):
        @pl.when(ref_pick[s] // per == me)
        def _():
            fetch(s).start()

        @pl.when(ref_pick[s] // per != me)
        def _():
            own_refs[s] = jnp.zeros(own_refs.shape[1:], BF)

    def store(c, src):
        return pltpu.make_async_copy(src, out.at[c % 2, c // 2], out_sem.at[c])

    empty[...] = jnp.zeros(empty.shape, BF)
    lane = lax.broadcasted_iota(jnp.int32, (8, 128), 1)
    tally = jnp.zeros((8, 128), F32)
    for i in range(6):
        tally = tally + (lane == classes[i]).astype(F32)
    counts[...] = tally
    for c in range(CLASSES):
        hit = classes[0] == c
        for i in range(1, 6):
            hit = hit | (classes[i] == c)

        @pl.when(jnp.logical_not(hit))
        def _():
            store(c, empty).start()

    def swap_ends():
        def body(m, _):
            blocks = []
            for k in range(2):
                blk = held[pl.ds(pl.multiple_of((2 * m + k) * 64, 64), 64), :].astype(F32)
                blocks += [jnp.where(low, blk, 0.0), jnp.where(low, 0.0, blk)]
            w = jnp.concatenate(blocks, 0).astype(BF)
            r = lax.dot_general(pair[...], w, (((1,), (1,)), ((), ())), preferred_element_type=F32).astype(BF)
            for k in range(2):
                held[pl.ds(pl.multiple_of((2 * m + k) * 64, 64), 64), :] = r[:, k * 128:k * 128 + 128]
            return 0
        lax.fori_loop(0, 16, body, 0, unroll=16)

    def swap_first():
        def widen(m, _):
            for k in range(4):
                b = m * 4 + k
                blk = held[pl.ds(pl.multiple_of(b * 64, 64), 64), :]
                wide[pl.ds(b * PITCH_WIDE, 64), :] = blk.astype(F32)
            return 0
        lax.fori_loop(0, 8, widen, 0, unroll=8)

        def gather(m, _):
            d = [wide[pl.ds(2 * m + k, 32, stride=PITCH_WIDE), :] for k in range(2)]
            mixed[pl.ds(pl.multiple_of(m * 32, 32), 32), :] = jnp.concatenate(d, 1).astype(BF)
            return 0
        lax.fori_loop(0, 32, gather, 0, unroll=32)

        def body(m, _):
            r = dot(mixed[pl.ds(pl.multiple_of(m * 256, 256), 256), :], lanes[...]).astype(BF)
            halves = [jnp.concatenate([r[k * 32:k * 32 + 32, h * 128:h * 128 + 128] for k in range(8)], 1)
                      for h in range(2)]
            t = dot(rows[...], jnp.concatenate(halves, 0)).astype(BF)
            for k in range(8):
                held[pl.ds(pl.multiple_of((m * 8 + k) * 64, 64), 64), :] = t[:, k * 128:k * 128 + 128]
            return 0
        lax.fori_loop(0, 4, body, 0, unroll=4)

    def turn(i, first):
        number = pick[i]
        order, place = number // 4, number % 4
        even = (order == 0) | (order == 3) | (order == 4)
        f0 = jnp.where(even, (place == 1) | (place == 2), (place == 0) | (place == 3)).astype(jnp.int32)
        f1 = place % 2
        f2 = place // 2
        for b in range(32):
            held[b * 64:b * 64 + 64, :] = v[i, :, b * 128:b * 128 + 128]
        pl.when((order == 1) | (order == 3) | (order == 5))(swap_ends)
        pl.when((order >= 1) & (order <= 4))(swap_first)
        pl.when((order == 1) | (order == 4))(swap_ends)
        j0 = table[pl.ds(pl.multiple_of(128 + f0 * 64, 64), 64), 384:448]
        jl = table[pl.ds(pl.multiple_of(place * 128, 128), 128), 256:384]

        def flip_ends(m, _):
            at = pl.ds(pl.multiple_of(m * 256, 256), 256)
            held[at, :] = dot(held[at, :], jl).astype(BF)
            return 0

        @pl.when(f1 + f2 > 0)
        def _():
            lax.fori_loop(0, 8, flip_ends, 0, unroll=8)

        def add(m, flipped):
            blocks = []
            for k in range(4):
                b = m * 4 + k
                src = b + f1 * (31 - 2 * b)
                blocks.append(held[pl.ds(pl.multiple_of(src * 64, 64), 64), :])
            if flipped:
                u = dot(j0, jnp.concatenate(blocks, 1))
                blocks = [u[:, k * 128:k * 128 + 128] for k in range(4)]
            for k in range(4):
                at = pl.ds(m * 4 + k, 64, stride=PITCH_TOTAL)
                u = blocks[k].astype(F32)
                total[at, :] = u if first else total[at, :] + u

        @pl.when(f0 > 0)
        def _():
            lax.fori_loop(0, 8, lambda m, c: (add(m, True), c)[1], 0, unroll=8)

        @pl.when(f0 == 0)
        def _():
            lax.fori_loop(0, 8, lambda m, c: (add(m, False), c)[1], 0, unroll=8)

    def one(i, _):
        c = classes[i]

        def count(j, n):
            return n + (classes[j] == c).astype(jnp.int32)

        @pl.when(lax.fori_loop(0, i, count, 0) == 0)
        def _():
            turn(i, True)

            def later(j, _):
                @pl.when(classes[j] == c)
                def _():
                    turn(j, False)
                return 0
            lax.fori_loop(i + 1, 6, later, 0)

            def shorten(k, _):
                for d in range(8):
                    at = pl.ds(pl.multiple_of(k * 256 + d * 32, 32), 32)
                    narrow[i, at, :] = total[pl.ds((k * 8 + d) * PITCH_TOTAL, 32), :].astype(BF)
                return 0
            lax.fori_loop(0, 8, shorten, 0, unroll=8)
            store(c, narrow.at[i]).start()
        return 0
    lax.fori_loop(0, 6, one, 0)

    for s in range(2):
        @pl.when(ref_pick[s] // per == me)
        def _():
            fetch(s).wait()
    for c in range(CLASSES):
        store(c, empty).wait()


def turn_call(ref_pick, pick, classes, refs, v):
    table = jnp.asarray(turn_tables(), dtype=BF)
    sm, vm, far = [pl.BlockSpec(memory_space=m) for m in (pltpu.SMEM, pltpu.VMEM, pl.ANY)]
    return pl.pallas_call(
        turn_kernel,
        out_shape=(
            jax.ShapeDtypeStruct((2, 8, 2048, 128), BF),
            jax.ShapeDtypeStruct((2,) + refs.shape[1:], BF),
            jax.ShapeDtypeStruct((8, 128), F32),
        ),
        in_specs=[sm] * 3 + [far] + [vm] * 2,
        out_specs=(far, vm, vm),
        scratch_shapes=[
            pltpu.VMEM((2048, 128), BF), pltpu.VMEM((2304, 128), F32), pltpu.VMEM((1024, 256), BF),
            pltpu.VMEM((2560, 128), F32), pltpu.VMEM((6, 2048, 128), BF), pltpu.VMEM((2048, 128), BF),
            pltpu.SemaphoreType.DMA((CLASSES,)), pltpu.SemaphoreType.DMA((2,)),
        ],
        compiler_params=pltpu.CompilerParams(vmem_limit_bytes=60 * 2**20),
    )(ref_pick, pick, classes, refs, v, table)


PARTS = (
    ((0, 1, 2), False, 0, 48), ((0, 1, 2), True, 48, 32),
    ((1, 2, 0), False, 80, 48), ((1, 2, 0), True, 128, 32),
    ((2, 0, 1), False, 160, 48), ((2, 0, 1), True, 208, 48),
)
MOVES = 10


class Place:
    def __init__(self):
        tomo, orient = lax.axis_index("tomo"), lax.axis_index("orient")
        self.core = orient % 2
        self.at = (orient // 4, (tomo // 4) * 2 + (orient // 2) % 2, tomo % 4)
        self.near = tuple(c + 1 - 2 * (c % 2) for c in self.at)
        self.far = tuple(3 - c for c in self.at)
        self.cross = tuple((c + 2) % 4 for c in self.at)

    def device(self, axis=None, to=None, core=None):
        z, y, x = [to if axis == k else c for k, c in enumerate(self.at)]
        core = self.core if core is None else core
        return ((y // 2) * 4 + x, z * 4 + (y % 2) * 2 + core)

    def other_core(self):
        return self.device(core=1 - self.core)

    def partners(self):
        return [self.other_core()] + [self.device(k, t[k]) for k in range(3) for t in (self.near, self.far)]

    def group(self, j):
        return (lax.axis_index("tomo"), j * 2 + self.core)

    def all_partners(self):
        j = self.at[0] * 2 + self.at[1] % 2
        around = [self.group((j + d) % 8) for d in range(1, 8)]
        return around + [self.other_core(), self.device(1, self.far[1]),
                         self.device(2, self.near[2]), self.device(2, self.far[2])]


def greet(place):
    barrier = pltpu.get_barrier_semaphore()
    for device in place.all_partners():
        pl.semaphore_signal(barrier, inc=1, device_id=device, device_id_type=MESH)
    pl.semaphore_wait(barrier, 11)


class ClassSums:
    def __init__(self, place, sums, mine, got, keep, send, first, second, total, send_sem, recv_sem, load_sem):
        self.p, self.sums, self.mine, self.got, self.keep, self.send = place, sums, mine, got, keep, send
        self.first, self.second, self.total = first, second, total
        self.send_sem, self.recv_sem = send_sem, recv_sem
        self.load = pltpu.make_async_copy(sums.at[place.core], mine, load_sem)
        self.sent = []
        self.coming = {}

    def move(self, part, k, src, dst, device):
        copy = pltpu.make_async_remote_copy(
            src_ref=src, dst_ref=dst, send_sem=self.send_sem.at[part * MOVES + k],
            recv_sem=self.recv_sem.at[part * MOVES + k], device_id=device, device_id_type=MESH)
        copy.start()
        self.sent.append(copy)
        self.coming[part, k] = copy

    def start(self):
        for i, (_, _, row, rows) in enumerate(PARTS):
            cells = pl.ds(row, rows)
            self.move(i, 0, self.sums.at[1 - self.p.core, :, cells, :], self.got.at[:, cells, :], self.p.other_core())
        self.load.start()

    def links(self, part, level):
        axis = PARTS[part][0][level]
        near, far = self.p.near[axis], self.p.far[axis]
        f, g = (far, near) if PARTS[part][1] else (near, far)
        return axis, self.p.at[axis], f, g, self.p.cross[axis]

    def prefix(self, part, level):
        base = 0
        for k in range(level):
            base = base + self.p.at[PARTS[part][0][k]] * 4 ** (2 - k)
        return base, 4 ** (2 - level)

    def halves(self, part, level, value):
        _, _, row, rows = PARTS[part]
        cells = pl.ds(row, rows)
        axis, c, f, g, h = self.links(part, level)
        base, size = self.prefix(part, level)
        for slot, d in ((1, h), (0, f)):
            def out(k, _, d=d):
                at = base + d * size + k
                self.send[at, cells, :] = value(d * size + k).astype(BF)
                return 0
            lax.fori_loop(0, size, out, 0, unroll=min(size, 4))
            self.move(part, 1 + 3 * level + slot, self.send.at[pl.ds(base + d * size, size), cells, :],
                      self.first[level].at[slot, :, cells, :], self.p.device(axis, f))
        for d in (g, c):
            def stay(k, _, d=d):
                self.keep[base + d * size + k, cells, :] = value(d * size + k)
                return 0
            lax.fori_loop(0, size, stay, 0, unroll=min(size, 4))

    def round(self, r):
        for part in range(len(PARTS)):
            self.step(r, part)

    def step(self, r, part):
        order, _, row, rows = PARTS[part]
        cells = pl.ds(row, rows)
        if r == 0:
            if part == 0:
                self.load.wait()
            self.coming[part, 0].wait_recv()

            def value(at):
                d = (at // 16, at // 4 % 4, at % 4)
                z, y, x = [d[order.index(k)] for k in range(3)]
                src = (z * 2 + y % 2) * 8 + (y // 2) * 4 + x
                return self.mine[src, cells, :].astype(F32) + self.got[src, cells, :].astype(F32)
            self.halves(part, 0, value)
            return
        level = (r - 1) // 2
        axis, c, f, g, h = self.links(part, level)
        base, size = self.prefix(part, level)
        if r % 2:
            self.coming[part, 2 + 3 * level].wait_recv()

            def body(k, _):
                at = base + g * size + k
                v = self.keep[at, cells, :] + self.first[level][1, k, cells, :].astype(F32)
                self.send[at, cells, :] = v.astype(BF)
                return 0
            lax.fori_loop(0, size, body, 0, unroll=min(size, 4))
            self.move(part, 3 + 3 * level, self.send.at[pl.ds(base + g * size, size), cells, :],
                      self.second[level].at[:, cells, :], self.p.device(axis, g))
            return
        self.coming[part, 1 + 3 * level].wait_recv()
        self.coming[part, 3 + 3 * level].wait_recv()

        def value(k):
            return (self.keep[base + c * size + k, cells, :] + self.first[level][0, k, cells, :].astype(F32)
                    + self.second[level][k, cells, :].astype(F32))
        if level < 2:
            self.halves(part, level + 1, value)
        else:
            self.total[cells, :] = value(0)

    def finish(self):
        for copy in self.sent:
            copy.wait_send()

    @staticmethod
    def scratch():
        vm = pltpu.VMEM
        return [
            vm((64, 256, 128), BF), vm((64, 256, 128), BF), vm((64, 256, 128), F32), vm((64, 256, 128), BF),
            vm((2, 16, 256, 128), BF), vm((2, 4, 256, 128), BF), vm((2, 1, 256, 128), BF),
            vm((16, 256, 128), BF), vm((4, 256, 128), BF), vm((1, 256, 128), BF),
            vm((256, 128), F32),
            pltpu.SemaphoreType.DMA((len(PARTS) * MOVES,)), pltpu.SemaphoreType.DMA((len(PARTS) * MOVES,)),
            pltpu.SemaphoreType.DMA(()),
        ]


class Counts:
    def __init__(self, place, own, held, got, send_sem, recv_sem):
        self.p, self.held, self.got, self.send_sem, self.recv_sem = place, held, got, send_sem, recv_sem
        held[0] = own[...]
        self.partners = place.partners()
        self.sent = []

    def go(self, k):
        copy = pltpu.make_async_remote_copy(
            src_ref=self.held.at[k], dst_ref=self.got.at[k], send_sem=self.send_sem.at[k],
            recv_sem=self.recv_sem.at[k], device_id=self.partners[k], device_id_type=MESH)
        copy.start()
        self.sent.append(copy)

    def start(self):
        self.go(0)

    def round(self, k):
        self.sent[k].wait_recv()
        self.held[k + 1] = self.held[k] + self.got[k]
        if k < 6:
            self.go(k + 1)

    def result(self):
        return self.held[7]

    def finish(self):
        for copy in self.sent:
            copy.wait_send()

    @staticmethod
    def scratch():
        return [pltpu.VMEM((8, 8, 128), F32), pltpu.VMEM((7, 8, 128), F32),
                pltpu.SemaphoreType.DMA((7,)), pltpu.SemaphoreType.DMA((7,))]


class References:
    ROUNDS = 4

    def __init__(self, place, own, full, half, acc, got, send_sem, recv_sem):
        self.p, self.own, self.full, self.half, self.acc, self.got = place, own, full, half, acc, got
        self.send_sem, self.recv_sem = send_sem, recv_sem
        self.sent, self.coming = [], {}
        self.j = place.at[0] * 2 + place.at[1] % 2
        self.lane = place.core * 2048

    def move(self, k, src, dst, device):
        copy = pltpu.make_async_remote_copy(
            src_ref=src, dst_ref=dst, send_sem=self.send_sem.at[k], recv_sem=self.recv_sem.at[k],
            device_id=device, device_id_type=MESH)
        copy.start()
        self.sent.append(copy)
        self.coming[k] = copy

    def lanes(self, at, size):
        return pl.ds(pl.multiple_of(at, 256), size)

    def share(self, k, j, device):
        cells = self.full.at[:, :, self.lanes(self.lane + j * 256, 256)]
        self.move(k, cells, cells, device)

    def start(self):
        for s in range(2):
            other = self.lanes((1 - self.p.core) * 2048, 2048)
            self.move(s, self.own.at[s, :, other], self.half.at[s], self.p.other_core())

    def round(self, r):
        if r == 0:
            for s in range(2):
                self.coming[s].wait_recv()
            for k in range(8):
                mine = self.own[:, :, self.lanes(self.lane + k * 256, 256)]
                self.acc[k] = mine + self.half[:, :, k * 256:k * 256 + 256]
            for d in (1, 7, 2, 6, 3, 5, 4):
                to = (self.j + d) % 8
                self.move(1 + d, self.acc.at[to], self.got.at[d - 1], self.p.group(to))
        elif r == 1:
            total = self.acc[self.j]
            for d in (1, 7, 2, 6, 3, 5, 4):
                self.coming[1 + d].wait_recv()
                total = total + self.got[d - 1]
            self.full[:, :, self.lanes(self.lane + self.j * 256, 256)] = total
            for d in (1, 7, 2, 6, 3, 5, 4):
                self.share(8 + d, self.j, self.p.group((self.j + d) % 8))
            self.share(16, self.j, self.p.other_core())
        elif r == 2:
            for d in (1, 7, 2, 6, 3, 5, 4):
                self.coming[8 + d].wait_recv()
                self.share(16 + d, (self.j - d + 8) % 8, self.p.other_core())
        else:
            for d in range(8):
                self.coming[16 + d].wait_recv()

    def finish(self):
        for copy in self.sent:
            copy.wait_send()

    @staticmethod
    def scratch():
        vm = pltpu.VMEM
        return [
            vm((2, 64, 4096), BF), vm((2, 64, 2048), BF), vm((8, 2, 64, 256), BF), vm((7, 2, 64, 256), BF),
            pltpu.SemaphoreType.DMA((24,)), pltpu.SemaphoreType.DMA((24,)),
        ]


def average(total, counts, orient, out):
    lane = lax.broadcasted_iota(jnp.int32, (8, 128), 1)
    row = lax.broadcasted_iota(jnp.int32, (8, 128), 0)
    count = jnp.sum(jnp.where((lane == orient) & (row == 0), counts, 0.0), keepdims=True)
    for b in range(32):
        out[0, :, b * 128:b * 128 + 128] = total[pl.ds(b, 8, stride=32), :] / count


class Scores:
    def __init__(self, v, wedge, full, table, out, scratch):
        self.v, self.wedge, self.full, self.out = v, wedge, full, out
        self.txf, self.tzf, self.tyf, self.tyi, self.tzi, self.txi, self.fr, self.fl = table_views(table)
        self.left, self.plane, self.spec, self.rspec, self.weight, self.edge, self.filt, self.extra = scratch
        self.low = lax.broadcasted_iota(jnp.int32, (64, 128), 1) < 64
        self.row = lax.broadcasted_iota(jnp.int32, (8, 128), 0)
        self.lane = lax.broadcasted_iota(jnp.int32, (8, 128), 1)
        self.result = jnp.zeros((8, 128), F32)
        self.twin, self.own = {}, {}

    def halves(self, t, op, fill):
        return [op(jnp.where(self.low[:8] == (k == 0), t, fill), keepdims=True) for k in range(2)]

    def forward(self, first, second, kind, out):
        def x():
            forward_x(first, 0, self.txf[kind][...], self.left)
            forward_x(second, 1, self.txf[kind][...], self.left)
        return [
            (0.6, x),
            (0.9, lambda: forward_z(self.tzf[kind][...], self.left, self.plane)),
            (0.6, lambda: forward_y(self.tyf[kind][...], self.plane, out)),
        ]

    def mirror(self, spec):
        return mirror(spec[0:128, :], self.fr[...], self.fl[...])

    def wedge_work(self):
        return self.forward(self.wedge, self.wedge, 1, self.rspec) + [
            (0.2, lambda: wedge_setup(self.rspec, self.fr[...], self.fl[...], self.weight, self.edge))]

    def pair_work(self, pair):
        spec = self.spec.at[pair]

        def after():
            self.twin[pair] = self.mirror(spec)
            self.own[pair] = self.halves(power(spec, self.twin[pair], self.weight, self.edge), jnp.sum, 0.0)
        return self.forward(self.v.at[2 * pair], self.v.at[2 * pair + 1], 0, spec) + [(0.3, after)]

    def reference_work(self):
        def after():
            t = self.mirror(self.rspec)
            self.norm = self.halves(power(self.rspec, t, self.weight, self.edge), jnp.sum, 0.0)
            reference_setup(self.rspec, t, self.weight, self.edge, self.low, self.filt, self.extra)
        return self.forward(self.full.at[0], self.full.at[1], 0, self.rspec) + [(0.7, after)]

    def score_work(self, pair, s):
        def last():
            top = self.halves(correlate_x(self.txi[...], self.plane), jnp.max, -jnp.inf)
            for k in range(2):
                score = top[k] / jnp.sqrt(self.own[pair][k] * self.norm[s] / float(N ** 3) + 1e-6)
                self.result = jnp.where((self.row == s) & (self.lane == 2 * pair + k), score, self.result)
        return [
            (1.0, lambda: correlate_y(self.spec.at[pair], self.twin[pair], self.filt.at[s], self.extra[s],
                                      self.tyi[...], self.left)),
            (0.6, lambda: correlate_z(self.tzi[...], self.left, self.plane)),
            (0.8, last),
        ]

    def finish(self):
        self.out[...] = self.result

    @staticmethod
    def scratch():
        vm = pltpu.VMEM
        return [
            vm((2048, 512), BF), vm((4608, 128), F32), vm((3, 4096, 128), BF), vm((4096, 128), BF),
            vm((2048, 128), F32), vm((128, 128), F32), vm((2, 4096, 128), F32), vm((2, 128, 128), F32),
        ]


def interleave(work, events):
    done = 0
    for before, action in events:
        while done < before:
            work[done][1]()
            done += 1
        action()
    for _, piece in work[done:]:
        piece()


ORDER = (
    (3, -1, 0), (6, 0, 0), (7, 1, 0), (9, 2, 0), (10, 3, 0), (10, -1, 1),
    (11, 4, 0), (13, 5, 0), (15, 0, 1), (15, 1, 1), (15, 2, 1), (15, 3, 1),
    (15, 4, 1), (15, 5, 1), (15, -1, 2), (15, -1, 3), (20, 0, 2), (21, 1, 2),
    (21, 2, 2), (22, 3, 2), (23, 4, 2), (23, 5, 2), (24, 0, 3), (25, 1, 3),
    (25, 2, 3), (26, 3, 3), (26, 4, 3), (27, 5, 3), (29, 0, 4), (29, 1, 4),
    (30, 2, 4), (30, 3, 4), (30, 4, 4), (30, 5, 4), (33, 0, 5), (33, 1, 5),
    (33, 2, 5), (33, 3, 5), (34, 4, 5), (34, 5, 5), (36, 0, 6), (36, 1, 6),
    (37, 2, 6), (37, 3, 6), (37, 4, 6), (38, 5, 6),
)


def fused_kernel(own_refs, sums, counts, v, wedges, table, scores_out, out, *scratch):
    place = Place()
    ends = np.cumsum([0] + [len(c.scratch()) for c in (ClassSums, Counts, References, Scores)])
    s, tally_s, refs_s, score_s = [scratch[i:j] for i, j in zip(ends, ends[1:])]
    classes = ClassSums(place, sums, s[0], s[1], s[2], s[3], s[4:7], s[7:10], s[10], s[11], s[12], s[13])
    tally = Counts(place, counts, *tally_s)
    refs = References(place, own_refs, *refs_s)
    orient = lax.axis_index("orient")
    scores = Scores(v, wedges.at[orient * wedges.shape[0] // lax.axis_size("orient")], refs.full, table, scores_out, score_s)
    greet(place)
    refs.start()
    tally.start()
    classes.start()
    events = []
    for before, part, r in ORDER:
        events.append((before, functools.partial(refs.round, r) if part < 0 else functools.partial(classes.step, r, part)))
        if part == len(PARTS) - 1:
            events.append((before, functools.partial(tally.round, r)))
    work = scores.wedge_work()
    for pair in range(3):
        work += scores.pair_work(pair)
    work += scores.reference_work()
    for pair in range(3):
        for step in range(STEPS):
            work += scores.score_work(pair, step)
    interleave(work, events)
    scores.finish()
    average(classes.total, tally.result(), orient, out)
    for part in (refs, tally, classes):
        part.finish()


def fused_call(own_refs, sums, counts, v, wedges):
    table = jnp.asarray(score_tables(), dtype=BF)
    vm = pl.BlockSpec(memory_space=pltpu.VMEM)
    return pl.pallas_call(
        fused_kernel,
        out_shape=(jax.ShapeDtypeStruct((8, 128), F32), jax.ShapeDtypeStruct((1, 8, 4096), F32)),
        in_specs=[vm, pl.BlockSpec(memory_space=pl.ANY)] + [vm] * 4,
        out_specs=(vm, vm),
        scratch_shapes=sum([c.scratch() for c in (ClassSums, Counts, References, Scores)], []),
        compiler_params=pltpu.CompilerParams(
            collective_id=0, has_side_effects=True, vmem_limit_bytes=60 * 2**20),
    )(own_refs, sums.reshape(2, 64, 256, 128), counts, v, wedges, table)


def local(subtomograms, rotated_refs, wedges, ref_pick, best_pick, class_of):
    sums, own_refs, counts = turn_call(ref_pick, best_pick, class_of[:, 0], rotated_refs, subtomograms)
    scores, averages = fused_call(own_refs, sums, counts, subtomograms, wedges)
    return (scores[:STEPS, :subtomograms.shape[0]], averages)


def solution(mesh):
    placed = (
        P(("tomo", "orient"), None, None),
        P("orient", None, None),
        P("tomo", None, None),
        P(),
        P(("tomo", "orient")),
        P(("tomo", "orient"), None),
    )
    return jax.shard_map(
        local,
        mesh=mesh,
        in_specs=placed,
        out_specs=(P(None, ("tomo", "orient")), P("orient", "tomo", None)),
        check_vma=False,
    )
```

```python
import functools

import jax
import jax.numpy as jnp
import numpy as np
from jax import lax
from jax.experimental import pallas as pl
from jax.experimental.pallas import tpu as pltpu
from jax.sharding import PartitionSpec as P

STEPS = 2
CLASSES = 16
N = 64
BF = jnp.bfloat16
F32 = jnp.float32
MESH = pl.DeviceIdType.MESH
PITCH_FWD = 36
PITCH_INV = 68
PITCH_WIDE = 68
PITCH_TOTAL = 36


def score_tables():
    i = np.arange(N)
    ang = (i[:, None] * i[None, :] % N) * (2.0 * np.pi / N)
    c, s = np.cos(ang), np.sin(ang)
    c[np.abs(c) < 1e-9] = 0.0
    s[np.abs(s) < 1e-9] = 0.0
    h = N // 2
    eye, rev = np.eye(N), np.eye(N)[(-i) % N]

    def pairs(m00, m01, m10, m11):
        return np.array([[m00, m01], [m10, m11]])

    def lanes_forward(b):
        t = np.einsum("abzk,qr,hg->qahzbgrk", b, np.eye(2), np.eye(2))
        return t.reshape(512, 512)

    def rows_forward(b):
        t = np.transpose(b, (1, 3, 0, 2)).reshape(2, N, 2, h, 2)
        return np.transpose(t, (0, 1, 2, 4, 3)).reshape(128, 128)

    fwd = pairs(c, -s, s, c)
    wdg = pairs(eye, 0 * eye, 0 * eye, rev)
    inv = pairs(c, s, -s, c)
    x_fwd = np.concatenate([c[:h], -s[:h]], 0)
    x_fwd[h] = c[h]
    x_wdg = np.concatenate([eye[:h], rev[:h]], 0)
    x_wdg[h] = eye[h]
    y_inv = np.transpose(inv, (1, 3, 0, 2)).reshape(128, 128)
    z_inv = np.einsum("abzk,qr->aqzbrk", inv, np.eye(2)).reshape(256, 256)
    x_inv = x_fwd.T
    flip_rows = np.kron(np.diag([1.0, -1.0]), rev)
    flip_lanes = np.kron(np.eye(2), rev)
    table = np.zeros((1408, 512))
    for k, t in enumerate((fwd, wdg)):
        table[512 * k:512 * k + 512] = lanes_forward(t)
        table[1024 + 128 * k:1152 + 128 * k, 256:384] = rows_forward(t)
    table[1024:1280, :256] = z_inv
    table[1024:1152, 384:] = y_inv
    table[1152:1280, 384:] = flip_rows
    table[1280:, :128] = flip_lanes
    table[1280:1344, 128:192] = x_fwd
    table[1344:, 128:192] = x_wdg
    table[1280:1344, 256:320] = x_inv
    return table


def table_views(table):
    return (
        [table.at[1280:1344, 128:192], table.at[1344:1408, 128:192]],
        [table.at[0:512, :], table.at[512:1024, :]],
        [table.at[1024:1152, 256:384], table.at[1152:1280, 256:384]],
        table.at[1024:1152, 384:512], table.at[1024:1280, 0:256], table.at[1280:1344, 256:320],
        table.at[1152:1280, 384:512], table.at[1280:1408, 0:128],
    )


def dot(a, b):
    return jnp.dot(a, b, preferred_element_type=F32)


def forward_x(vol, q, tx, left):
    def x_pass(c, _):
        at = pl.multiple_of(c * 512, 512)
        r = dot(tx, vol[:, pl.ds(at, 512)]).astype(BF)
        for k in range(4):
            rows = pl.ds(pl.multiple_of((c * 4 + k) * 32, 32), 32)
            left[rows, q * 256:q * 256 + 128] = r[:32, k * 128:k * 128 + 128]
            left[rows, q * 256 + 128:q * 256 + 256] = r[32:, k * 128:k * 128 + 128]
        return 0
    lax.fori_loop(0, 8, x_pass, 0, unroll=8)


def forward_z(tz, left, plane):
    def z_pass(m, _):
        at = pl.multiple_of(m * 128, 128)
        r = dot(left[pl.ds(at, 128), :], tz)
        for col in range(4):
            for k in range(4):
                row = (col * 32 + m * 4 + k) * PITCH_FWD
                plane[pl.ds(row, 32), :] = r[k * 32:k * 32 + 32, col * 128:col * 128 + 128]
        return 0
    lax.fori_loop(0, 8, z_pass, 0, unroll=8)


def forward_y(ty, plane, out):
    def y_pass(m, _):
        d = jnp.concatenate(
            [plane[pl.ds(2 * m + k, 128, stride=PITCH_FWD), :] for k in range(2)], 1).astype(BF)
        r = dot(ty, d).astype(BF)
        for k in range(2):
            out[pl.ds(pl.multiple_of((2 * m + k) * 128, 128), 128), :] = r[:, k * 128:k * 128 + 128]
        return 0
    lax.fori_loop(0, 16, y_pass, 0, unroll=16)


def mirror(g, flip_rows, flip_lanes):
    return dot(dot(flip_rows, g).astype(BF), flip_lanes)


def split(g, t):
    gr, gi, tr, ti = g[:64], g[64:], t[:64], t[64:]
    return (0.5 * (gr + tr), 0.5 * (gi + ti)), (0.5 * (gi - ti), -0.5 * (gr - tr))


def fold(v):
    return functools.reduce(jnp.add, [v[8 * k:8 * k + 8] for k in range(v.shape[0] // 8)])


def power(spec, twin, weight, edge):
    a, b = split(spec[0:128, :].astype(F32), twin)
    total = fold(edge[0:64, :] * (a[0] ** 2 + a[1] ** 2) + edge[64:128, :] * (b[0] ** 2 + b[1] ** 2))

    def body(kx, total):
        v = spec[pl.ds(pl.multiple_of(kx * 128, 128), 128), :].astype(F32)
        w = weight[pl.ds(pl.multiple_of(kx * 64, 64), 64), :]
        return total + fold(w * (v[:64] ** 2 + v[64:] ** 2))
    return lax.fori_loop(1, 32, body, total, unroll=31)


def wedge_setup(spec, flip_rows, flip_lanes, weight, edge):
    g = spec[0:128, :]
    t = mirror(g, jnp.abs(flip_rows), flip_lanes)
    edge[...] = 0.5 * (g.astype(F32) + t)

    def body(kx, _):
        v = spec[pl.ds(pl.multiple_of(kx * 128, 128), 128), :].astype(F32)
        weight[pl.ds(pl.multiple_of(kx * 64, 64), 64), :] = v[:64] + v[64:]
        return 0
    lax.fori_loop(1, 32, body, 0)


def spread_half(v, s, low):
    r = pltpu.roll(v, 64, 1)
    return jnp.where(low, v, r) if s == 0 else jnp.where(low, r, v)


def reference_setup(spec, twin, weight, edge, low, filt, extra):
    a, b = split(spec[0:128, :].astype(F32), twin)
    w0, w32 = edge[0:64, :], edge[64:128, :]
    for s in range(2):
        p = [spread_half(v, s, low) for v in (w0 * a[0], -w0 * a[1])]
        q = [spread_half(v, s, low) for v in (w32 * b[0], -w32 * b[1])]
        for k in range(2):
            filt[s, 64 * k:64 * k + 64, :] = 0.5 * (p[k] + q[k])
            extra[s, 64 * k:64 * k + 64, :] = 0.5 * (p[k] - q[k])

    def body(kx, _):
        v = spec[pl.ds(pl.multiple_of(kx * 128, 128), 128), :].astype(F32)
        w = weight[pl.ds(pl.multiple_of(kx * 64, 64), 64), :]
        re, im = w * v[:64], -w * v[64:]
        for s in range(2):
            filt[s, pl.ds(pl.multiple_of(kx * 128, 128), 64), :] = spread_half(re, s, low)
            filt[s, pl.ds(pl.multiple_of(kx * 128 + 64, 64), 64), :] = spread_half(im, s, low)
        return 0
    lax.fori_loop(1, 32, body, 0)


def correlate_y(spec, twin, filt, extra, ty, left):
    def times(v, w):
        return (v[:64] * w[:64] - v[64:] * w[64:], v[:64] * w[64:] + v[64:] * w[:64])

    def cross(kx):
        at = pl.multiple_of(kx * 128, 128)
        return times(spec[pl.ds(at, 128), :].astype(F32), filt[pl.ds(at, 128), :])

    def finish(m, parts):
        d = jnp.concatenate([jnp.concatenate(p, 0).astype(BF) for p in parts], 1)
        r = dot(ty, d).astype(BF)
        for k in range(2):
            rows = pl.ds(pl.multiple_of((2 * m + k) * 64, 64), 64)
            left[rows, 0:128] = r[:64, k * 128:k * 128 + 128]
            left[rows, 128:256] = r[64:, k * 128:k * 128 + 128]

    c0, e0 = cross(0), times(twin, extra)
    finish(0, [(c0[0] + e0[0], c0[1] + e0[1]), cross(1)])

    def y_pass(m, _):
        finish(m, [cross(2 * m), cross(2 * m + 1)])
        return 0
    lax.fori_loop(1, 16, y_pass, 0, unroll=15)


def correlate_z(tz, left, plane):
    def z_pass(m, _):
        at = pl.multiple_of(m * 256, 256)
        r = dot(left[pl.ds(at, 256), 0:256], tz)
        for p in range(2):
            for k in range(4):
                row = (p * 32 + m * 4 + k) * PITCH_INV
                plane[pl.ds(row, 64), :] = r[k * 64:k * 64 + 64, p * 128:p * 128 + 128]
        return 0
    lax.fori_loop(0, 8, z_pass, 0, unroll=8)


def correlate_x(tx, plane):
    def x_pass(m, top):
        d = jnp.concatenate(
            [plane[pl.ds(2 * m + k, 64, stride=PITCH_INV), :] for k in range(2)], 1).astype(BF)
        r = dot(tx, d)
        return jnp.maximum(top, jnp.maximum(r[:, :128], r[:, 128:]))
    top = lax.fori_loop(0, 32, x_pass, jnp.full((64, 128), -jnp.inf, F32), unroll=16)
    return functools.reduce(jnp.maximum, [top[8 * k:8 * k + 8] for k in range(8)])


def turn_tables():
    eye, rev = np.eye(N), np.eye(N)[::-1]
    two, swap = np.eye(2), np.eye(2)[::-1]
    pair = np.concatenate([eye, eye], 1)
    lanes = np.einsum("ac,hg,zw->ahzgcw", two, two, eye).reshape(256, 256)
    rows = np.transpose(eye.reshape(N, 32, 2), (0, 2, 1)).reshape(N, N)
    flip_rows = np.stack([eye, rev])
    flip_lanes = np.stack([np.kron(a, b) for b in (eye, rev) for a in (two, swap)])
    table = np.zeros((512, 512))
    table[:256, :256] = lanes
    table[:, 256:384] = flip_lanes.reshape(512, 128)
    table[:64, 384:] = pair
    table[64:128, 384:448] = rows
    table[128:256, 384:448] = flip_rows.reshape(128, 64)
    return table


def turn_kernel(ref_pick, pick, classes, refs, v, table,
                out, own_refs, counts, held, wide, mixed, total, narrow, empty, out_sem, ref_sem):
    pair, lanes, rows = table.at[0:64, 384:512], table.at[0:256, 0:256], table.at[64:128, 384:448]
    low = lax.broadcasted_iota(jnp.int32, (64, 128), 1) < 64
    me, per = lax.axis_index("orient"), refs.shape[0]

    def fetch(s):
        return pltpu.make_async_copy(refs.at[ref_pick[s] % per], own_refs.at[s], ref_sem.at[s])

    for s in range(2):
        @pl.when(ref_pick[s] // per == me)
        def _():
            fetch(s).start()

        @pl.when(ref_pick[s] // per != me)
        def _():
            own_refs[s] = jnp.zeros(own_refs.shape[1:], BF)

    def store(c, src):
        return pltpu.make_async_copy(src, out.at[c % 2, c // 2], out_sem.at[c])

    empty[...] = jnp.zeros(empty.shape, BF)
    lane = lax.broadcasted_iota(jnp.int32, (8, 128), 1)
    tally = jnp.zeros((8, 128), F32)
    for i in range(6):
        tally = tally + (lane == classes[i]).astype(F32)
    counts[...] = tally
    for c in range(CLASSES):
        hit = classes[0] == c
        for i in range(1, 6):
            hit = hit | (classes[i] == c)

        @pl.when(jnp.logical_not(hit))
        def _():
            store(c, empty).start()

    def swap_ends():
        def body(m, _):
            blocks = []
            for k in range(2):
                blk = held[pl.ds(pl.multiple_of((2 * m + k) * 64, 64), 64), :].astype(F32)
                blocks += [jnp.where(low, blk, 0.0), jnp.where(low, 0.0, blk)]
            w = jnp.concatenate(blocks, 0).astype(BF)
            r = lax.dot_general(pair[...], w, (((1,), (1,)), ((), ())), preferred_element_type=F32).astype(BF)
            for k in range(2):
                held[pl.ds(pl.multiple_of((2 * m + k) * 64, 64), 64), :] = r[:, k * 128:k * 128 + 128]
            return 0
        lax.fori_loop(0, 16, body, 0, unroll=16)

    def swap_first():
        def widen(m, _):
            for k in range(4):
                b = m * 4 + k
                blk = held[pl.ds(pl.multiple_of(b * 64, 64), 64), :]
                wide[pl.ds(b * PITCH_WIDE, 64), :] = blk.astype(F32)
            return 0
        lax.fori_loop(0, 8, widen, 0, unroll=8)

        def gather(m, _):
            d = [wide[pl.ds(2 * m + k, 32, stride=PITCH_WIDE), :] for k in range(2)]
            mixed[pl.ds(pl.multiple_of(m * 32, 32), 32), :] = jnp.concatenate(d, 1).astype(BF)
            return 0
        lax.fori_loop(0, 32, gather, 0, unroll=32)

        def body(m, _):
            r = dot(mixed[pl.ds(pl.multiple_of(m * 256, 256), 256), :], lanes[...]).astype(BF)
            halves = [jnp.concatenate([r[k * 32:k * 32 + 32, h * 128:h * 128 + 128] for k in range(8)], 1)
                      for h in range(2)]
            t = dot(rows[...], jnp.concatenate(halves, 0)).astype(BF)
            for k in range(8):
                held[pl.ds(pl.multiple_of((m * 8 + k) * 64, 64), 64), :] = t[:, k * 128:k * 128 + 128]
            return 0
        lax.fori_loop(0, 4, body, 0, unroll=4)

    def turn(i, first):
        number = pick[i]
        order, place = number // 4, number % 4
        even = (order == 0) | (order == 3) | (order == 4)
        f0 = jnp.where(even, (place == 1) | (place == 2), (place == 0) | (place == 3)).astype(jnp.int32)
        f1 = place % 2
        f2 = place // 2
        for b in range(32):
            held[b * 64:b * 64 + 64, :] = v[i, :, b * 128:b * 128 + 128]
        pl.when((order == 1) | (order == 3) | (order == 5))(swap_ends)
        pl.when((order >= 1) & (order <= 4))(swap_first)
        pl.when((order == 1) | (order == 4))(swap_ends)
        j0 = table[pl.ds(pl.multiple_of(128 + f0 * 64, 64), 64), 384:448]
        jl = table[pl.ds(pl.multiple_of(place * 128, 128), 128), 256:384]

        def flip_ends(m, _):
            at = pl.ds(pl.multiple_of(m * 256, 256), 256)
            held[at, :] = dot(held[at, :], jl).astype(BF)
            return 0

        @pl.when(f1 + f2 > 0)
        def _():
            lax.fori_loop(0, 8, flip_ends, 0, unroll=8)

        def add(m, flipped):
            blocks = []
            for k in range(4):
                b = m * 4 + k
                src = b + f1 * (31 - 2 * b)
                blocks.append(held[pl.ds(pl.multiple_of(src * 64, 64), 64), :])
            if flipped:
                u = dot(j0, jnp.concatenate(blocks, 1))
                blocks = [u[:, k * 128:k * 128 + 128] for k in range(4)]
            for k in range(4):
                at = pl.ds(m * 4 + k, 64, stride=PITCH_TOTAL)
                u = blocks[k].astype(F32)
                total[at, :] = u if first else total[at, :] + u

        @pl.when(f0 > 0)
        def _():
            lax.fori_loop(0, 8, lambda m, c: (add(m, True), c)[1], 0, unroll=8)

        @pl.when(f0 == 0)
        def _():
            lax.fori_loop(0, 8, lambda m, c: (add(m, False), c)[1], 0, unroll=8)

    def one(i, _):
        c = classes[i]

        def count(j, n):
            return n + (classes[j] == c).astype(jnp.int32)

        @pl.when(lax.fori_loop(0, i, count, 0) == 0)
        def _():
            turn(i, True)

            def later(j, _):
                @pl.when(classes[j] == c)
                def _():
                    turn(j, False)
                return 0
            lax.fori_loop(i + 1, 6, later, 0)

            def shorten(k, _):
                for d in range(8):
                    at = pl.ds(pl.multiple_of(k * 256 + d * 32, 32), 32)
                    narrow[i, at, :] = total[pl.ds((k * 8 + d) * PITCH_TOTAL, 32), :].astype(BF)
                return 0
            lax.fori_loop(0, 8, shorten, 0, unroll=8)
            store(c, narrow.at[i]).start()
        return 0
    lax.fori_loop(0, 6, one, 0)

    for s in range(2):
        @pl.when(ref_pick[s] // per == me)
        def _():
            fetch(s).wait()
    for c in range(CLASSES):
        store(c, empty).wait()


def turn_call(ref_pick, pick, classes, refs, v):
    table = jnp.asarray(turn_tables(), dtype=BF)
    sm, vm, far = [pl.BlockSpec(memory_space=m) for m in (pltpu.SMEM, pltpu.VMEM, pl.ANY)]
    return pl.pallas_call(
        turn_kernel,
        out_shape=(
            jax.ShapeDtypeStruct((2, 8, 2048, 128), BF),
            jax.ShapeDtypeStruct((2,) + refs.shape[1:], BF),
            jax.ShapeDtypeStruct((8, 128), F32),
        ),
        in_specs=[sm] * 3 + [far] + [vm] * 2,
        out_specs=(far, vm, vm),
        scratch_shapes=[
            pltpu.VMEM((2048, 128), BF), pltpu.VMEM((2304, 128), F32), pltpu.VMEM((1024, 256), BF),
            pltpu.VMEM((2560, 128), F32), pltpu.VMEM((6, 2048, 128), BF), pltpu.VMEM((2048, 128), BF),
            pltpu.SemaphoreType.DMA((CLASSES,)), pltpu.SemaphoreType.DMA((2,)),
        ],
        compiler_params=pltpu.CompilerParams(vmem_limit_bytes=60 * 2**20),
    )(ref_pick, pick, classes, refs, v, table)


PARTS = (
    ((0, 1, 2), False, 0, 48), ((0, 1, 2), True, 48, 32),
    ((1, 2, 0), False, 80, 48), ((1, 2, 0), True, 128, 32),
    ((2, 0, 1), False, 160, 48), ((2, 0, 1), True, 208, 48),
)
MOVES = 10


class Place:
    def __init__(self):
        tomo, orient = lax.axis_index("tomo"), lax.axis_index("orient")
        self.core = orient % 2
        self.at = (orient // 4, (tomo // 4) * 2 + (orient // 2) % 2, tomo % 4)
        self.near = tuple(c + 1 - 2 * (c % 2) for c in self.at)
        self.far = tuple(3 - c for c in self.at)
        self.cross = tuple((c + 2) % 4 for c in self.at)

    def device(self, axis=None, to=None, core=None):
        z, y, x = [to if axis == k else c for k, c in enumerate(self.at)]
        core = self.core if core is None else core
        return ((y // 2) * 4 + x, z * 4 + (y % 2) * 2 + core)

    def other_core(self):
        return self.device(core=1 - self.core)

    def partners(self):
        return [self.other_core()] + [self.device(k, t[k]) for k in range(3) for t in (self.near, self.far)]

    def group(self, j):
        return (lax.axis_index("tomo"), j * 2 + self.core)

    def all_partners(self):
        j = self.at[0] * 2 + self.at[1] % 2
        around = [self.group((j + d) % 8) for d in range(1, 8)]
        return around + [self.other_core(), self.device(1, self.far[1]),
                         self.device(2, self.near[2]), self.device(2, self.far[2])]


def greet(place):
    barrier = pltpu.get_barrier_semaphore()
    for device in place.all_partners():
        pl.semaphore_signal(barrier, inc=1, device_id=device, device_id_type=MESH)
    pl.semaphore_wait(barrier, 11)


class ClassSums:
    def __init__(self, place, sums, mine, got, keep, send, first, second, total, send_sem, recv_sem, load_sem):
        self.p, self.sums, self.mine, self.got, self.keep, self.send = place, sums, mine, got, keep, send
        self.first, self.second, self.total = first, second, total
        self.send_sem, self.recv_sem = send_sem, recv_sem
        self.load = pltpu.make_async_copy(sums.at[place.core], mine, load_sem)
        self.sent = []
        self.coming = {}

    def move(self, part, k, src, dst, device):
        copy = pltpu.make_async_remote_copy(
            src_ref=src, dst_ref=dst, send_sem=self.send_sem.at[part * MOVES + k],
            recv_sem=self.recv_sem.at[part * MOVES + k], device_id=device, device_id_type=MESH)
        copy.start()
        self.sent.append(copy)
        self.coming[part, k] = copy

    def start(self):
        for i, (_, _, row, rows) in enumerate(PARTS):
            cells = pl.ds(row, rows)
            self.move(i, 0, self.sums.at[1 - self.p.core, :, cells, :], self.got.at[:, cells, :], self.p.other_core())
        self.load.start()

    def links(self, part, level):
        axis = PARTS[part][0][level]
        near, far = self.p.near[axis], self.p.far[axis]
        f, g = (far, near) if PARTS[part][1] else (near, far)
        return axis, self.p.at[axis], f, g, self.p.cross[axis]

    def prefix(self, part, level):
        base = 0
        for k in range(level):
            base = base + self.p.at[PARTS[part][0][k]] * 4 ** (2 - k)
        return base, 4 ** (2 - level)

    def halves(self, part, level, value):
        _, _, row, rows = PARTS[part]
        cells = pl.ds(row, rows)
        axis, c, f, g, h = self.links(part, level)
        base, size = self.prefix(part, level)
        for slot, d in ((1, h), (0, f)):
            def out(k, _, d=d):
                at = base + d * size + k
                self.send[at, cells, :] = value(d * size + k).astype(BF)
                return 0
            lax.fori_loop(0, size, out, 0, unroll=min(size, 4))
            self.move(part, 1 + 3 * level + slot, self.send.at[pl.ds(base + d * size, size), cells, :],
                      self.first[level].at[slot, :, cells, :], self.p.device(axis, f))
        for d in (g, c):
            def stay(k, _, d=d):
                self.keep[base + d * size + k, cells, :] = value(d * size + k)
                return 0
            lax.fori_loop(0, size, stay, 0, unroll=min(size, 4))

    def round(self, r):
        for part in range(len(PARTS)):
            self.step(r, part)

    def step(self, r, part):
        order, _, row, rows = PARTS[part]
        cells = pl.ds(row, rows)
        if r == 0:
            if part == 0:
                self.load.wait()
            self.coming[part, 0].wait_recv()

            def value(at):
                d = (at // 16, at // 4 % 4, at % 4)
                z, y, x = [d[order.index(k)] for k in range(3)]
                src = (z * 2 + y % 2) * 8 + (y // 2) * 4 + x
                return self.mine[src, cells, :].astype(F32) + self.got[src, cells, :].astype(F32)
            self.halves(part, 0, value)
            return
        level = (r - 1) // 2
        axis, c, f, g, h = self.links(part, level)
        base, size = self.prefix(part, level)
        if r % 2:
            self.coming[part, 2 + 3 * level].wait_recv()

            def body(k, _):
                at = base + g * size + k
                v = self.keep[at, cells, :] + self.first[level][1, k, cells, :].astype(F32)
                self.send[at, cells, :] = v.astype(BF)
                return 0
            lax.fori_loop(0, size, body, 0, unroll=min(size, 4))
            self.move(part, 3 + 3 * level, self.send.at[pl.ds(base + g * size, size), cells, :],
                      self.second[level].at[:, cells, :], self.p.device(axis, g))
            return
        self.coming[part, 1 + 3 * level].wait_recv()
        self.coming[part, 3 + 3 * level].wait_recv()

        def value(k):
            return (self.keep[base + c * size + k, cells, :] + self.first[level][0, k, cells, :].astype(F32)
                    + self.second[level][k, cells, :].astype(F32))
        if level < 2:
            self.halves(part, level + 1, value)
        else:
            self.total[cells, :] = value(0)

    def finish(self):
        for copy in self.sent:
            copy.wait_send()

    @staticmethod
    def scratch():
        vm = pltpu.VMEM
        return [
            vm((64, 256, 128), BF), vm((64, 256, 128), BF), vm((64, 256, 128), F32), vm((64, 256, 128), BF),
            vm((2, 16, 256, 128), BF), vm((2, 4, 256, 128), BF), vm((2, 1, 256, 128), BF),
            vm((16, 256, 128), BF), vm((4, 256, 128), BF), vm((1, 256, 128), BF),
            vm((256, 128), F32),
            pltpu.SemaphoreType.DMA((len(PARTS) * MOVES,)), pltpu.SemaphoreType.DMA((len(PARTS) * MOVES,)),
            pltpu.SemaphoreType.DMA(()),
        ]


class Counts:
    def __init__(self, place, own, held, got, send_sem, recv_sem):
        self.p, self.held, self.got, self.send_sem, self.recv_sem = place, held, got, send_sem, recv_sem
        held[0] = own[...]
        self.partners = place.partners()
        self.sent = []

    def go(self, k):
        copy = pltpu.make_async_remote_copy(
            src_ref=self.held.at[k], dst_ref=self.got.at[k], send_sem=self.send_sem.at[k],
            recv_sem=self.recv_sem.at[k], device_id=self.partners[k], device_id_type=MESH)
        copy.start()
        self.sent.append(copy)

    def start(self):
        self.go(0)

    def round(self, k):
        self.sent[k].wait_recv()
        self.held[k + 1] = self.held[k] + self.got[k]
        if k < 6:
            self.go(k + 1)

    def result(self):
        return self.held[7]

    def finish(self):
        for copy in self.sent:
            copy.wait_send()

    @staticmethod
    def scratch():
        return [pltpu.VMEM((8, 8, 128), F32), pltpu.VMEM((7, 8, 128), F32),
                pltpu.SemaphoreType.DMA((7,)), pltpu.SemaphoreType.DMA((7,))]


class References:
    ROUNDS = 4

    def __init__(self, place, own, full, half, acc, got, send_sem, recv_sem):
        self.p, self.own, self.full, self.half, self.acc, self.got = place, own, full, half, acc, got
        self.send_sem, self.recv_sem = send_sem, recv_sem
        self.sent, self.coming = [], {}
        self.j = place.at[0] * 2 + place.at[1] % 2
        self.lane = place.core * 2048

    def move(self, k, src, dst, device):
        copy = pltpu.make_async_remote_copy(
            src_ref=src, dst_ref=dst, send_sem=self.send_sem.at[k], recv_sem=self.recv_sem.at[k],
            device_id=device, device_id_type=MESH)
        copy.start()
        self.sent.append(copy)
        self.coming[k] = copy

    def lanes(self, at, size):
        return pl.ds(pl.multiple_of(at, 256), size)

    def share(self, k, j, device):
        cells = self.full.at[:, :, self.lanes(self.lane + j * 256, 256)]
        self.move(k, cells, cells, device)

    def start(self):
        for s in range(2):
            other = self.lanes((1 - self.p.core) * 2048, 2048)
            self.move(s, self.own.at[s, :, other], self.half.at[s], self.p.other_core())

    def round(self, r):
        if r == 0:
            for s in range(2):
                self.coming[s].wait_recv()
            for k in range(8):
                mine = self.own[:, :, self.lanes(self.lane + k * 256, 256)]
                self.acc[k] = mine + self.half[:, :, k * 256:k * 256 + 256]
            for d in (1, 7, 2, 6, 3, 5, 4):
                to = (self.j + d) % 8
                self.move(1 + d, self.acc.at[to], self.got.at[d - 1], self.p.group(to))
        elif r == 1:
            total = self.acc[self.j]
            for d in (1, 7, 2, 6, 3, 5, 4):
                self.coming[1 + d].wait_recv()
                total = total + self.got[d - 1]
            self.full[:, :, self.lanes(self.lane + self.j * 256, 256)] = total
            for d in (1, 7, 2, 6, 3, 5, 4):
                self.share(8 + d, self.j, self.p.group((self.j + d) % 8))
            self.share(16, self.j, self.p.other_core())
        elif r == 2:
            for d in (1, 7, 2, 6, 3, 5, 4):
                self.coming[8 + d].wait_recv()
                self.share(16 + d, (self.j - d + 8) % 8, self.p.other_core())
        else:
            for d in range(8):
                self.coming[16 + d].wait_recv()

    def finish(self):
        for copy in self.sent:
            copy.wait_send()

    @staticmethod
    def scratch():
        vm = pltpu.VMEM
        return [
            vm((2, 64, 4096), BF), vm((2, 64, 2048), BF), vm((8, 2, 64, 256), BF), vm((7, 2, 64, 256), BF),
            pltpu.SemaphoreType.DMA((24,)), pltpu.SemaphoreType.DMA((24,)),
        ]


def average(total, counts, orient, out):
    lane = lax.broadcasted_iota(jnp.int32, (8, 128), 1)
    row = lax.broadcasted_iota(jnp.int32, (8, 128), 0)
    count = jnp.sum(jnp.where((lane == orient) & (row == 0), counts, 0.0), keepdims=True)
    for b in range(32):
        out[0, :, b * 128:b * 128 + 128] = total[pl.ds(b, 8, stride=32), :] / count


class Scores:
    def __init__(self, v, wedge, full, table, out, scratch):
        self.v, self.wedge, self.full, self.out = v, wedge, full, out
        self.txf, self.tzf, self.tyf, self.tyi, self.tzi, self.txi, self.fr, self.fl = table_views(table)
        self.left, self.plane, self.spec, self.rspec, self.weight, self.edge, self.filt, self.extra = scratch
        self.low = lax.broadcasted_iota(jnp.int32, (64, 128), 1) < 64
        self.row = lax.broadcasted_iota(jnp.int32, (8, 128), 0)
        self.lane = lax.broadcasted_iota(jnp.int32, (8, 128), 1)
        self.result = jnp.zeros((8, 128), F32)
        self.twin, self.own = {}, {}

    def halves(self, t, op, fill):
        return [op(jnp.where(self.low[:8] == (k == 0), t, fill), keepdims=True) for k in range(2)]

    def forward(self, first, second, kind, out):
        def x():
            forward_x(first, 0, self.txf[kind][...], self.left)
            forward_x(second, 1, self.txf[kind][...], self.left)
        return [
            (0.6, x),
            (0.9, lambda: forward_z(self.tzf[kind][...], self.left, self.plane)),
            (0.6, lambda: forward_y(self.tyf[kind][...], self.plane, out)),
        ]

    def mirror(self, spec):
        return mirror(spec[0:128, :], self.fr[...], self.fl[...])

    def wedge_work(self):
        return self.forward(self.wedge, self.wedge, 1, self.rspec) + [
            (0.2, lambda: wedge_setup(self.rspec, self.fr[...], self.fl[...], self.weight, self.edge))]

    def pair_work(self, pair):
        spec = self.spec.at[pair]

        def after():
            self.twin[pair] = self.mirror(spec)
            self.own[pair] = self.halves(power(spec, self.twin[pair], self.weight, self.edge), jnp.sum, 0.0)
        return self.forward(self.v.at[2 * pair], self.v.at[2 * pair + 1], 0, spec) + [(0.3, after)]

    def reference_work(self):
        def after():
            t = self.mirror(self.rspec)
            self.norm = self.halves(power(self.rspec, t, self.weight, self.edge), jnp.sum, 0.0)
            reference_setup(self.rspec, t, self.weight, self.edge, self.low, self.filt, self.extra)
        return self.forward(self.full.at[0], self.full.at[1], 0, self.rspec) + [(0.7, after)]

    def score_work(self, pair, s):
        def last():
            top = self.halves(correlate_x(self.txi[...], self.plane), jnp.max, -jnp.inf)
            for k in range(2):
                score = top[k] / jnp.sqrt(self.own[pair][k] * self.norm[s] / float(N ** 3) + 1e-6)
                self.result = jnp.where((self.row == s) & (self.lane == 2 * pair + k), score, self.result)
        return [
            (1.0, lambda: correlate_y(self.spec.at[pair], self.twin[pair], self.filt.at[s], self.extra[s],
                                      self.tyi[...], self.left)),
            (0.6, lambda: correlate_z(self.tzi[...], self.left, self.plane)),
            (0.8, last),
        ]

    def finish(self):
        self.out[...] = self.result

    @staticmethod
    def scratch():
        vm = pltpu.VMEM
        return [
            vm((2048, 512), BF), vm((4608, 128), F32), vm((3, 4096, 128), BF), vm((4096, 128), BF),
            vm((2048, 128), F32), vm((128, 128), F32), vm((2, 4096, 128), F32), vm((2, 128, 128), F32),
            vm((64, 4096), BF), vm((6, 64, 4096), BF), pltpu.SemaphoreType.DMA((2,)),
        ]


def interleave(work, events):
    done = 0
    for before, action in events:
        while done < before:
            work[done][1]()
            done += 1
        action()
    for _, piece in work[done:]:
        piece()


ORDER = (
    (3, -1, 0), (6, 0, 0), (7, 1, 0), (9, 2, 0), (10, 3, 0), (10, -1, 1),
    (11, 4, 0), (13, 5, 0), (15, 0, 1), (15, 1, 1), (15, 2, 1), (15, 3, 1),
    (15, 4, 1), (15, 5, 1), (15, -1, 2), (15, -1, 3), (20, 0, 2), (21, 1, 2),
    (21, 2, 2), (22, 3, 2), (23, 4, 2), (23, 5, 2), (24, 0, 3), (25, 1, 3),
    (25, 2, 3), (26, 3, 3), (26, 4, 3), (27, 5, 3), (29, 0, 4), (29, 1, 4),
    (30, 2, 4), (30, 3, 4), (30, 4, 4), (30, 5, 4), (33, 0, 5), (33, 1, 5),
    (33, 2, 5), (33, 3, 5), (34, 4, 5), (34, 5, 5), (36, 0, 6), (36, 1, 6),
    (37, 2, 6), (37, 3, 6), (37, 4, 6), (38, 5, 6),
)


def fused_kernel(own_refs, sums, counts, v, wedges, table, scores_out, out, *scratch):
    place = Place()
    ends = np.cumsum([0] + [len(c.scratch()) for c in (ClassSums, Counts, References, Scores)])
    s, tally_s, refs_s, score_s = [scratch[i:j] for i, j in zip(ends, ends[1:])]
    classes = ClassSums(place, sums, s[0], s[1], s[2], s[3], s[4:7], s[7:10], s[10], s[11], s[12], s[13])
    tally = Counts(place, counts, *tally_s)
    refs = References(place, own_refs, *refs_s)
    orient = lax.axis_index("orient")
    wedge_in, v_in, in_sem = score_s[-3:]
    wedge_copy = pltpu.make_async_copy(
        wedges.at[orient * wedges.shape[0] // lax.axis_size("orient")], wedge_in, in_sem.at[0])
    v_copy = pltpu.make_async_copy(v, v_in, in_sem.at[1])
    scores = Scores(v_in, wedge_in, refs.full, table, scores_out, score_s[:-3])
    wedge_copy.start()
    v_copy.start()
    greet(place)
    refs.start()
    tally.start()
    classes.start()
    wedge_copy.wait()
    v_copy.wait()
    events = []
    for before, part, r in ORDER:
        events.append((before, functools.partial(refs.round, r) if part < 0 else functools.partial(classes.step, r, part)))
        if part == len(PARTS) - 1:
            events.append((before, functools.partial(tally.round, r)))
    work = scores.wedge_work()
    for pair in range(3):
        work += scores.pair_work(pair)
    work += scores.reference_work()
    for pair in range(3):
        for step in range(STEPS):
            work += scores.score_work(pair, step)
    interleave(work, events)
    scores.finish()
    average(classes.total, tally.result(), orient, out)
    for part in (refs, tally, classes):
        part.finish()


def fused_call(own_refs, sums, counts, v, wedges):
    table = jnp.asarray(score_tables(), dtype=BF)
    vm, far = pl.BlockSpec(memory_space=pltpu.VMEM), pl.BlockSpec(memory_space=pl.ANY)
    return pl.pallas_call(
        fused_kernel,
        out_shape=(jax.ShapeDtypeStruct((8, 128), F32), jax.ShapeDtypeStruct((1, 8, 4096), F32)),
        in_specs=[vm, far, vm, far, far, vm],
        out_specs=(vm, vm),
        scratch_shapes=sum([c.scratch() for c in (ClassSums, Counts, References, Scores)], []),
        compiler_params=pltpu.CompilerParams(
            collective_id=0, has_side_effects=True, vmem_limit_bytes=60 * 2**20),
    )(own_refs, sums.reshape(2, 64, 256, 128), counts, v, wedges, table)


def local(subtomograms, rotated_refs, wedges, ref_pick, best_pick, class_of):
    sums, own_refs, counts = turn_call(ref_pick, best_pick, class_of[:, 0], rotated_refs, subtomograms)
    scores, averages = fused_call(own_refs, sums, counts, subtomograms, wedges)
    return (scores[:STEPS, :subtomograms.shape[0]], averages)


def solution(mesh):
    placed = (
        P(("tomo", "orient"), None, None),
        P("orient", None, None),
        P("tomo", None, None),
        P(),
        P(("tomo", "orient")),
        P(("tomo", "orient"), None),
    )
    return jax.shard_map(
        local,
        mesh=mesh,
        in_specs=placed,
        out_specs=(P(None, ("tomo", "orient")), P("orient", "tomo", None)),
        check_vma=False,
    )
```
